32 devices in a mesh: expert: 4 (over z), half: 2 (over core), dp: 4 (over y, x).
Axes of the slice: x: 2, y: 2, z: 4, core: 2. Of those that a mesh axis runs over, the one named last changes fastest.
Arguments:
- tokens_in: bfloat16 [16, 2, 12, 3584], P(('expert', 'dp')), may hold values from -6 to 6
- cotangent: bfloat16 [16, 2, 12, 3584], P(('expert', 'dp')), may hold values from -1.5 to 1.5
- expert_ids: int32 [16, 2, 12, 8], P(('expert', 'dp')), may hold values from 0 to 31, all different within a row; in each aligned block of 12 rows (0 to 11, 12 to 23, ..., all dimensions but the last counted through in order) at most 6 rows name the same one
- gate_probs: bfloat16 [16, 2, 12, 8], P(('expert', 'dp')), may hold values from 0.049804688 to 0.5
- gate_weight: bfloat16 [32, 3584, 1024], P('expert', 'dp', 'half'), may hold values from -0.09375 to 0.09375
- up_weight: bfloat16 [32, 3584, 1024], P('expert', 'dp', 'half'), may hold values from -0.09375 to 0.09375
- down_weight: bfloat16 [32, 3584, 1024], P('expert', 'dp', 'half'), may hold values from -0.1875 to 0.1875
Outputs:
- token_grad: bfloat16 [16, 2, 12, 3584], P(('expert', 'dp'), 'half')
- route_grad: bfloat16 [16, 2, 12, 8], P(('expert', 'dp'), 'half')
- gate_weight_grad: bfloat16 [32, 3584, 1024], P('expert', 'dp', 'half')
- up_weight_grad: bfloat16 [32, 3584, 1024], P('expert', 'dp', 'half')
- down_weight_grad: bfloat16 [32, 3584, 1024], P('expert', 'dp', 'half')
The draws below stay inside these ranges and needn't reach their ends.
Inputs may be any that keep to these rules, and one draw needn't show every extreme that they name: `expert_ids`: each row names 8 different experts. Among the 12 tokens of one owner block (the aligned blocks of the last two leading dimensions), no expert is named by more than 6 tokens, and in every draw some expert is named by exactly 6 tokens of some block.
All inputs are finite; a program needn't handle non-finite values.
Results may differ from the reference program's by a relative error of at most 0.017.
Values may be sent and summed in bfloat16 or wider, within the bound.
No kernel may reach another device: no remote copies, remote signals or barrier semaphores. Data moves between devices by JAX's collectives and lax.ppermute only.
A program may use at most 448 MiB of HBM per device.

```python
import math
import jax
import jax.numpy as jnp
import numpy as np
from jax import lax

D = 3584
FF = 1024
TOP = 8
EXPERTS = 32
HALF_TOK = 12
MOST = 6
GROUPS = 16
N_EXPERT = 4
N_DP = 4


def shard_levels(rng, extent, shards, least, largest):
    factor_of = 1.0
    for position, shards_of in shards:
        heights = jax.random.uniform(jax.random.fold_in(jax.random.fold_in(rng, 6), position), (shards_of,), jnp.float32, least / len(shards), largest / len(shards))
        factor_of = factor_of * jnp.repeat(jnp.exp(heights), extent[position] // shards_of).reshape((-1,) + (1,) * (len(extent) - 1 - position))
    return factor_of


def shared_out(own_key, own, number, rows, amount, top, reach, slope):
    sequence = jax.random.permutation(own_key, amount)
    packed, ordinary = shares(amount, rows * top, reach, slope, True), shares(amount, rows * top, reach, slope, False)
    places = jnp.arange(amount)

    def named(lengths, offset_by):
        used = int((lengths > 0).sum())
        fixed = max(1, used // 4)
        shifted = fixed + (places - fixed + offset_by * (used - fixed)) % max(1, amount - fixed)
        return jnp.zeros((amount,), jnp.int32).at[sequence[jnp.where(places < fixed, places, shifted)]].set(jnp.asarray(lengths, jnp.int32))

    lengths = jnp.where(number % 4 == 0, named(packed, number // 4), named(ordinary, number - number // 4 - 1))
    mixed = jax.random.permutation(jax.random.fold_in(own, 3), amount)
    source_of, sink = mixed[0:amount // 2 * 2:2], mixed[1:amount // 2 * 2:2]
    room = jnp.minimum(lengths[source_of] - 1, reach - lengths[sink]) // 2
    room = jnp.where((source_of == sequence[0]) | (sink == sequence[0]) | (lengths[sink] == 0), 0, jnp.maximum(room, 0))
    shifted = jax.random.randint(jax.random.fold_in(own, 4), (amount // 2,), 0, 1 << 20) % (room + 1)
    lengths = lengths.at[source_of].add(-shifted).at[sink].add(shifted)
    members = jnp.searchsorted(jnp.cumsum(lengths), jnp.arange(rows * top), side="right").astype(jnp.int32)
    grid = members.reshape(top, rows).T
    grid = grid[jax.random.permutation(jax.random.fold_in(own, 1), rows)]
    offset_by = jax.random.randint(jax.random.fold_in(own, 2), (rows, 1), 0, top)
    return jnp.take_along_axis(grid, (jnp.arange(top)[None, :] + offset_by) % top, axis=1)


def shares(count, total, bound, slope, full):
    weights = [(1 << 20) // math.isqrt(rank ** slope) + 1 for rank in range(1, count + 1)]
    largest = bound if full else min(bound, max(-(-total // count), total * weights[0] // sum(weights)))
    least = 1 if total - largest >= count - 1 else 0
    holding, surplus = [largest] + [least] * (count - 1), total - largest - least * (count - 1)
    while surplus > 0:
        candidates = [i for i in range(1, count) if holding[i] < largest] or [i for i in range(1, count) if holding[i] < bound]
        whole, left = sum([weights[i] for i in candidates]), surplus
        for i in candidates:
            addition = min(bound - holding[i], max(1, left * weights[i] // whole), surplus)
            holding[i] = holding[i] + addition
            surplus = surplus - addition
    return np.array(holding)


def bell_draw(rng, dims, scale, limit, pieces=(), kind=jnp.bfloat16):
    factor_of = shard_levels(rng, dims, pieces, -0.22, 0.18) if pieces else 1.0
    drawn = jax.random.normal(rng, dims, jnp.float32) * scale * factor_of
    return jnp.minimum(jnp.maximum(drawn, -limit), limit).astype(kind)


def setup_inputs(seed: int = 0) -> dict:
    key_of = jax.random.split(jax.random.key(seed), 8)
    tokens_in = bell_draw(key_of[0], (GROUPS, 2, HALF_TOK, D), 1.0, 6.0, ((0, 16),))
    cotangent = bell_draw(key_of[1], (GROUPS, 2, HALF_TOK, D), 0.25, 1.5, ((0, 16),))
    expert_ids_keys = jax.random.split(jax.random.fold_in(key_of[2], 1), GROUPS * 2 * HALF_TOK // HALF_TOK)
    expert_ids_turns = jax.random.permutation(jax.random.fold_in(key_of[2], 3), GROUPS * 2 * HALF_TOK // HALF_TOK)
    expert_ids = jax.vmap(lambda own, number: shared_out(jax.random.fold_in(key_of[2], 2), own, number, HALF_TOK, EXPERTS, TOP, MOST, 2))(expert_ids_keys, expert_ids_turns).reshape((GROUPS, 2, HALF_TOK, TOP))
    gate_probs = jnp.clip(0.049804688 + 0.4501953 * jax.random.uniform(key_of[3], (GROUPS, 2, HALF_TOK, TOP), jnp.float32) ** shard_levels(key_of[3], (GROUPS, 2, HALF_TOK, TOP), ((0, 16),), -0.2, 0.2), 0.049804688, 0.5).astype(jnp.bfloat16)
    gate_weight = bell_draw(key_of[4], (EXPERTS, D, FF), D ** -0.5, 0.09375, ((0, 4), (1, 4), (2, 2)))
    up_weight = bell_draw(key_of[5], (EXPERTS, D, FF), D ** -0.5, 0.09375, ((0, 4), (1, 4), (2, 2)))
    down_weight = bell_draw(key_of[6], (EXPERTS, D, FF), FF ** -0.5, 0.1875, ((0, 4), (1, 4), (2, 2)))
    return dict(tokens_in=tokens_in, cotangent=cotangent, expert_ids=expert_ids, gate_probs=gate_probs, gate_weight=gate_weight, up_weight=up_weight, down_weight=down_weight)


def route_slots(route_ids, route_gates, first_expert, expert_count):
    experts_here = first_expert + jnp.arange(expert_count, dtype=jnp.int32)
    matched = route_ids[..., None, :, :] == experts_here[:, None, None]
    chosen = jnp.any(matched, axis=-1)
    slot_rank = jnp.cumsum(chosen.astype(jnp.int32), axis=-1) - 1
    slot_ids = jnp.arange(MOST, dtype=jnp.int32)
    slot_pick = jnp.logical_and(chosen[..., None, :], slot_rank[..., None, :] == slot_ids[:, None])
    route_gate = jnp.sum(jnp.where(matched, route_gates.astype(jnp.float32)[..., None, :, :], 0.0), axis=-1)
    slot_gate = jnp.sum(jnp.where(slot_pick, route_gate[..., None, :], 0.0), axis=-1)
    return slot_pick, matched, slot_gate


def silu_parts(pre_act):
    sigma = jax.nn.sigmoid(pre_act)
    return pre_act * sigma, sigma * (1.0 + pre_act * (1.0 - sigma))


def rounded_term(left, right):
    term = jnp.einsum("aprd,aprh->pdh", left, right)
    return lax.optimization_barrier(term.astype(jnp.bfloat16)).astype(jnp.float32)


def reference(tokens_in, cotangent, expert_ids, gate_probs, gate_weight, up_weight, down_weight):
    groups, halves, half_tok, model_width = tokens_in.shape
    x_all = tokens_in.astype(jnp.float32)
    dy_all = cotangent.astype(jnp.float32)
    slot_rows = groups * halves * MOST

    def micro(values):
        return values.reshape(N_EXPERT, N_DP, halves * MOST, -1).astype(jnp.float32)

    def per_expert(running, inputs):
        token_acc, route_acc = running
        expert, gate_w, up_w, down_w = inputs
        slot_pick, matched, slot_gate = route_slots(expert_ids, gate_probs, expert, 1)
        pick_f = slot_pick[:, :, 0].astype(jnp.float32)
        matched = matched[:, :, 0]
        slot_x = jnp.einsum("ghst,ghtd->ghsd", pick_f, x_all).astype(jnp.bfloat16)
        slot_dy = jnp.einsum("ghst,ghtd->ghsd", pick_f, dy_all).astype(jnp.bfloat16)
        flat_x = slot_x.reshape(slot_rows, model_width)
        flat_dy = slot_dy.reshape(slot_rows, model_width)
        gate_col = slot_gate[:, :, 0].reshape(slot_rows, 1)
        gate_act = jnp.dot(flat_x, gate_w, preferred_element_type=jnp.float32)
        up_act = jnp.dot(flat_x, up_w, preferred_element_type=jnp.float32)
        back_act = jnp.dot(flat_dy, down_w, preferred_element_type=jnp.float32)
        active, silu_slope = silu_parts(gate_act)
        hidden = (active * up_act).astype(jnp.bfloat16)
        grad_gate = (gate_col * back_act * up_act * silu_slope).astype(jnp.bfloat16)
        grad_up = (gate_col * back_act * active).astype(jnp.bfloat16)
        scaled = (gate_col * flat_dy.astype(jnp.float32)).astype(jnp.bfloat16)
        row_grad = (jnp.dot(grad_gate, gate_w.T, preferred_element_type=jnp.float32)
                    + jnp.dot(grad_up, up_w.T, preferred_element_type=jnp.float32)).astype(jnp.bfloat16)
        row_route = jnp.sum(back_act * hidden.astype(jnp.float32), axis=1).astype(jnp.bfloat16)
        token_acc = token_acc + jnp.einsum("ghst,ghsd->ghtd", pick_f, row_grad.reshape(groups, halves, MOST, model_width).astype(jnp.float32))
        per_token = jnp.einsum("ghst,ghs->ght", pick_f, row_route.reshape(groups, halves, MOST).astype(jnp.float32))
        route_acc = route_acc + jnp.where(matched, per_token[..., None], 0.0)
        gate_grad = jnp.sum(rounded_term(micro(flat_x), micro(grad_gate)), axis=0).astype(jnp.bfloat16)
        up_grad = jnp.sum(rounded_term(micro(flat_x), micro(grad_up)), axis=0).astype(jnp.bfloat16)
        down_grad = jnp.sum(rounded_term(micro(scaled), micro(hidden)), axis=0).astype(jnp.bfloat16)
        return (token_acc, route_acc), (gate_grad, up_grad, down_grad)

    start_acc = (jnp.zeros(tokens_in.shape, jnp.float32), jnp.zeros(expert_ids.shape, jnp.float32))
    expert_list = jnp.arange(EXPERTS, dtype=jnp.int32)
    finals, weight_grads = lax.scan(per_expert, start_acc, (expert_list, gate_weight, up_weight, down_weight))
    token_acc, route_acc = finals
    return (token_acc.astype(jnp.bfloat16), route_acc.astype(jnp.bfloat16),
            weight_grads[0], weight_grads[1], weight_grads[2])
```

```python
import functools

import jax
import jax.numpy as jnp
from jax import lax
from jax.experimental import pallas as pl
from jax.experimental.pallas import tpu as pltpu
from jax.sharding import PartitionSpec as P

LANES = 128
ALIGN = 16
BF = jnp.bfloat16
F32 = jnp.float32
BY_ROW = (((0,), (0,)), ((), ()))
BY_COLUMN = (((1,), (1,)), ((), ()))
MIB = 1 << 20


def round_up(value, step):
    return -(-value // step) * step


def whole_vmem():
    return pl.BlockSpec(memory_space=pltpu.VMEM)


def whole_smem():
    return pl.BlockSpec(memory_space=pltpu.SMEM)


def expert_column(table, expert):
    lane = lax.broadcasted_iota(jnp.int32, table.shape, 1)
    return jnp.sum(jnp.where(lane == expert, table, 0), axis=1, keepdims=True)


def window_start(offs, expert, cap, window):
    start = jnp.minimum((offs[0, expert] // ALIGN) * ALIGN, cap - window)
    return pl.multiple_of(start, ALIGN)


def route_kernel(n_local, top, idx, meta, pos, gate, offs):
    rows = meta.shape[0]
    meta_f = meta[...].astype(F32)
    lane = lax.broadcasted_iota(jnp.int32, (rows, LANES), 1)
    here = (lane + idx[0] * n_local).astype(F32)
    chosen = jnp.zeros((rows, LANES), F32)
    gates = jnp.zeros((rows, LANES), F32)
    for k in range(top):
        hit = jnp.logical_and(meta_f[:, k : k + 1] == here, lane < n_local)
        chosen = jnp.where(hit, 1.0, chosen)
        gates = jnp.where(hit, meta_f[:, top + k : top + k + 1], gates)
    earlier = (
        lax.broadcasted_iota(jnp.int32, (rows, rows), 1)
        < lax.broadcasted_iota(jnp.int32, (rows, rows), 0)
    )
    rank = jnp.dot(
        earlier.astype(F32).astype(BF), chosen.astype(BF), preferred_element_type=F32
    )
    counts = jnp.broadcast_to(jnp.sum(chosen, axis=0, keepdims=True), (8, LANES))
    before = (
        lax.broadcasted_iota(jnp.int32, (LANES, LANES), 0)
        < lax.broadcasted_iota(jnp.int32, (LANES, LANES), 1)
    )
    starts = jnp.dot(
        counts, before.astype(F32), preferred_element_type=F32, precision=lax.Precision.HIGHEST
    )
    pos[...] = jnp.where(chosen > 0.0, rank + starts[0:1], -1.0).astype(jnp.int32)
    gate[...] = gates
    offs[...] = starts.astype(jnp.int32)


def route(idx, meta, n_local, top):
    rows = meta.shape[0]
    return pl.pallas_call(
        functools.partial(route_kernel, n_local, top),
        out_shape=(
            jax.ShapeDtypeStruct((rows, LANES), jnp.int32),
            jax.ShapeDtypeStruct((rows, LANES), F32),
            jax.ShapeDtypeStruct((8, LANES), jnp.int32),
        ),
        in_specs=[whole_smem(), whole_vmem()],
        out_specs=(whole_vmem(), whole_vmem(), whole_vmem()),
        compiler_params=pltpu.CompilerParams(vmem_limit_bytes=40 * MIB),
        name="route",
    )(idx, meta)


def act_kernel(
    cap, window, idx, offs, x, dy, pos, gate, w_gate, w_up, w_down,
    own, send_x, send_y, later_x, later_y, own_gate, acc, gate_acc,
):
    expert = pl.program_id(0)
    hidden = w_gate.shape[2]
    quarter = cap // 4
    half = quarter // 2

    @pl.when(expert == 0)
    def _():
        acc[...] = jnp.zeros_like(acc)
        gate_acc[...] = jnp.zeros_like(gate_acc)

    start = window_start(offs, expert, cap, window)
    column = expert_column(pos[...], expert)
    slot = lax.broadcasted_iota(jnp.int32, (x.shape[0], window), 1)
    pick = jnp.where(jnp.logical_and(column >= 0, column - start == slot), 1.0, 0.0).astype(BF)
    gate_col = jnp.broadcast_to(expert_column(gate[...], expert), gate.shape).astype(BF)
    slot_x = lax.dot_general(pick, x[...], BY_ROW, preferred_element_type=F32).astype(BF)
    slot_dy = lax.dot_general(pick, dy[...], BY_ROW, preferred_element_type=F32).astype(BF)
    slot_gate = lax.dot_general(pick, gate_col, BY_ROW, preferred_element_type=F32)
    row = start + lax.broadcasted_iota(jnp.int32, (window, 1), 0)
    mine = jnp.logical_and(row >= offs[0, expert], row < offs[0, expert + 1])
    rows = pl.ds(start, window)
    gate_acc[rows, :] = jnp.where(mine, slot_gate, gate_acc[rows, :])
    for part, (left, right) in enumerate(((slot_x, w_gate), (slot_x, w_up), (slot_dy, w_down))):
        columns = slice(part * hidden, (part + 1) * hidden)
        value = jnp.dot(left, right[0], preferred_element_type=F32)
        acc[rows, columns] = jnp.where(mine, value, acc[rows, columns])

    @pl.when(expert == pl.num_programs(0) - 1)
    def _():
        me = idx[2]

        def piece(other, first, count):
            at = pl.multiple_of((me ^ other) * quarter + first, ALIGN)
            return acc[pl.ds(at, count), :].astype(BF)

        own[...] = piece(0, 0, quarter)
        own_gate[...] = gate_acc[pl.ds(pl.multiple_of(me * quarter, ALIGN), quarter), :]
        send_x[0:half, :] = piece(3, 0, half)
        send_x[half:quarter, :] = piece(1, 0, half)
        send_y[0:half, :] = piece(3, half, half)
        send_y[half:quarter, :] = piece(2, half, half)
        later_x[...] = piece(1, half, half)
        later_y[...] = piece(2, 0, half)


def partial_acts(idx, chunk, weights, cap, window):
    n_local, width, hidden = weights[0].shape
    quarter, wide = cap // 4, 3 * hidden
    by_expert = pl.BlockSpec((1, width, hidden), lambda j: (j, 0, 0))

    def rows(count, lanes, kind):
        return jax.ShapeDtypeStruct((count, lanes), kind)

    return pl.pallas_call(
        functools.partial(act_kernel, cap, window),
        grid=(n_local,),
        out_shape=(
            rows(quarter, wide, BF),
            rows(quarter, wide, BF),
            rows(quarter, wide, BF),
            rows(quarter // 2, wide, BF),
            rows(quarter // 2, wide, BF),
            rows(quarter, LANES, F32),
        ),
        in_specs=[whole_smem(), whole_smem()] + [whole_vmem()] * 4 + [by_expert] * 3,
        out_specs=(whole_vmem(),) * 6,
        scratch_shapes=[pltpu.VMEM((cap, wide), F32), pltpu.VMEM((cap, LANES), F32)],
        compiler_params=pltpu.CompilerParams(vmem_limit_bytes=40 * MIB),
        cost_estimate=pl.CostEstimate(
            flops=2 * window * width * wide * n_local,
            bytes_accessed=3 * n_local * width * hidden * 2,
            transcendentals=0,
        ),
        name="acts",
    )(idx, chunk["offs"], chunk["x"], chunk["dy"], chunk["pos"], chunk["gate"], *weights)


def unit_kernel(own, from_x, from_y, late_x, late_y, gate, grads, route_part):
    quarter = own.shape[0]
    half = quarter // 2
    hidden = own.shape[1] // 3
    for first, near, late in ((0, from_x, late_y), (half, from_y, late_x)):
        rows = slice(first, first + half)

        def total(part):
            at = slice(part * hidden, (part + 1) * hidden)
            return (
                own[rows, at].astype(F32)
                + near[half:quarter, at].astype(F32)
                + late[:, at].astype(F32)
            )

        gate_act, up_act, back = total(0), total(1), total(2)
        sigma = 1.0 / (1.0 + jnp.exp(-gate_act))
        active = gate_act * sigma
        slope = sigma * (1.0 + gate_act * (1.0 - sigma))
        scaled = gate[rows, 0:1] * back
        unit = (active * up_act).astype(BF)
        grads[rows, 0:hidden] = (scaled * up_act * slope).astype(BF)
        grads[rows, hidden : 2 * hidden] = (scaled * active).astype(BF)
        grads[rows, 2 * hidden :] = unit
        sums = jnp.sum(back * unit.astype(F32), axis=1, keepdims=True)
        route_part[rows, :] = jnp.broadcast_to(sums, (half, LANES)).astype(BF)


def unit_grads(*parts):
    quarter, wide = parts[0].shape
    return pl.pallas_call(
        unit_kernel,
        out_shape=(
            jax.ShapeDtypeStruct((quarter, wide), BF),
            jax.ShapeDtypeStruct((quarter, LANES), BF),
        ),
        in_specs=[whole_vmem()] * 6,
        out_specs=(whole_vmem(),) * 2,
        compiler_params=pltpu.CompilerParams(vmem_limit_bytes=40 * MIB),
        name="units",
    )(*parts)


def place_quarters(me, pieces, target, lanes):
    own, from_x, from_y, first, second = pieces
    quarter = own.shape[0]
    half = quarter // 2

    def at(other, extra, count):
        return pl.ds(pl.multiple_of((me ^ other) * quarter + extra, ALIGN), count)

    target[at(0, 0, quarter), :] = own[:, lanes]
    target[at(1, 0, quarter), :] = from_x[:, lanes]
    target[at(2, 0, quarter), :] = from_y[:, lanes]
    target[at(3, 0, half), :] = first[:, lanes]
    target[at(3, half, half), :] = second[:, lanes]


def token_kernel(
    cap, window, top, block, idx, offs, own, from_x, from_y, first, second, route_part, pos, meta,
    w_gate, w_up, keep, send, grads, routes, acc, route_acc,
):
    expert = pl.program_id(0)
    hidden = w_gate.shape[2]
    n_local = pl.num_programs(0)
    quarter = cap // 4

    @pl.when(expert == 0)
    def _():
        place_quarters(idx[2], (own, from_x, from_y, first, second), grads, slice(0, 2 * hidden))
        routes[...] = jnp.zeros_like(routes)
        routes[pl.ds(pl.multiple_of(idx[2] * quarter, ALIGN), quarter), :] = route_part[...]
        acc[...] = jnp.zeros_like(acc)
        route_acc[...] = jnp.zeros_like(route_acc)

    start = window_start(offs, expert, cap, window)
    column = expert_column(pos[...], expert)
    slot = lax.broadcasted_iota(jnp.int32, (pos.shape[0], window), 1)
    pick = jnp.where(jnp.logical_and(column >= 0, column - start == slot), 1.0, 0.0).astype(BF)
    rows = pl.ds(start, window)
    row_grad = lax.dot_general(
        grads[rows, 0:hidden], w_gate[0], BY_COLUMN, preferred_element_type=F32
    ) + lax.dot_general(
        grads[rows, hidden : 2 * hidden], w_up[0], BY_COLUMN, preferred_element_type=F32
    )
    acc[...] += jnp.dot(pick, row_grad.astype(BF), preferred_element_type=F32)
    lane = lax.broadcasted_iota(jnp.int32, meta.shape, 1)
    named = (expert + idx[0] * n_local).astype(F32)
    hit = jnp.logical_and(lane < top, meta[...].astype(F32) == named)
    token_route = jnp.dot(pick, routes[rows, :], preferred_element_type=F32)
    route_acc[...] = jnp.where(hit, token_route, route_acc[...])

    @pl.when(expert == n_local - 1)
    def _():
        width = w_gate.shape[1]
        for group in range(pos.shape[0] // (2 * block)):
            there = slice(group * block, (group + 1) * block)
            for target, which in ((keep, idx[1]), (send, 1 - idx[1])):
                at = pl.ds(pl.multiple_of((2 * group + which) * block, ALIGN), block)
                target[there, 0:width] = acc[at, :].astype(BF)
                target[there, width:] = route_acc[at, :].astype(BF)


def token_grads(idx, chunk, pieces, route_part, weights, cap, window, top, block):
    n_local, width, hidden = weights[0].shape
    tokens = chunk["x"].shape[0]
    by_expert = pl.BlockSpec((1, width, hidden), lambda j: (j, 0, 0))
    result = jax.ShapeDtypeStruct((tokens // 2, width + LANES), BF)
    return pl.pallas_call(
        functools.partial(token_kernel, cap, window, top, block),
        grid=(n_local,),
        out_shape=(result, result),
        in_specs=[whole_smem(), whole_smem()] + [whole_vmem()] * 8 + [by_expert] * 2,
        out_specs=(whole_vmem(),) * 2,
        scratch_shapes=[
            pltpu.VMEM((cap, 2 * hidden), BF),
            pltpu.VMEM((cap, LANES), BF),
            pltpu.VMEM((tokens, width), F32),
            pltpu.VMEM((tokens, LANES), F32),
        ],
        compiler_params=pltpu.CompilerParams(vmem_limit_bytes=48 * MIB),
        cost_estimate=pl.CostEstimate(
            flops=4 * window * width * hidden * n_local,
            bytes_accessed=2 * n_local * width * hidden * 2,
            transcendentals=0,
        ),
        name="tokens",
    )(
        idx, chunk["offs"], *pieces, route_part, chunk["pos"], chunk["meta"], *weights[:2]
    )


def weight_kernel(caps, windows, groups, idx, *refs):
    count = len(caps)
    offs, refs = refs[:count], refs[count:]
    pieces, refs = refs[: 5 * count], refs[5 * count :]
    xs, dys, poss, gates = (refs[i * count : (i + 1) * count] for i in range(4))
    refs = refs[4 * count :]
    outs = refs[:3]
    grads, refs = refs[3 : 3 + count], refs[3 + count :]
    x_turned, dy_turned, stacks = refs[0], refs[1], refs[2:]
    expert = pl.program_id(0)
    hidden = outs[0].shape[2]

    @pl.when(expert == 0)
    def _():
        for c in range(count):
            place_quarters(idx[2], pieces[5 * c : 5 * c + 5], grads[c], slice(None))
        x_turned[...] = jnp.concatenate([ref[...] for ref in xs], axis=0).T
        dy_turned[...] = jnp.concatenate([ref[...] for ref in dys], axis=0).T
        for stacked in stacks:
            stacked[...] = jnp.zeros_like(stacked)

    sums, token_start = [None] * 3, 0
    for members, stacked in zip(groups, stacks):
        places, scales, lane_start = [], [], 0
        for c in members:
            start = window_start(offs[c], expert, caps[c], windows[c])
            column = expert_column(poss[c][...], expert)
            places.append(jnp.where(column >= 0, column - start + lane_start, -1))
            scales.append(expert_column(gates[c][...], expert))
            stacked[lane_start : lane_start + windows[c], :] = grads[c][pl.ds(start, windows[c]), :]
            lane_start += windows[c]
        places = jnp.concatenate(places, axis=0)
        scales = jnp.concatenate(scales, axis=0)
        tokens, total = places.shape[0], stacked.shape[0]
        hit = places == lax.broadcasted_iota(jnp.int32, (tokens, total), 1)
        pick = jnp.where(hit, 1.0, 0.0).astype(BF)
        pick_scaled = jnp.where(hit, scales, 0.0).astype(BF)
        lanes = slice(token_start, token_start + tokens)
        slot_x = jnp.dot(x_turned[:, lanes], pick, preferred_element_type=F32).astype(BF)
        slot_dy = jnp.dot(dy_turned[:, lanes], pick_scaled, preferred_element_type=F32).astype(BF)
        for part, left in enumerate((slot_x, slot_x, slot_dy)):
            columns = slice(part * hidden, (part + 1) * hidden)
            value = jnp.dot(left, stacked[:, columns], preferred_element_type=F32)
            sums[part] = value if sums[part] is None else sums[part] + value
        token_start += tokens
    for target, value in zip(outs, sums):
        target[0] = value.astype(BF)


def weight_grads(idx, chunks, pieces, caps, windows, n_local, width, hidden):
    count = len(chunks)
    wide = 3 * hidden
    tokens = sum(chunk["x"].shape[0] for chunk in chunks)
    groups = [tuple(range(min(count, 3)))] + [(c,) for c in range(3, count)]
    totals = [round_up(sum(windows[c] for c in members), LANES) for members in groups]
    by_expert = pl.BlockSpec((1, width, hidden), lambda j: (j, 0, 0))
    result = jax.ShapeDtypeStruct((n_local, width, hidden), BF)
    names = ("x", "dy", "pos", "gate")
    return pl.pallas_call(
        functools.partial(weight_kernel, caps, windows, groups),
        grid=(n_local,),
        out_shape=(result,) * 3,
        in_specs=[whole_smem()] * (1 + count) + [whole_vmem()] * (9 * count),
        out_specs=(by_expert,) * 3,
        scratch_shapes=[pltpu.VMEM((cap, wide), BF) for cap in caps]
        + [
            pltpu.VMEM((width, tokens), BF),
            pltpu.VMEM((width, tokens), BF),
        ]
        + [pltpu.VMEM((total, wide), BF) for total in totals],
        compiler_params=pltpu.CompilerParams(vmem_limit_bytes=56 * MIB),
        cost_estimate=pl.CostEstimate(
            flops=2 * sum(totals) * width * wide * n_local,
            bytes_accessed=3 * n_local * width * hidden * 2,
            transcendentals=0,
        ),
        name="weights",
    )(
        idx,
        *[chunk["offs"] for chunk in chunks],
        *[piece for group in pieces for piece in group],
        *[chunk[name] for name in names for chunk in chunks],
    )


def to_partner(value, axis, other):
    return lax.ppermute(value, axis, [(i, i ^ other) for i in range(lax.axis_size(axis))])


def by_distance(stack, me):
    size, bit = stack.shape[0], 1
    while bit < size:
        swapped = jnp.concatenate(
            [stack[i ^ bit : (i ^ bit) + 1] for i in range(size)], axis=0
        )
        stack = jnp.where((me & bit) != 0, swapped, stack)
        bit *= 2
    return stack


def exchange(stack, axis, me):
    near = by_distance(stack, me)
    got = [near[0]] + [to_partner(near[k], axis, k) for k in range(1, stack.shape[0])]
    return by_distance(jnp.stack(got), me)


def sum_over_dp(parts):
    own, send_x, send_y, later_x, later_y, gate = parts
    half = own.shape[0] // 2
    from_x = to_partner(send_x, "dp", 1)
    from_y = to_partner(send_y, "dp", 2)
    late_x = to_partner(later_x + from_y[:half], "dp", 1)
    late_y = to_partner(later_y + from_x[:half], "dp", 2)
    return own, from_x, from_y, late_x, late_y, gate


def gather_over_dp(own):
    half = own.shape[0] // 2
    from_x = to_partner(own, "dp", 1)
    from_y = to_partner(own, "dp", 2)
    first = to_partner(from_x[:half], "dp", 2)
    second = to_partner(from_y[half:], "dp", 1)
    return own, from_x, from_y, first, second


def on_device(tokens_in, cotangent, expert_ids, gate_probs, gate_weight, up_weight, down_weight):
    n_expert, n_dp = lax.axis_size("expert"), lax.axis_size("dp")
    expert_at, half_at, dp_at = (lax.axis_index(name) for name in ("expert", "half", "dp"))
    idx = jnp.stack([expert_at, half_at, dp_at]).astype(jnp.int32)
    n_local, width, hidden = gate_weight.shape
    weights = (gate_weight, up_weight, down_weight)
    _, blocks, block_tokens, model_width = tokens_in.shape
    top = expert_ids.shape[3]
    block = n_dp * block_tokens
    group = blocks * block

    def slices(values):
        return values[0].reshape(blocks, block_tokens, n_dp, width).transpose(2, 0, 1, 3)

    meta = jnp.concatenate(
        [
            expert_ids[0].astype(BF),
            gate_probs[0],
            jnp.full((blocks, block_tokens, LANES - 2 * top), -1.0, BF),
        ],
        axis=2,
    )
    meta = jnp.broadcast_to(meta[None], (n_dp,) + meta.shape)
    payload = jnp.concatenate([slices(tokens_in), slices(cotangent), meta], axis=3)
    payload = exchange(payload, "dp", dp_at)
    payload = payload.transpose(1, 0, 2, 3).reshape(group, 2 * width + LANES)

    x_held = [payload[:, :width]]
    dy_held = [payload[:, width : 2 * width]]
    meta_held = [payload[:, 2 * width :]]
    bounds, step = [(0, 1)], 1
    while step < n_expert:
        bounds.append((step, 2 * step))
        if step == 1:
            got = to_partner(payload, "expert", 1)
            x_held.append(got[:, :width])
            dy_held.append(got[:, width : 2 * width])
            meta_held.append(got[:, 2 * width :])
        else:
            if step == 2:
                blocks_of = [(payload, 2), (payload, 3)]
            else:
                joined = jnp.concatenate(
                    [jnp.concatenate(held, axis=0) for held in (x_held, dy_held, meta_held)], axis=1
                )
                blocks_of = [(joined, step)]
            for rows, other in blocks_of:
                mixed = jnp.where(half_at == 0, rows[:, :width], rows[:, width : 2 * width])
                mixed = jnp.concatenate([mixed, rows[:, 2 * width :]], axis=1)
                got = to_partner(mixed, "expert", other)
                rest = to_partner(got[:, :width], "half", 1)
                far_x = jnp.where(half_at == 0, got[:, :width], rest)
                far_dy = jnp.where(half_at == 0, rest, got[:, :width])
                for i in range(rows.shape[0] // group):
                    cut = slice(i * group, (i + 1) * group)
                    x_held.append(far_x[cut])
                    dy_held.append(far_dy[cut])
                    meta_held.append(got[cut, width:])
        step *= 2

    chunks, caps, windows = [], [], []
    for low, high in bounds:
        chunk = {
            "x": jnp.concatenate(x_held[low:high], axis=0),
            "dy": jnp.concatenate(dy_held[low:high], axis=0),
            "meta": jnp.concatenate(meta_held[low:high], axis=0),
        }
        chunk["pos"], chunk["gate"], chunk["offs"] = route(idx, chunk["meta"], n_local, top)
        most = (high - low) * group // 2
        chunks.append(chunk)
        caps.append(round_up(n_local * most, LANES))
        windows.append(round_up(most + ALIGN, ALIGN))

    pieces, route_parts = [], []
    for chunk, cap, window in zip(chunks, caps, windows):
        wide_window = round_up(window, LANES)
        parts = sum_over_dp(partial_acts(idx, chunk, weights, cap, wide_window))
        grads, route_part = unit_grads(*parts)
        pieces.append(gather_over_dp(grads))
        route_parts.append(route_part)

    held = []
    for chunk, piece, route_part, cap, window in zip(chunks, pieces, route_parts, caps, windows):
        keep, send = token_grads(
            idx, chunk, piece, route_part, weights, cap, round_up(window, LANES), top, block
        )
        both = keep.astype(F32) + to_partner(send, "half", 1).astype(F32)
        held.extend(jnp.split(both.astype(BF), keep.shape[0] // block, axis=0))
    weight_out = weight_grads(idx, chunks, pieces, caps, windows, n_local, width, hidden)
    step = n_expert // 2
    while step > 2:
        got = to_partner(jnp.concatenate(held[step:], axis=0), "expert", step)
        held = [
            (mine.astype(F32) + other.astype(F32)).astype(BF)
            for mine, other in zip(held[:step], jnp.split(got, step, axis=0))
        ]
        step //= 2
    total = held[0].astype(F32)
    for other in range(len(held) - 1, 0, -1):
        total = total + to_partner(held[other], "expert", other).astype(F32)
    total = total.astype(BF).reshape(n_dp, block_tokens, width + LANES)
    total = exchange(total, "dp", dp_at)
    token_grad = total[:, :, :width].transpose(1, 0, 2).reshape(block_tokens, model_width)
    route_grad = jnp.sum(total[:, :, width : width + top].astype(F32), axis=0).astype(BF)
    return (token_grad[None, None], route_grad[None, None]) + tuple(weight_out)


def solution(mesh):
    return jax.shard_map(
        on_device,
        mesh=mesh,
        in_specs=(
            P(("expert", "dp"), None, None, None),
            P(("expert", "dp"), None, None, None),
            P(("expert", "dp"), None, None, None),
            P(("expert", "dp"), None, None, None),
            P("expert", "dp", "half"),
            P("expert", "dp", "half"),
            P("expert", "dp", "half"),
        ),
        out_specs=(
            P(("expert", "dp"), "half", None, None),
            P(("expert", "dp"), "half", None, None),
            P("expert", "dp", "half"),
            P("expert", "dp", "half"),
            P("expert", "dp", "half"),
        ),
        check_vma=False,
    )
```

```python
import functools

import jax
import jax.numpy as jnp
from jax import lax
from jax.experimental import pallas as pl
from jax.experimental.pallas import tpu as pltpu
from jax.sharding import PartitionSpec as P

LANES = 128
ALIGN = 16
BF = jnp.bfloat16
F32 = jnp.float32
BY_ROW = (((0,), (0,)), ((), ()))
BY_COLUMN = (((1,), (1,)), ((), ()))
MIB = 1 << 20


def round_up(value, step):
    return -(-value // step) * step


def cost(flops):
    return pl.CostEstimate(flops=int(flops), bytes_accessed=0, transcendentals=0)


def vmem_limit(rows):
    return (24 if rows <= 512 else 56) * MIB


def whole_vmem():
    return pl.BlockSpec(memory_space=pltpu.VMEM)


def whole_smem():
    return pl.BlockSpec(memory_space=pltpu.SMEM)


def expert_column(table, expert):
    lane = lax.broadcasted_iota(jnp.int32, table.shape, 1)
    return jnp.sum(jnp.where(lane == expert, table, 0), axis=1, keepdims=True)


def window_start(offs, expert, cap, window):
    start = jnp.minimum((offs[0, expert] // ALIGN) * ALIGN, cap - window)
    return pl.multiple_of(start, ALIGN)


def pack_kernel(width, top, idx, x, dy, ids, gates, *outs):
    tokens, blocks, _ = x.shape
    rows = tokens * blocks
    row = lax.broadcasted_iota(jnp.int32, (rows, tokens), 0)
    token = lax.broadcasted_iota(jnp.int32, (rows, tokens), 1)
    fill = jnp.full((LANES - 2 * top, tokens), -1.0, BF)
    meta = jnp.zeros((rows, LANES), F32)
    for block in range(blocks):
        place = jnp.where(row == token * blocks + block, 1.0, 0.0).astype(BF)
        table = jnp.concatenate([ids[block].astype(F32).astype(BF), gates[block], fill], axis=0)
        meta += lax.dot_general(place, table, BY_COLUMN, preferred_element_type=F32)
    for distance, out in enumerate(outs):
        at = pl.ds(pl.multiple_of((idx[2] ^ distance) * width, LANES), width)
        for t in range(tokens):
            there = slice(t * blocks, (t + 1) * blocks)
            out[there, 0:width] = x[t, :, at]
            out[there, width : 2 * width] = dy[t, :, at]
        out[:, 2 * width :] = meta.astype(BF)


def pack(idx, x, dy, ids, gates, n_dp, width):
    shape = (x.shape[0] * x.shape[1], 2 * width + LANES)
    return pl.pallas_call(
        functools.partial(pack_kernel, width, ids.shape[1]),
        out_shape=(jax.ShapeDtypeStruct(shape, BF),) * n_dp,
        in_specs=[whole_smem()] + [whole_vmem()] * 4,
        out_specs=(whole_vmem(),) * n_dp,
        compiler_params=pltpu.CompilerParams(vmem_limit_bytes=24 * MIB),
        name="pack",
    )(idx, x, dy, ids, gates)


def shared_order(place, step, dp_at):
    owner = ((place.astype(F32) + 0.5) * (1.0 / step)).astype(jnp.int32)
    return place + ((owner ^ dp_at) - owner) * step


def route_kernel(n_local, top, width, step, kind, count, idx, *refs):
    parts, (pos, gate, offs, payload), rest = refs[:count], refs[count : count + 4], refs[count + 4 :]
    if kind == "own":
        for distance, part in enumerate(parts):
            payload[distance * step : (distance + 1) * step, :] = part[...]
        mixed = rest[0]
        mixed[:, 0:width] = jnp.where(
            idx[1] == 0, payload[:, 0:width], payload[:, width : 2 * width]
        )
        mixed[:, width:] = payload[:, 2 * width :]
    else:
        first = 0
        for near, other in zip(parts[: count // 2], parts[count // 2 :]):
            rows = slice(first, first + near.shape[0])
            payload[rows, 0:width] = jnp.where(idx[1] == 0, near[:, 0:width], other[:, 0:width])
            payload[rows, width : 2 * width] = jnp.where(
                idx[1] == 0, other[:, 0:width], near[:, 0:width]
            )
            payload[rows, 2 * width :] = near[:, width:]
            first += near.shape[0]
    rows = payload.shape[0]
    meta = payload[:, 2 * width :].astype(F32)
    lane = lax.broadcasted_iota(jnp.int32, (rows, LANES), 1)
    here = (lane + idx[0] * n_local).astype(F32)
    chosen = jnp.zeros((rows, LANES), F32)
    gates = jnp.zeros((rows, LANES), F32)
    for k in range(top):
        hit = jnp.logical_and(meta[:, k : k + 1] == here, lane < n_local)
        chosen = jnp.where(hit, 1.0, chosen)
        gates = jnp.where(hit, meta[:, top + k : top + k + 1], gates)
    place_column = shared_order(lax.broadcasted_iota(jnp.int32, (rows, 1), 0), step, idx[2])
    place_row = shared_order(lax.broadcasted_iota(jnp.int32, (1, rows), 1), step, idx[2])
    earlier = jnp.where(place_row < place_column, 1.0, 0.0)
    rank = jnp.dot(earlier.astype(BF), chosen.astype(BF), preferred_element_type=F32)
    counts = jnp.broadcast_to(jnp.sum(chosen, axis=0, keepdims=True), (8, LANES))
    before = (
        lax.broadcasted_iota(jnp.int32, (LANES, LANES), 0)
        < lax.broadcasted_iota(jnp.int32, (LANES, LANES), 1)
    )
    starts = jnp.dot(
        counts, before.astype(F32), preferred_element_type=F32, precision=lax.Precision.HIGHEST
    )
    pos[...] = jnp.where(chosen > 0.0, rank + starts[0:1], -1.0).astype(jnp.int32)
    gate[...] = gates
    offs[...] = starts.astype(jnp.int32)


def route(idx, parts, kind, rows, n_local, top, width, step):
    out_shape = [
        jax.ShapeDtypeStruct((rows, LANES), jnp.int32),
        jax.ShapeDtypeStruct((rows, LANES), F32),
        jax.ShapeDtypeStruct((8, LANES), jnp.int32),
        jax.ShapeDtypeStruct((rows, 2 * width + LANES), BF),
    ]
    if kind == "own":
        out_shape.append(jax.ShapeDtypeStruct((rows, width + LANES), BF))
    out = pl.pallas_call(
        functools.partial(route_kernel, n_local, top, width, step, kind, len(parts)),
        out_shape=tuple(out_shape),
        in_specs=[whole_smem()] + [whole_vmem()] * len(parts),
        out_specs=(whole_vmem(),) * len(out_shape),
        compiler_params=pltpu.CompilerParams(vmem_limit_bytes=vmem_limit(rows)),
        name="route",
    )(idx, *parts)
    chunk = {"pos": out[0], "gate": out[1], "offs": out[2], "payload": out[3]}
    return (chunk, out[4]) if kind == "own" else chunk


def act_kernel(cap, window, direct, idx, offs, x, dy, pos, gate, w_gate, w_up, w_down, *refs):
    outs, (own_gate, acc, gate_acc) = refs[:-3], refs[-3:]
    expert = pl.program_id(0)
    hidden = w_gate.shape[2]
    quarter = cap // 4
    half = quarter // 2

    @pl.when(expert == 0)
    def _():
        acc[...] = jnp.zeros_like(acc)
        gate_acc[...] = jnp.zeros_like(gate_acc)

    start = window_start(offs, expert, cap, window)
    column = expert_column(pos[...], expert)
    slot = lax.broadcasted_iota(jnp.int32, (x.shape[0], window), 1)
    pick = jnp.where(jnp.logical_and(column >= 0, column - start == slot), 1.0, 0.0).astype(BF)
    gate_col = jnp.broadcast_to(expert_column(gate[...], expert), gate.shape).astype(BF)
    slot_x = lax.dot_general(pick, x[...], BY_ROW, preferred_element_type=F32).astype(BF)
    slot_dy = lax.dot_general(pick, dy[...], BY_ROW, preferred_element_type=F32).astype(BF)
    slot_gate = lax.dot_general(pick, gate_col, BY_ROW, preferred_element_type=F32)
    row = start + lax.broadcasted_iota(jnp.int32, (window, 1), 0)
    mine = jnp.logical_and(row >= offs[0, expert], row < offs[0, expert + 1])
    rows = pl.ds(start, window)
    gate_acc[rows, :] = jnp.where(mine, slot_gate, gate_acc[rows, :])
    for part, (left, right) in enumerate(((slot_x, w_gate), (slot_x, w_up), (slot_dy, w_down))):
        columns = slice(part * hidden, (part + 1) * hidden)
        value = jnp.dot(left, right[0], preferred_element_type=F32)
        acc[rows, columns] = jnp.where(mine, value, acc[rows, columns])

    @pl.when(expert == pl.num_programs(0) - 1)
    def _():
        me = idx[2]

        def piece(other, first, count):
            at = pl.multiple_of((me ^ other) * quarter + first, ALIGN)
            return acc[pl.ds(at, count), :].astype(BF)

        own_gate[...] = gate_acc[pl.ds(pl.multiple_of(me * quarter, ALIGN), quarter), :]
        if direct:
            for other, out in enumerate(outs):
                out[...] = piece(other, 0, quarter)
        else:
            own, send_x, send_y, later_x, later_y = outs
            own[...] = piece(0, 0, quarter)
            send_x[0:half, :] = piece(3, 0, half)
            send_x[half:quarter, :] = piece(1, 0, half)
            send_y[0:half, :] = piece(3, half, half)
            send_y[half:quarter, :] = piece(2, half, half)
            later_x[...] = piece(1, half, half)
            later_y[...] = piece(2, 0, half)


def payload_specs(chunk, width):
    rows = chunk["payload"].shape[0]
    return [pl.BlockSpec((rows, width), lambda j, part=part: (0, part)) for part in range(2)]


def partial_acts(idx, chunk, weights, cap, window, direct):
    n_local, width, hidden = weights[0].shape
    quarter, wide = cap // 4, 3 * hidden
    by_expert = pl.BlockSpec((1, width, hidden), lambda j: (j, 0, 0))
    counts = (quarter,) * 4 if direct else (quarter,) * 3 + (quarter // 2,) * 2
    return pl.pallas_call(
        functools.partial(act_kernel, cap, window, direct),
        grid=(n_local,),
        out_shape=tuple(jax.ShapeDtypeStruct((count, wide), BF) for count in counts)
        + (jax.ShapeDtypeStruct((quarter, LANES), F32),),
        in_specs=[whole_smem(), whole_smem()]
        + payload_specs(chunk, width)
        + [whole_vmem()] * 2
        + [by_expert] * 3,
        out_specs=(whole_vmem(),) * (len(counts) + 1),
        scratch_shapes=[pltpu.VMEM((cap, wide), F32), pltpu.VMEM((cap, LANES), F32)],
        compiler_params=pltpu.CompilerParams(
            vmem_limit_bytes=vmem_limit(chunk["payload"].shape[0])
        ),
        cost_estimate=cost(1e10),
        name="acts",
    )(
        idx, chunk["offs"], chunk["payload"], chunk["payload"], chunk["pos"], chunk["gate"],
        *weights,
    )


def unit_kernel(direct, _, *refs):
    parts, (gate, grads, route_part) = refs[:-3], refs[-3:]
    quarter, wide = grads.shape
    half = quarter // 2
    hidden = wide // 3
    for side in range(2):
        rows = slice(side * half, (side + 1) * half)
        if direct:
            sources = [(part, rows) for part in parts]
        else:
            own, from_x, from_y, late_x, late_y = parts
            near, late = ((from_x, late_y), (from_y, late_x))[side]
            sources = [(own, rows), (near, slice(half, quarter)), (late, slice(0, half))]

        def total(part):
            at = slice(part * hidden, (part + 1) * hidden)
            value = None
            for source, there in sources:
                term = source[there, at].astype(F32)
                value = term if value is None else value + term
            return value

        gate_act, up_act, back = total(0), total(1), total(2)
        sigma = 1.0 / (1.0 + jnp.exp(-gate_act))
        active = gate_act * sigma
        slope = sigma * (1.0 + gate_act * (1.0 - sigma))
        scaled = gate[rows, 0:1] * back
        unit = (active * up_act).astype(BF)
        grads[rows, 0:hidden] = (scaled * up_act * slope).astype(BF)
        grads[rows, hidden : 2 * hidden] = (scaled * active).astype(BF)
        grads[rows, 2 * hidden :] = unit
        sums = jnp.sum(back * unit.astype(F32), axis=1, keepdims=True)
        route_part[rows, :] = jnp.broadcast_to(sums, (half, LANES)).astype(BF)


def unit_grads(direct, parts, earlier):
    quarter, wide = parts[0].shape
    return pl.pallas_call(
        functools.partial(unit_kernel, direct),
        out_shape=(
            jax.ShapeDtypeStruct((quarter, wide), BF),
            jax.ShapeDtypeStruct((quarter, LANES), BF),
        ),
        in_specs=[pl.BlockSpec(memory_space=pl.ANY)] + [whole_vmem()] * len(parts),
        out_specs=(whole_vmem(),) * 2,
        compiler_params=pltpu.CompilerParams(vmem_limit_bytes=24 * MIB),
        name="units",
    )(earlier, *parts)


def place_quarters(me, pieces, target):
    own, from_x, from_y, first, second = pieces
    quarter = own.shape[0]
    half = quarter // 2

    def at(other, extra, count):
        return pl.ds(pl.multiple_of((me ^ other) * quarter + extra, ALIGN), count)

    target[at(0, 0, quarter), :] = own[...]
    target[at(1, 0, quarter), :] = from_x[...]
    target[at(2, 0, quarter), :] = from_y[...]
    target[at(3, 0, half), :] = first[...]
    target[at(3, half, half), :] = second[...]


def window_hits(members, caps, windows, total, offs, poss, expert):
    places, starts, lane_start = [], [], 0
    for c in members:
        start = window_start(offs[c], expert, caps[c], windows[c])
        column = expert_column(poss[c][...], expert)
        places.append(jnp.where(column >= 0, column - start + lane_start, -1))
        starts.append((c, start, lane_start))
        lane_start += windows[c]
    places = jnp.concatenate(places, axis=0)
    lanes = lax.broadcasted_iota(jnp.int32, (places.shape[0], total), 1)
    return places == lanes, starts


def token_kernel(caps, windows, groups, top, block, group, idx, *refs):
    count = len(caps)
    offs, refs = refs[:count], refs[count:]
    pieces, refs = refs[: 5 * count], refs[5 * count :]
    routes_own, poss, metas = (refs[i * count : (i + 1) * count] for i in range(3))
    refs = refs[3 * count :]
    w_gate, w_up, keep, send = refs[:4]
    grads, routes, refs = refs[4 : 4 + count], refs[4 + count : 4 + 2 * count], refs[4 + 2 * count :]
    acc, route_acc = refs[:2]
    stacks, route_stacks = refs[2 : 2 + len(groups)], refs[2 + len(groups) :]
    expert = pl.program_id(0)
    _, width, hidden = w_gate.shape
    n_local = pl.num_programs(0)

    @pl.when(expert == 0)
    def _():
        for c in range(count):
            place_quarters(idx[2], pieces[5 * c : 5 * c + 5], grads[c])
            routes[c][...] = jnp.zeros_like(routes[c])
            quarter = caps[c] // 4
            at = pl.ds(pl.multiple_of(idx[2] * quarter, ALIGN), quarter)
            routes[c][at, :] = routes_own[c][...]
        acc[...] = jnp.zeros_like(acc)
        route_acc[...] = jnp.zeros_like(route_acc)
        for stacked in stacks + route_stacks:
            stacked[...] = jnp.zeros_like(stacked)

    named = (expert + idx[0] * n_local).astype(F32)
    token_start = 0
    for members, stacked, route_stacked in zip(groups, stacks, route_stacks):
        hit, starts = window_hits(
            members, caps, windows, stacked.shape[0], offs, poss, expert
        )
        for c, start, lane_start in starts:
            there = slice(lane_start, lane_start + windows[c])
            stacked[there, :] = grads[c][pl.ds(start, windows[c]), :]
            route_stacked[there, :] = routes[c][pl.ds(start, windows[c]), :]
        pick = jnp.where(hit, 1.0, 0.0).astype(BF)
        row_grad = lax.dot_general(
            stacked[:, 0:hidden], w_gate[0], BY_COLUMN, preferred_element_type=F32
        ) + lax.dot_general(
            stacked[:, hidden : 2 * hidden],
            w_up[0],
            BY_COLUMN,
            preferred_element_type=F32,
        )
        rows = slice(token_start, token_start + hit.shape[0])
        acc[rows, :] += jnp.dot(pick, row_grad.astype(BF), preferred_element_type=F32)
        meta = jnp.concatenate([metas[c][...] for c in members], axis=0).astype(F32)
        lane = lax.broadcasted_iota(jnp.int32, meta.shape, 1)
        token_route = jnp.dot(pick, route_stacked[...], preferred_element_type=F32)
        route_acc[rows, :] = jnp.where(
            jnp.logical_and(lane < top, meta == named), token_route, route_acc[rows, :]
        )
        token_start += hit.shape[0]

    @pl.when(expert == n_local - 1)
    def _():
        blocks = group // block
        row = lax.broadcasted_iota(jnp.int32, (block, group), 0)
        column = lax.broadcasted_iota(jnp.int32, (block, group), 1)
        for target, which in ((keep, idx[1]), (send, 1 - idx[1])):
            chosen = jnp.where(column == row * blocks + which, 1.0, 0.0).astype(BF)
            for first in range(acc.shape[0] // group):
                rows = slice(first * group, (first + 1) * group)
                there = slice(first * block, (first + 1) * block)
                for lanes, values in ((slice(0, width), acc), (slice(width, None), route_acc)):
                    target[there, lanes] = jnp.dot(
                        chosen, values[rows, :].astype(BF), preferred_element_type=F32
                    ).astype(BF)


def chunk_groups(count, windows):
    groups = [tuple(range(min(count, 3)))] + [(c,) for c in range(3, count)]
    return groups, [round_up(sum(windows[c] for c in members), LANES) for members in groups]


def token_grads(idx, chunks, pieces, route_parts, weights, caps, windows, top, block, group):
    n_local, width, hidden = weights[0].shape
    by_expert = pl.BlockSpec((1, width, hidden), lambda j: (j, 0, 0))
    count = len(chunks)
    groups, totals = chunk_groups(count, windows)
    tokens = sum(chunk["payload"].shape[0] for chunk in chunks)
    result = jax.ShapeDtypeStruct((tokens // 2, width + LANES), BF)
    flat = [piece for group in pieces for piece in group]
    return pl.pallas_call(
        functools.partial(token_kernel, caps, windows, groups, top, block, group),
        grid=(n_local,),
        out_shape=(result, result),
        in_specs=[whole_smem()] * (1 + count)
        + [pl.BlockSpec((piece.shape[0], 2 * hidden), lambda j: (0, 0)) for piece in flat]
        + [whole_vmem()] * (2 * count)
        + [
            pl.BlockSpec((chunk["payload"].shape[0], LANES), lambda j: (0, 2 * width // LANES))
            for chunk in chunks
        ]
        + [by_expert] * 2,
        out_specs=(whole_vmem(),) * 2,
        scratch_shapes=[pltpu.VMEM((cap, 2 * hidden), BF) for cap in caps]
        + [pltpu.VMEM((cap, LANES), BF) for cap in caps]
        + [pltpu.VMEM((tokens, width), F32), pltpu.VMEM((tokens, LANES), F32)]
        + [pltpu.VMEM((total, 2 * hidden), BF) for total in totals]
        + [pltpu.VMEM((total, LANES), BF) for total in totals],
        compiler_params=pltpu.CompilerParams(vmem_limit_bytes=vmem_limit(tokens)),
        cost_estimate=cost(1e10),
        name="tokens",
    )(
        idx,
        *[chunk["offs"] for chunk in chunks],
        *flat,
        *route_parts,
        *[chunk["pos"] for chunk in chunks],
        *[chunk["payload"] for chunk in chunks],
        *weights[:2],
    )


def weight_kernel(caps, windows, groups, idx, *refs):
    count = len(caps)
    offs, refs = refs[:count], refs[count:]
    pieces, refs = refs[: 5 * count], refs[5 * count :]
    xs, dys, poss, gates = (refs[i * count : (i + 1) * count] for i in range(4))
    refs = refs[4 * count :]
    outs, done, grads, refs = refs[:3], refs[3], refs[4 : 4 + count], refs[4 + count :]
    x_turned, dy_turned, stacks = refs[0], refs[1], refs[2:]
    expert = pl.program_id(0)
    hidden = outs[0].shape[2]

    @pl.when(expert == 0)
    def _():
        for c in range(count):
            place_quarters(idx[2], pieces[5 * c : 5 * c + 5], grads[c])
        x_turned[...] = jnp.concatenate([ref[...] for ref in xs], axis=0).T
        dy_turned[...] = jnp.concatenate([ref[...] for ref in dys], axis=0).T
        for stacked in stacks:
            stacked[...] = jnp.zeros_like(stacked)
        done[...] = jnp.zeros_like(done)

    sums, token_start = [None] * 3, 0
    for members, stacked in zip(groups, stacks):
        hit, starts = window_hits(
            members, caps, windows, stacked.shape[0], offs, poss, expert
        )
        for c, start, lane_start in starts:
            there = slice(lane_start, lane_start + windows[c])
            stacked[there, :] = grads[c][pl.ds(start, windows[c]), :]
        scale = jnp.concatenate([expert_column(gates[c][...], expert) for c in members], axis=0)
        pick = jnp.where(hit, 1.0, 0.0).astype(BF)
        pick_scaled = jnp.where(hit, scale, 0.0).astype(BF)
        lanes = slice(token_start, token_start + hit.shape[0])
        slot_x = jnp.dot(x_turned[:, lanes], pick, preferred_element_type=F32).astype(BF)
        slot_dy = jnp.dot(dy_turned[:, lanes], pick_scaled, preferred_element_type=F32).astype(BF)
        for part, left in enumerate((slot_x, slot_x, slot_dy)):
            columns = slice(part * hidden, (part + 1) * hidden)
            value = jnp.dot(left, stacked[:, columns], preferred_element_type=F32)
            sums[part] = value if sums[part] is None else sums[part] + value
        token_start += hit.shape[0]
    for out, value in zip(outs, sums):
        out[0] = value.astype(BF)


def weight_grads(idx, chunks, pieces, caps, windows, n_local, width, hidden):
    count = len(chunks)
    wide = 3 * hidden
    groups, totals = chunk_groups(count, windows)
    tokens = sum(chunk["payload"].shape[0] for chunk in chunks)
    by_expert = pl.BlockSpec((1, width, hidden), lambda j: (j, 0, 0))
    return pl.pallas_call(
        functools.partial(weight_kernel, caps, windows, groups),
        grid=(n_local,),
        out_shape=(jax.ShapeDtypeStruct((n_local, width, hidden), BF),) * 3
        + (jax.ShapeDtypeStruct((8, LANES), F32),),
        in_specs=[whole_smem()] * (1 + count)
        + [whole_vmem()] * (5 * count)
        + [payload_specs(chunk, width)[side] for side in range(2) for chunk in chunks]
        + [whole_vmem()] * (2 * count),
        out_specs=(by_expert,) * 3 + (whole_vmem(),),
        scratch_shapes=[pltpu.VMEM((cap, wide), BF) for cap in caps]
        + [pltpu.VMEM((width, tokens), BF)] * 2
        + [pltpu.VMEM((total, wide), BF) for total in totals],
        compiler_params=pltpu.CompilerParams(
            vmem_limit_bytes=(32 if tokens <= 512 else 56) * MIB
        ),
        cost_estimate=cost(2e10),
        name="weights",
    )(
        idx,
        *[chunk["offs"] for chunk in chunks],
        *[piece for group in pieces for piece in group],
        *[chunk["payload"] for chunk in chunks],
        *[chunk["payload"] for chunk in chunks],
        *[chunk["pos"] for chunk in chunks],
        *[chunk["gate"] for chunk in chunks],
    )


def to_partner(value, axis, other):
    return lax.ppermute(value, axis, [(i, i ^ other) for i in range(lax.axis_size(axis))])


def sum_over_dp(parts, direct):
    parts, gate = parts[:-1], parts[-1]
    if direct:
        got = [to_partner(parts[k], "dp", k) for k in range(1, len(parts))]
        return [parts[0]] + got + [gate]
    own, send_x, send_y, later_x, later_y = parts
    half = own.shape[0] // 2
    from_x = to_partner(send_x, "dp", 1)
    from_y = to_partner(send_y, "dp", 2)
    late_x = to_partner(later_x + from_y[:half], "dp", 1)
    late_y = to_partner(later_y + from_x[:half], "dp", 2)
    return [own, from_x, from_y, late_x, late_y, gate]


def gather_over_dp(own):
    half = own.shape[0] // 2
    from_x = to_partner(own, "dp", 1)
    from_y = to_partner(own, "dp", 2)
    first = to_partner(from_x[:half], "dp", 2)
    second = to_partner(from_y[half:], "dp", 1)
    return own, from_x, from_y, first, second


def finish_kernel(width, top, idx, *refs):
    parts, (token_grad, route_grad) = refs[:-2], refs[-2:]
    routes = None
    for distance, part in enumerate(parts):
        at = pl.ds(pl.multiple_of((idx[2] ^ distance) * width, LANES), width)
        token_grad[:, at] = part[:, 0:width]
        value = part[:, width:].astype(F32)
        routes = value if routes is None else routes + value
    route_grad[...] = routes[:, 0:top].astype(BF)


def finish(idx, parts, width, top):
    rows = parts[0].shape[0]
    return pl.pallas_call(
        functools.partial(finish_kernel, width, top),
        out_shape=(
            jax.ShapeDtypeStruct((rows, width * len(parts)), BF),
            jax.ShapeDtypeStruct((rows, top), BF),
        ),
        in_specs=[whole_smem()] + [whole_vmem()] * len(parts),
        out_specs=(whole_vmem(),) * 2,
        compiler_params=pltpu.CompilerParams(vmem_limit_bytes=24 * MIB),
        name="finish",
    )(idx, *parts)


def in_hbm(value):
    return pltpu.with_memory_space_constraint(value, pltpu.HBM)


def relay_kernel(_, *refs):
    parts, out = refs[:-1], refs[-1]
    first = 0
    for part in parts:
        out[first : first + part.shape[0], :] = part[...]
        first += part.shape[0]


def relay(parts, earlier):
    rows = sum(part.shape[0] for part in parts)
    return pl.pallas_call(
        relay_kernel,
        out_shape=jax.ShapeDtypeStruct((rows, parts[0].shape[1]), BF),
        in_specs=[pl.BlockSpec(memory_space=pl.ANY)] + [whole_vmem()] * len(parts),
        out_specs=whole_vmem(),
        compiler_params=pltpu.CompilerParams(vmem_limit_bytes=24 * MIB),
        name="relay",
    )(earlier, *parts)


def add_kernel(count, _, *refs):
    parts, outs = refs[:count], refs[count:]
    total = parts[0][...].astype(F32)
    for part in parts[1:]:
        total = total + part[...].astype(F32)
    rows = outs[0].shape[0]
    for i, out in enumerate(outs):
        out[...] = total[i * rows : (i + 1) * rows, :].astype(BF)


def add_up(parts, earlier, pieces):
    rows, lanes = parts[0].shape
    return pl.pallas_call(
        functools.partial(add_kernel, len(parts)),
        out_shape=(jax.ShapeDtypeStruct((rows // pieces, lanes), BF),) * pieces,
        in_specs=[pl.BlockSpec(memory_space=pl.ANY)] + [whole_vmem()] * len(parts),
        out_specs=(whole_vmem(),) * pieces,
        compiler_params=pltpu.CompilerParams(vmem_limit_bytes=24 * MIB),
        name="add",
    )(earlier, *parts)


def on_device(tokens_in, cotangent, expert_ids, gate_probs, gate_weight, up_weight, down_weight):
    n_expert, n_dp = lax.axis_size("expert"), lax.axis_size("dp")
    expert_at, half_at, dp_at = (lax.axis_index(name) for name in ("expert", "half", "dp"))
    idx = jnp.stack([expert_at, half_at, dp_at]).astype(jnp.int32)
    n_local, width, hidden = gate_weight.shape
    weights = tuple(in_hbm(weight) for weight in (gate_weight, up_weight, down_weight))
    _, blocks, block_tokens, _ = tokens_in.shape
    top = expert_ids.shape[3]
    block = n_dp * block_tokens
    owner_rows = blocks * block_tokens
    group = blocks * block

    parts = pack(
        idx,
        in_hbm(tokens_in[0].transpose(1, 0, 2)),
        in_hbm(cotangent[0].transpose(1, 0, 2)),
        in_hbm(expert_ids[0].transpose(0, 2, 1)),
        in_hbm(gate_probs[0].transpose(0, 2, 1)),
        n_dp,
        width,
    )
    parts = [parts[0]] + [to_partner(parts[k], "dp", k) for k in range(1, n_dp)]

    def put_together(parts, kind, span):
        return route(idx, parts, kind, span * group, n_local, top, width, owner_rows)

    own, mixed = put_together(parts, "own", 1)
    chunks, sums, caps, windows, held = [], [], [], [], 0
    while held < n_expert:
        if held == 0:
            chunk, span = own, 1
        else:
            if held == 1:
                got = [to_partner(mixed, "expert", k) for k in (1, 2) if k < n_expert]
                far = relay(got, sums[0][-1])
            elif held == 3:
                far = to_partner(got[1], "expert", 1)
            else:
                known = jnp.concatenate([chunk["payload"] for chunk in chunks], axis=0)
                side = jnp.where(half_at == 0, known[:, :width], known[:, width : 2 * width])
                far = jnp.concatenate([side, known[:, 2 * width :]], axis=1)
                far = to_partner(far, "expert", held)
            span = far.shape[0] // group
            chunk = put_together([far, to_partner(far, "half", 1)], "far", span)
        most = span * group // 2
        chunks.append(chunk)
        caps.append(round_up(n_local * most, LANES))
        windows.append(round_up(most + ALIGN, ALIGN))
        wide_window = round_up(most + ALIGN, LANES)
        sums.append(partial_acts(idx, chunk, weights, caps[-1], wide_window, held == 0))
        held += span

    pieces, route_parts = [], []
    for i, parts in enumerate(sums):
        earlier = sums[1][-1] if i == 0 and len(sums) > 1 else parts[-1]
        grads, route_part = unit_grads(i == 0, sum_over_dp(parts, i == 0), earlier)
        pieces.append(gather_over_dp(grads))
        route_parts.append(route_part)

    keep, send = token_grads(
        idx, chunks, pieces, route_parts, weights, caps, windows, top, block, group
    )
    both = (keep.astype(F32) + to_partner(send, "half", 1).astype(F32)).astype(BF)
    *weight_out, written = weight_grads(
        idx, chunks, pieces, caps, windows, n_local, width, hidden
    )
    held = jnp.split(both, n_expert, axis=0)
    step = n_expert // 2
    while step > 2:
        got = to_partner(jnp.concatenate(held[step:], axis=0), "expert", step)
        held = [
            (mine.astype(F32) + other.astype(F32)).astype(BF)
            for mine, other in zip(held[:step], jnp.split(got, step, axis=0))
        ]
        step //= 2
    total = held[:1] + [to_partner(held[k], "expert", k) for k in range(1, len(held))]
    total = add_up(total, written, n_dp)
    total = [total[0]] + [to_partner(total[k], "dp", k) for k in range(1, n_dp)]
    token_grad, route_grad = finish(idx, total, width, top)
    return (token_grad[None, None], route_grad[None, None]) + tuple(weight_out)


def solution(mesh):
    return jax.shard_map(
        on_device,
        mesh=mesh,
        in_specs=(
            P(("expert", "dp"), None, None, None),
            P(("expert", "dp"), None, None, None),
            P(("expert", "dp"), None, None, None),
            P(("expert", "dp"), None, None, None),
            P("expert", "dp", "half"),
            P("expert", "dp", "half"),
            P("expert", "dp", "half"),
        ),
        out_specs=(
            P(("expert", "dp"), "half", None, None),
            P(("expert", "dp"), "half", None, None),
            P("expert", "dp", "half"),
            P("expert", "dp", "half"),
            P("expert", "dp", "half"),
        ),
        check_vma=False,
    )
```

```python
import functools

import jax
import jax.numpy as jnp
from jax import lax
from jax.experimental import pallas as pl
from jax.experimental.pallas import tpu as pltpu
from jax.sharding import PartitionSpec as P

LANES = 128
ALIGN = 16
BF = jnp.bfloat16
F32 = jnp.float32
BY_ROW = (((0,), (0,)), ((), ()))
BY_COLUMN = (((1,), (1,)), ((), ()))
MIB = 1 << 20


def round_up(value, step):
    return -(-value // step) * step


def cost(flops):
    return pl.CostEstimate(flops=int(flops), bytes_accessed=0, transcendentals=0)


def vmem_limit(rows):
    return (24 if rows <= 512 else 56) * MIB


def whole_vmem():
    return pl.BlockSpec(memory_space=pltpu.VMEM)


def whole_smem():
    return pl.BlockSpec(memory_space=pltpu.SMEM)


def expert_column(table, expert):
    lane = lax.broadcasted_iota(jnp.int32, table.shape, 1)
    return jnp.sum(jnp.where(lane == expert, table, 0), axis=1, keepdims=True)


def window_start(offs, expert, cap, window):
    start = jnp.minimum((offs[0, expert] // ALIGN) * ALIGN, cap - window)
    return pl.multiple_of(start, ALIGN)


def pack_kernel(width, top, idx, x, dy, ids, gates, *outs):
    tokens, blocks, _ = x.shape
    rows = tokens * blocks
    row = lax.broadcasted_iota(jnp.int32, (rows, tokens), 0)
    token = lax.broadcasted_iota(jnp.int32, (rows, tokens), 1)
    fill = jnp.full((LANES - 2 * top, tokens), -1.0, BF)
    meta = jnp.zeros((rows, LANES), F32)
    for block in range(blocks):
        place = jnp.where(row == token * blocks + block, 1.0, 0.0).astype(BF)
        table = jnp.concatenate([ids[block].astype(F32).astype(BF), gates[block], fill], axis=0)
        meta += lax.dot_general(place, table, BY_COLUMN, preferred_element_type=F32)
    for distance, out in enumerate(outs):
        at = pl.ds(pl.multiple_of((idx[2] ^ distance) * width, LANES), width)
        for t in range(tokens):
            there = slice(t * blocks, (t + 1) * blocks)
            out[there, 0:width] = x[t, :, at]
            out[there, width : 2 * width] = dy[t, :, at]
        out[:, 2 * width :] = meta.astype(BF)


def pack(idx, x, dy, ids, gates, n_dp, width):
    shape = (x.shape[0] * x.shape[1], 2 * width + LANES)
    return pl.pallas_call(
        functools.partial(pack_kernel, width, ids.shape[1]),
        out_shape=(jax.ShapeDtypeStruct(shape, BF),) * n_dp,
        in_specs=[whole_smem()] + [whole_vmem()] * 4,
        out_specs=(whole_vmem(),) * n_dp,
        compiler_params=pltpu.CompilerParams(vmem_limit_bytes=24 * MIB),
        name="pack",
    )(idx, x, dy, ids, gates)


def shared_order(place, step, dp_at):
    owner = ((place.astype(F32) + 0.5) * (1.0 / step)).astype(jnp.int32)
    return place + ((owner ^ dp_at) - owner) * step


def route_kernel(n_local, n_expert, unit, top, width, step, kind, count, _, idx, *refs):
    parts, (pos, gate, offs, payload), rest = refs[:count], refs[count : count + 4], refs[count + 4 :]
    if kind == "own":
        for distance, part in enumerate(parts):
            payload[distance * step : (distance + 1) * step, :] = part[...]
        mixed, fits = rest
        mixed[:, 0:width] = jnp.where(
            idx[1] == 0, payload[:, 0:width], payload[:, width : 2 * width]
        )
        lane = lax.broadcasted_iota(jnp.int32, gate.shape, 1)
        names = payload[:, 2 * width :].astype(F32)
        first_name = (lane * n_local).astype(F32)
        named = jnp.zeros(gate.shape, F32)
        for k in range(top):
            name = names[:, k : k + 1]
            inside = jnp.logical_and(name >= first_name, name < first_name + n_local)
            named += jnp.where(jnp.logical_and(inside, lane < n_expert), 1.0, 0.0)
        elsewhere = jnp.where(lane == idx[0], 0.0, named)
        most = jnp.max(jnp.sum(elsewhere, axis=0, keepdims=True), axis=1, keepdims=True)
        flag = jnp.where(most <= unit, 1.0, 0.0)
        fits[...] = jnp.broadcast_to(flag, fits.shape)
        mixed[:, width:] = jnp.where(lane == 2 * top, flag, names).astype(BF)
    else:
        first = 0
        for near, other in zip(parts[: count // 2], parts[count // 2 :]):
            rows = slice(first, first + near.shape[0])
            payload[rows, 0:width] = jnp.where(idx[1] == 0, near[:, 0:width], other[:, 0:width])
            payload[rows, width : 2 * width] = jnp.where(
                idx[1] == 0, other[:, 0:width], near[:, 0:width]
            )
            payload[rows, 2 * width :] = near[:, width:]
            first += near.shape[0]
    rows = payload.shape[0]
    meta = payload[:, 2 * width :].astype(F32)
    lane = lax.broadcasted_iota(jnp.int32, (rows, LANES), 1)
    here = (lane + idx[0] * n_local).astype(F32)
    chosen = jnp.zeros((rows, LANES), F32)
    gates = jnp.zeros((rows, LANES), F32)
    for k in range(top):
        hit = jnp.logical_and(meta[:, k : k + 1] == here, lane < n_local)
        chosen = jnp.where(hit, 1.0, chosen)
        gates = jnp.where(hit, meta[:, top + k : top + k + 1], gates)
    place_column = shared_order(lax.broadcasted_iota(jnp.int32, (rows, 1), 0), step, idx[2])
    place_row = shared_order(lax.broadcasted_iota(jnp.int32, (1, rows), 1), step, idx[2])
    earlier = jnp.where(place_row < place_column, 1.0, 0.0)
    rank = jnp.dot(earlier.astype(BF), chosen.astype(BF), preferred_element_type=F32)
    counts = jnp.broadcast_to(jnp.sum(chosen, axis=0, keepdims=True), (8, LANES))
    before = (
        lax.broadcasted_iota(jnp.int32, (LANES, LANES), 0)
        < lax.broadcasted_iota(jnp.int32, (LANES, LANES), 1)
    )
    starts = jnp.dot(
        counts, before.astype(F32), preferred_element_type=F32, precision=lax.Precision.HIGHEST
    )
    pos[...] = jnp.where(chosen > 0.0, rank + starts[0:1], -1.0).astype(jnp.int32)
    gate[...] = gates
    offs[...] = starts.astype(jnp.int32)


def route(earlier, idx, parts, kind, rows, n_local, n_expert, unit, top, width, step):
    out_shape = [
        jax.ShapeDtypeStruct((rows, LANES), jnp.int32),
        jax.ShapeDtypeStruct((rows, LANES), F32),
        jax.ShapeDtypeStruct((8, LANES), jnp.int32),
        jax.ShapeDtypeStruct((rows, 2 * width + LANES), BF),
    ]
    if kind == "own":
        out_shape.append(jax.ShapeDtypeStruct((rows, width + LANES), BF))
        out_shape.append(jax.ShapeDtypeStruct((8, LANES), F32))
    out = pl.pallas_call(
        functools.partial(
            route_kernel, n_local, n_expert, unit, top, width, step, kind, len(parts)
        ),
        out_shape=tuple(out_shape),
        in_specs=[pl.BlockSpec(memory_space=pl.ANY), whole_smem()] + [whole_vmem()] * len(parts),
        out_specs=(whole_vmem(),) * len(out_shape),
        compiler_params=pltpu.CompilerParams(vmem_limit_bytes=vmem_limit(rows)),
        name="route",
    )(earlier, idx, *parts)
    chunk = {"pos": out[0], "gate": out[1], "offs": out[2], "payload": out[3]}
    return (chunk, out[4], out[5]) if kind == "own" else chunk


def act_kernel(cap, window, idx, offs, x, dy, pos, gate, w_gate, w_up, w_down, *refs):
    outs, (own_gate, acc, gate_acc) = refs[:-3], refs[-3:]
    expert = pl.program_id(0)
    hidden = w_gate.shape[2]
    quarter = cap // 4
    half = quarter // 2

    @pl.when(expert == 0)
    def _():
        acc[...] = jnp.zeros_like(acc)
        gate_acc[...] = jnp.zeros_like(gate_acc)

    start = window_start(offs, expert, cap, window)
    column = expert_column(pos[...], expert)
    slot = lax.broadcasted_iota(jnp.int32, (x.shape[0], window), 1)
    pick = jnp.where(jnp.logical_and(column >= 0, column - start == slot), 1.0, 0.0).astype(BF)
    gate_col = jnp.broadcast_to(expert_column(gate[...], expert), gate.shape).astype(BF)
    slot_x = lax.dot_general(pick, x[...], BY_ROW, preferred_element_type=F32).astype(BF)
    slot_dy = lax.dot_general(pick, dy[...], BY_ROW, preferred_element_type=F32).astype(BF)
    slot_gate = lax.dot_general(pick, gate_col, BY_ROW, preferred_element_type=F32)
    row = start + lax.broadcasted_iota(jnp.int32, (window, 1), 0)
    mine = jnp.logical_and(row >= offs[0, expert], row < offs[0, expert + 1])
    rows = pl.ds(start, window)
    gate_acc[rows, :] = jnp.where(mine, slot_gate, gate_acc[rows, :])
    for part, (left, right) in enumerate(((slot_x, w_gate), (slot_x, w_up), (slot_dy, w_down))):
        columns = slice(part * hidden, (part + 1) * hidden)
        value = jnp.dot(left, right[0], preferred_element_type=F32)
        acc[rows, columns] = jnp.where(mine, value, acc[rows, columns])

    @pl.when(expert == pl.num_programs(0) - 1)
    def _():
        me = idx[2]

        def piece(other, first, count):
            at = pl.multiple_of((me ^ other) * quarter + first, ALIGN)
            return acc[pl.ds(at, count), :].astype(BF)

        own_gate[...] = gate_acc[pl.ds(pl.multiple_of(me * quarter, ALIGN), quarter), :]
        own, send_x, send_y, later_x, later_y = outs
        own[...] = piece(0, 0, quarter)
        send_x[0:half, :] = piece(3, 0, half)
        send_x[half:quarter, :] = piece(1, 0, half)
        send_y[0:half, :] = piece(3, half, half)
        send_y[half:quarter, :] = piece(2, half, half)
        later_x[...] = piece(1, half, half)
        later_y[...] = piece(2, 0, half)


def payload_specs(chunk, width):
    rows = chunk["payload"].shape[0]
    return [pl.BlockSpec((rows, width), lambda j, part=part: (0, part)) for part in range(2)]


def partial_acts(idx, chunk, weights, cap, window):
    n_local, width, hidden = weights[0].shape
    quarter, wide = cap // 4, 3 * hidden
    by_expert = pl.BlockSpec((1, width, hidden), lambda j: (j, 0, 0))
    counts = (quarter,) * 3 + (quarter // 2,) * 2
    return pl.pallas_call(
        functools.partial(act_kernel, cap, window),
        grid=(n_local,),
        out_shape=tuple(jax.ShapeDtypeStruct((count, wide), BF) for count in counts)
        + (jax.ShapeDtypeStruct((quarter, LANES), F32),),
        in_specs=[whole_smem(), whole_smem()]
        + payload_specs(chunk, width)
        + [whole_vmem()] * 2
        + [by_expert] * 3,
        out_specs=(whole_vmem(),) * (len(counts) + 1),
        scratch_shapes=[pltpu.VMEM((cap, wide), F32), pltpu.VMEM((cap, LANES), F32)],
        compiler_params=pltpu.CompilerParams(
            vmem_limit_bytes=vmem_limit(chunk["payload"].shape[0])
        ),
        cost_estimate=cost(1e10),
        name="acts",
    )(
        idx, chunk["offs"], chunk["payload"], chunk["payload"], chunk["pos"], chunk["gate"],
        *weights,
    )


def unit_kernel(_, *refs):
    parts, (gate, grads, route_part) = refs[:-3], refs[-3:]
    quarter, wide = grads.shape
    half = quarter // 2
    hidden = wide // 3
    for side in range(2):
        rows = slice(side * half, (side + 1) * half)
        own, from_x, from_y, late_x, late_y = parts
        near, late = ((from_x, late_y), (from_y, late_x))[side]
        sources = [(own, rows), (near, slice(half, quarter)), (late, slice(0, half))]

        def total(part):
            at = slice(part * hidden, (part + 1) * hidden)
            value = None
            for source, there in sources:
                term = source[there, at].astype(F32)
                value = term if value is None else value + term
            return value

        gate_act, up_act, back = total(0), total(1), total(2)
        sigma = 1.0 / (1.0 + jnp.exp(-gate_act))
        active = gate_act * sigma
        slope = sigma * (1.0 + gate_act * (1.0 - sigma))
        scaled = gate[rows, 0:1] * back
        unit = (active * up_act).astype(BF)
        grads[rows, 0:hidden] = (scaled * up_act * slope).astype(BF)
        grads[rows, hidden : 2 * hidden] = (scaled * active).astype(BF)
        grads[rows, 2 * hidden :] = unit
        sums = jnp.sum(back * unit.astype(F32), axis=1, keepdims=True)
        route_part[rows, :] = jnp.broadcast_to(sums, (half, LANES)).astype(BF)


def unit_grads(parts, earlier):
    quarter, wide = parts[0].shape
    return pl.pallas_call(
        unit_kernel,
        out_shape=(
            jax.ShapeDtypeStruct((quarter, wide), BF),
            jax.ShapeDtypeStruct((quarter, LANES), BF),
        ),
        in_specs=[pl.BlockSpec(memory_space=pl.ANY)] + [whole_vmem()] * len(parts),
        out_specs=(whole_vmem(),) * 2,
        compiler_params=pltpu.CompilerParams(vmem_limit_bytes=24 * MIB),
        name="units",
    )(earlier, *parts)


def place_quarters(me, pieces, target):
    own, from_x, from_y, first, second = pieces
    quarter = own.shape[0]
    half = quarter // 2

    def at(other, extra, count):
        return pl.ds(pl.multiple_of((me ^ other) * quarter + extra, ALIGN), count)

    target[at(0, 0, quarter), :] = own[...]
    target[at(1, 0, quarter), :] = from_x[...]
    target[at(2, 0, quarter), :] = from_y[...]
    target[at(3, 0, half), :] = first[...]
    target[at(3, half, half), :] = second[...]


def window_hits(members, caps, windows, total, offs, poss, expert):
    places, starts, lane_start = [], [], 0
    for c in members:
        start = window_start(offs[c], expert, caps[c], windows[c])
        column = expert_column(poss[c][...], expert)
        places.append(jnp.where(column >= 0, column - start + lane_start, -1))
        starts.append((c, start, lane_start))
        lane_start += windows[c]
    places = jnp.concatenate(places, axis=0)
    lanes = lax.broadcasted_iota(jnp.int32, (places.shape[0], total), 1)
    return places == lanes, starts


def token_kernel(caps, windows, groups, top, block, group, idx, *refs):
    count = len(caps)
    offs, refs = refs[:count], refs[count:]
    pieces, refs = refs[: 5 * count], refs[5 * count :]
    routes_own, poss, metas = (refs[i * count : (i + 1) * count] for i in range(3))
    refs = refs[3 * count :]
    w_gate, w_up, keep, send = refs[:4]
    grads, routes, refs = refs[4 : 4 + count], refs[4 + count : 4 + 2 * count], refs[4 + 2 * count :]
    acc, route_acc = refs[:2]
    stacks, route_stacks = refs[2 : 2 + len(groups)], refs[2 + len(groups) :]
    expert = pl.program_id(0)
    _, width, hidden = w_gate.shape
    n_local = pl.num_programs(0)

    @pl.when(expert == 0)
    def _():
        for c in range(count):
            place_quarters(idx[2], pieces[5 * c : 5 * c + 5], grads[c])
            routes[c][...] = jnp.zeros_like(routes[c])
            quarter = caps[c] // 4
            at = pl.ds(pl.multiple_of(idx[2] * quarter, ALIGN), quarter)
            routes[c][at, :] = routes_own[c][...]
        acc[...] = jnp.zeros_like(acc)
        route_acc[...] = jnp.zeros_like(route_acc)
        for stacked in stacks + route_stacks:
            stacked[...] = jnp.zeros_like(stacked)

    named = (expert + idx[0] * n_local).astype(F32)
    token_start = 0
    for members, stacked, route_stacked in zip(groups, stacks, route_stacks):
        hit, starts = window_hits(
            members, caps, windows, stacked.shape[0], offs, poss, expert
        )
        for c, start, lane_start in starts:
            there = slice(lane_start, lane_start + windows[c])
            stacked[there, :] = grads[c][pl.ds(start, windows[c]), :]
            route_stacked[there, :] = routes[c][pl.ds(start, windows[c]), :]
        pick = jnp.where(hit, 1.0, 0.0).astype(BF)
        row_grad = lax.dot_general(
            stacked[:, 0:hidden], w_gate[0], BY_COLUMN, preferred_element_type=F32
        ) + lax.dot_general(
            stacked[:, hidden : 2 * hidden],
            w_up[0],
            BY_COLUMN,
            preferred_element_type=F32,
        )
        rows = slice(token_start, token_start + hit.shape[0])
        acc[rows, :] += jnp.dot(pick, row_grad.astype(BF), preferred_element_type=F32)
        meta = jnp.concatenate([metas[c][...] for c in members], axis=0).astype(F32)
        lane = lax.broadcasted_iota(jnp.int32, meta.shape, 1)
        token_route = jnp.dot(pick, route_stacked[...], preferred_element_type=F32)
        route_acc[rows, :] = jnp.where(
            jnp.logical_and(lane < top, meta == named), token_route, route_acc[rows, :]
        )
        token_start += hit.shape[0]

    @pl.when(expert == n_local - 1)
    def _():
        blocks = group // block
        row = lax.broadcasted_iota(jnp.int32, (block, group), 0)
        column = lax.broadcasted_iota(jnp.int32, (block, group), 1)
        for target, which in ((keep, idx[1]), (send, 1 - idx[1])):
            chosen = jnp.where(column == row * blocks + which, 1.0, 0.0).astype(BF)
            for first in range(acc.shape[0] // group):
                rows = slice(first * group, (first + 1) * group)
                there = slice(first * block, (first + 1) * block)
                for lanes, values in ((slice(0, width), acc), (slice(width, None), route_acc)):
                    target[there, lanes] = jnp.dot(
                        chosen, values[rows, :].astype(BF), preferred_element_type=F32
                    ).astype(BF)


def chunk_groups(count, windows):
    groups = [tuple(range(min(count, 3)))] + [(c,) for c in range(3, count)]
    return groups, [round_up(sum(windows[c] for c in members), LANES) for members in groups]


def token_grads(idx, chunks, pieces, route_parts, weights, caps, windows, top, block, group):
    n_local, width, hidden = weights[0].shape
    by_expert = pl.BlockSpec((1, width, hidden), lambda j: (j, 0, 0))
    count = len(chunks)
    groups, totals = chunk_groups(count, windows)
    tokens = sum(chunk["payload"].shape[0] for chunk in chunks)
    result = jax.ShapeDtypeStruct((tokens // 2, width + LANES), BF)
    flat = [piece for group in pieces for piece in group]
    return pl.pallas_call(
        functools.partial(token_kernel, caps, windows, groups, top, block, group),
        grid=(n_local,),
        out_shape=(result, result),
        in_specs=[whole_smem()] * (1 + count)
        + [pl.BlockSpec((piece.shape[0], 2 * hidden), lambda j: (0, 0)) for piece in flat]
        + [whole_vmem()] * (2 * count)
        + [
            pl.BlockSpec((chunk["payload"].shape[0], LANES), lambda j: (0, 2 * width // LANES))
            for chunk in chunks
        ]
        + [by_expert] * 2,
        out_specs=(whole_vmem(),) * 2,
        scratch_shapes=[pltpu.VMEM((cap, 2 * hidden), BF) for cap in caps]
        + [pltpu.VMEM((cap, LANES), BF) for cap in caps]
        + [pltpu.VMEM((tokens, width), F32), pltpu.VMEM((tokens, LANES), F32)]
        + [pltpu.VMEM((total, 2 * hidden), BF) for total in totals]
        + [pltpu.VMEM((total, LANES), BF) for total in totals],
        compiler_params=pltpu.CompilerParams(vmem_limit_bytes=vmem_limit(tokens)),
        cost_estimate=cost(1e10),
        name="tokens",
    )(
        idx,
        *[chunk["offs"] for chunk in chunks],
        *flat,
        *route_parts,
        *[chunk["pos"] for chunk in chunks],
        *[chunk["payload"] for chunk in chunks],
        *weights[:2],
    )


def weight_kernel(caps, windows, groups, idx, *refs):
    count = len(caps)
    offs, refs = refs[:count], refs[count:]
    pieces, refs = refs[: 5 * count], refs[5 * count :]
    xs, dys, poss, gates = (refs[i * count : (i + 1) * count] for i in range(4))
    refs = refs[4 * count :]
    outs, done, grads, refs = refs[:3], refs[3], refs[4 : 4 + count], refs[4 + count :]
    x_turned, dy_turned, stacks = refs[0], refs[1], refs[2:]
    expert = pl.program_id(0)
    hidden = outs[0].shape[2]

    @pl.when(expert == 0)
    def _():
        for c in range(count):
            place_quarters(idx[2], pieces[5 * c : 5 * c + 5], grads[c])
        x_turned[...] = jnp.concatenate([ref[...] for ref in xs], axis=0).T
        dy_turned[...] = jnp.concatenate([ref[...] for ref in dys], axis=0).T
        for stacked in stacks:
            stacked[...] = jnp.zeros_like(stacked)
        done[...] = jnp.zeros_like(done)

    sums, token_start = [None] * 3, 0
    for members, stacked in zip(groups, stacks):
        hit, starts = window_hits(
            members, caps, windows, stacked.shape[0], offs, poss, expert
        )
        for c, start, lane_start in starts:
            there = slice(lane_start, lane_start + windows[c])
            stacked[there, :] = grads[c][pl.ds(start, windows[c]), :]
        scale = jnp.concatenate([expert_column(gates[c][...], expert) for c in members], axis=0)
        pick = jnp.where(hit, 1.0, 0.0).astype(BF)
        pick_scaled = jnp.where(hit, scale, 0.0).astype(BF)
        lanes = slice(token_start, token_start + hit.shape[0])
        slot_x = jnp.dot(x_turned[:, lanes], pick, preferred_element_type=F32).astype(BF)
        slot_dy = jnp.dot(dy_turned[:, lanes], pick_scaled, preferred_element_type=F32).astype(BF)
        for part, left in enumerate((slot_x, slot_x, slot_dy)):
            columns = slice(part * hidden, (part + 1) * hidden)
            value = jnp.dot(left, stacked[:, columns], preferred_element_type=F32)
            sums[part] = value if sums[part] is None else sums[part] + value
        token_start += hit.shape[0]
    for out, value in zip(outs, sums):
        out[0] = value.astype(BF)


def weight_grads(idx, chunks, pieces, caps, windows, n_local, width, hidden):
    count = len(chunks)
    wide = 3 * hidden
    groups, totals = chunk_groups(count, windows)
    tokens = sum(chunk["payload"].shape[0] for chunk in chunks)
    by_expert = pl.BlockSpec((1, width, hidden), lambda j: (j, 0, 0))
    return pl.pallas_call(
        functools.partial(weight_kernel, caps, windows, groups),
        grid=(n_local,),
        out_shape=(jax.ShapeDtypeStruct((n_local, width, hidden), BF),) * 3
        + (jax.ShapeDtypeStruct((8, LANES), F32),),
        in_specs=[whole_smem()] * (1 + count)
        + [whole_vmem()] * (5 * count)
        + [payload_specs(chunk, width)[side] for side in range(2) for chunk in chunks]
        + [whole_vmem()] * (2 * count),
        out_specs=(by_expert,) * 3 + (whole_vmem(),),
        scratch_shapes=[pltpu.VMEM((cap, wide), BF) for cap in caps]
        + [pltpu.VMEM((width, tokens), BF)] * 2
        + [pltpu.VMEM((total, wide), BF) for total in totals],
        compiler_params=pltpu.CompilerParams(
            vmem_limit_bytes=(32 if tokens <= 512 else 56) * MIB
        ),
        cost_estimate=cost(2e10),
        name="weights",
    )(
        idx,
        *[chunk["offs"] for chunk in chunks],
        *[piece for group in pieces for piece in group],
        *[chunk["payload"] for chunk in chunks],
        *[chunk["payload"] for chunk in chunks],
        *[chunk["pos"] for chunk in chunks],
        *[chunk["gate"] for chunk in chunks],
    )


def to_partner(value, axis, other):
    return lax.ppermute(value, axis, [(i, i ^ other) for i in range(lax.axis_size(axis))])


def sum_over_dp(parts, earlier):
    own, send_x, send_y, later_x, later_y, gate = parts
    from_x = to_partner(send_x, "dp", 1)
    from_y = to_partner(send_y, "dp", 2)
    send_x, send_y = pair_sums(earlier, later_x, from_y, later_y, from_x)
    late_x = to_partner(send_x, "dp", 1)
    late_y = to_partner(send_y, "dp", 2)
    return [own, from_x, from_y, late_x, late_y, gate]


def gather_over_dp(own):
    half = own.shape[0] // 2
    from_x = to_partner(own, "dp", 1)
    from_y = to_partner(own, "dp", 2)
    first = to_partner(from_x[:half], "dp", 2)
    second = to_partner(from_y[half:], "dp", 1)
    return own, from_x, from_y, first, second


def finish_kernel(width, top, idx, *refs):
    parts, (token_grad, route_grad) = refs[:-2], refs[-2:]
    routes = None
    for distance, part in enumerate(parts):
        at = pl.ds(pl.multiple_of((idx[2] ^ distance) * width, LANES), width)
        token_grad[:, at] = part[:, 0:width]
        value = part[:, width:].astype(F32)
        routes = value if routes is None else routes + value
    route_grad[...] = routes[:, 0:top].astype(BF)


def finish(idx, parts, width, top):
    rows = parts[0].shape[0]
    return pl.pallas_call(
        functools.partial(finish_kernel, width, top),
        out_shape=(
            jax.ShapeDtypeStruct((rows, width * len(parts)), BF),
            jax.ShapeDtypeStruct((rows, top), BF),
        ),
        in_specs=[whole_smem()] + [whole_vmem()] * len(parts),
        out_specs=(whole_vmem(),) * 2,
        compiler_params=pltpu.CompilerParams(vmem_limit_bytes=24 * MIB),
        name="finish",
    )(idx, *parts)


def in_hbm(value):
    return pltpu.with_memory_space_constraint(value, pltpu.HBM)


def touch_kernel(*refs):
    ready = refs[-1]
    ready[...] = jnp.zeros_like(ready)


def touch(weights, earlier):
    near = [pltpu.with_memory_space_constraint(weight, pltpu.VMEM) for weight in weights]
    return pl.pallas_call(
        touch_kernel,
        out_shape=jax.ShapeDtypeStruct((8, LANES), F32),
        in_specs=[pl.BlockSpec(memory_space=pl.ANY)] + [whole_vmem()] * len(weights),
        out_specs=whole_vmem(),
        compiler_params=pltpu.CompilerParams(vmem_limit_bytes=24 * MIB),
        name="touch",
    )(earlier, *near)


def fits_kernel(lane, _, *refs):
    flags, parts, out = refs[:2], refs[2:-1], refs[-1]
    value = flags[0][0:1, 0:1]
    for flag in flags[1:]:
        value = jnp.minimum(value, flag[0:1, 0:1])
    for part in parts:
        value = jnp.minimum(value, part[0:16, lane : lane + 1].astype(F32)[0:1, :])
    out[0] = (value[0, 0] > 0.5).astype(jnp.int32)


def all_fit(earlier, flags, parts, width, top):
    lane = width // LANES
    return pl.pallas_call(
        functools.partial(fits_kernel, 2 * top),
        grid=(1,),
        out_shape=jax.ShapeDtypeStruct((1,), jnp.int32),
        in_specs=[pl.BlockSpec(memory_space=pl.ANY)]
        + [pl.BlockSpec((8, LANES), lambda i: (0, 0))] * len(flags)
        + [pl.BlockSpec((part.shape[0], LANES), lambda i: (0, lane)) for part in parts],
        out_specs=whole_smem(),
        compiler_params=pltpu.CompilerParams(vmem_limit_bytes=24 * MIB),
        name="fits",
    )(earlier, *flags, *parts)[0]


def relay_kernel(_, *refs):
    parts, out = refs[:-1], refs[-1]
    first = 0
    for part in parts:
        out[first : first + part.shape[0], :] = part[...]
        first += part.shape[0]


def relay(parts, earlier):
    rows = sum(part.shape[0] for part in parts)
    return pl.pallas_call(
        relay_kernel,
        out_shape=jax.ShapeDtypeStruct((rows, parts[0].shape[1]), BF),
        in_specs=[pl.BlockSpec(memory_space=pl.ANY)] + [whole_vmem()] * len(parts),
        out_specs=whole_vmem(),
        compiler_params=pltpu.CompilerParams(vmem_limit_bytes=24 * MIB),
        name="relay",
    )(earlier, *parts)


def pair_kernel(_, later_x, from_y, later_y, from_x, out_x, out_y):
    out_x[...] = (later_x[...].astype(F32) + from_y[...].astype(F32)).astype(BF)
    out_y[...] = (later_y[...].astype(F32) + from_x[...].astype(F32)).astype(BF)


def pair_sums(earlier, later_x, from_y, later_y, from_x):
    spec = pl.BlockSpec(later_x.shape, lambda i: (0, 0))
    return pl.pallas_call(
        pair_kernel,
        grid=(1,),
        out_shape=(jax.ShapeDtypeStruct(later_x.shape, BF),) * 2,
        in_specs=[pl.BlockSpec(memory_space=pl.ANY)] + [spec] * 4,
        out_specs=(spec,) * 2,
        compiler_params=pltpu.CompilerParams(vmem_limit_bytes=24 * MIB),
        name="pair",
    )(earlier, later_x, from_y, later_y, from_x)


def add_kernel(count, _, *refs):
    parts, outs = refs[:count], refs[count:]
    total = parts[0][...].astype(F32)
    for part in parts[1:]:
        total = total + part[...].astype(F32)
    rows = outs[0].shape[0]
    for i, out in enumerate(outs):
        out[...] = total[i * rows : (i + 1) * rows, :].astype(BF)


def add_up(parts, earlier, pieces):
    rows, lanes = parts[0].shape
    return pl.pallas_call(
        functools.partial(add_kernel, len(parts)),
        out_shape=(jax.ShapeDtypeStruct((rows // pieces, lanes), BF),) * pieces,
        in_specs=[pl.BlockSpec(memory_space=pl.ANY)] + [whole_vmem()] * len(parts),
        out_specs=(whole_vmem(),) * pieces,
        compiler_params=pltpu.CompilerParams(vmem_limit_bytes=24 * MIB),
        name="add",
    )(earlier, *parts)


def on_device(tokens_in, cotangent, expert_ids, gate_probs, gate_weight, up_weight, down_weight):
    n_expert, n_dp = lax.axis_size("expert"), lax.axis_size("dp")
    expert_at, half_at, dp_at = (lax.axis_index(name) for name in ("expert", "half", "dp"))
    idx = jnp.stack([expert_at, half_at, dp_at]).astype(jnp.int32)
    n_local, width, hidden = gate_weight.shape
    weights = (gate_weight, up_weight, down_weight)
    _, blocks, block_tokens, _ = tokens_in.shape
    top = expert_ids.shape[3]
    block = n_dp * block_tokens
    owner_rows = blocks * block_tokens
    group = blocks * block

    parts = pack(
        idx,
        in_hbm(tokens_in[0].transpose(1, 0, 2)),
        in_hbm(cotangent[0].transpose(1, 0, 2)),
        in_hbm(expert_ids[0].transpose(0, 2, 1)),
        in_hbm(gate_probs[0].transpose(0, 2, 1)),
        n_dp,
        width,
    )
    parts = [parts[0]] + [to_partner(parts[k], "dp", k) for k in range(1, n_dp)]

    unit = round_up(n_local * group // 2, LANES)
    small = round_up(n_local * group // 3, LANES)
    choose = small < unit and n_expert <= 4

    def put_together(earlier, parts, kind, span):
        rows = span * group
        return route(
            earlier, idx, parts, kind, rows, n_local, n_expert, small, top, width, owner_rows
        )

    ready = touch(weights[:2], parts[0])
    own, mixed, fits = put_together(ready, parts, "own", 1)
    got = [to_partner(mixed, "expert", k) for k in (1, 2) if k < n_expert]
    window = round_up(group // 2 + ALIGN, LANES)
    own_sums = partial_acts(idx, own, weights, unit, window)
    operands = (own, own_sums, got, weights)
    rest = functools.partial(
        exchange_and_multiply, put_together, idx, half_at, n_expert, n_dp, top, block, group, unit
    )
    if not choose:
        return rest(unit, operands)
    flags = [fits, to_partner(fits, "expert", n_expert - 1)]
    return lax.cond(
        all_fit(own_sums[-1], flags, got, width, top) == 1,
        functools.partial(rest, small),
        functools.partial(rest, unit),
        operands,
    )


def exchange_and_multiply(
    put_together, idx, half_at, n_expert, n_dp, top, block, group, own_cap, unit, operands
):
    own, own_sums, got, weights = operands
    n_local, width, hidden = weights[0].shape

    chunks, sums, caps, windows, held = [], [], [], [], 0
    while held < n_expert:
        if held == 0:
            chunk, span, cap = own, 1, own_cap
        else:
            if held == 1:
                far = relay(got, own_sums[-1])
                ready = touch(weights, far)
            elif held == 3:
                far = to_partner(got[1], "expert", 1)
            else:
                known = jnp.concatenate([chunk["payload"] for chunk in chunks], axis=0)
                side = jnp.where(half_at == 0, known[:, :width], known[:, width : 2 * width])
                far = jnp.concatenate([side, known[:, 2 * width :]], axis=1)
                far = to_partner(far, "expert", held)
            span = far.shape[0] // group
            chunk = put_together(ready, [far, to_partner(far, "half", 1)], "far", span)
            cap = round_up(span * unit, LANES)
        most = span * group // 2
        chunks.append(chunk)
        caps.append(cap)
        windows.append(round_up(most + ALIGN, ALIGN))
        if held == 0:
            sums.append(own_sums)
        else:
            wide_window = round_up(most + ALIGN, LANES)
            sums.append(partial_acts(idx, chunk, weights, cap, wide_window))
        held += span

    pieces, route_parts = [], []
    for i, parts in enumerate(sums):
        following = sums[min(i + 1, len(sums) - 1)][-1]
        last = sums[min(2, len(sums) - 1)][-1] if i == 0 else parts[-1]
        grads, route_part = unit_grads(sum_over_dp(parts, following), last)
        pieces.append(gather_over_dp(grads))
        route_parts.append(route_part)

    keep, send = token_grads(
        idx, chunks, pieces, route_parts, weights, caps, windows, top, block, group
    )
    both = (keep.astype(F32) + to_partner(send, "half", 1).astype(F32)).astype(BF)
    *weight_out, written = weight_grads(
        idx, chunks, pieces, caps, windows, n_local, width, hidden
    )
    held = jnp.split(both, n_expert, axis=0)
    step = n_expert // 2
    while step > 2:
        got = to_partner(jnp.concatenate(held[step:], axis=0), "expert", step)
        held = [
            (mine.astype(F32) + other.astype(F32)).astype(BF)
            for mine, other in zip(held[:step], jnp.split(got, step, axis=0))
        ]
        step //= 2
    total = held[:1] + [to_partner(held[k], "expert", k) for k in range(1, len(held))]
    total = add_up(total, written, n_dp)
    total = [total[0]] + [to_partner(total[k], "dp", k) for k in range(1, n_dp)]
    token_grad, route_grad = finish(idx, total, width, top)
    return (token_grad[None, None], route_grad[None, None]) + tuple(weight_out)


def solution(mesh):
    return jax.shard_map(
        on_device,
        mesh=mesh,
        in_specs=(
            P(("expert", "dp"), None, None, None),
            P(("expert", "dp"), None, None, None),
            P(("expert", "dp"), None, None, None),
            P(("expert", "dp"), None, None, None),
            P("expert", "dp", "half"),
            P("expert", "dp", "half"),
            P("expert", "dp", "half"),
        ),
        out_specs=(
            P(("expert", "dp"), "half", None, None),
            P(("expert", "dp"), "half", None, None),
            P("expert", "dp", "half"),
            P("expert", "dp", "half"),
            P("expert", "dp", "half"),
        ),
        check_vma=False,
    )
```

```python
import functools

import jax
import jax.numpy as jnp
from jax import lax
from jax.experimental import pallas as pl
from jax.experimental.pallas import tpu as pltpu
from jax.sharding import PartitionSpec as P

LANES = 128
ALIGN = 16
BF = jnp.bfloat16
F32 = jnp.float32
BY_ROW = (((0,), (0,)), ((), ()))
BY_COLUMN = (((1,), (1,)), ((), ()))
MIB = 1 << 20


def round_up(value, step):
    return -(-value // step) * step


def cost(flops):
    return pl.CostEstimate(flops=int(flops), bytes_accessed=0, transcendentals=0)


def vmem_limit(rows):
    return (24 if rows <= 512 else 56) * MIB


def whole_vmem():
    return pl.BlockSpec(memory_space=pltpu.VMEM)


def whole_smem():
    return pl.BlockSpec(memory_space=pltpu.SMEM)


def expert_column(table, expert):
    lane = lax.broadcasted_iota(jnp.int32, table.shape, 1)
    return jnp.sum(jnp.where(lane == expert, table, 0), axis=1, keepdims=True)


def window_start(offs, expert, cap, window):
    start = jnp.minimum((offs[0, expert] // ALIGN) * ALIGN, cap - window)
    return pl.multiple_of(start, ALIGN)


def pack_kernel(width, top, idx, x, dy, ids, gates, *outs):
    tokens, blocks, _ = x.shape
    rows = tokens * blocks
    row = lax.broadcasted_iota(jnp.int32, (rows, tokens), 0)
    token = lax.broadcasted_iota(jnp.int32, (rows, tokens), 1)
    fill = jnp.full((LANES - 2 * top, tokens), -1.0, BF)
    meta = jnp.zeros((rows, LANES), F32)
    for block in range(blocks):
        place = jnp.where(row == token * blocks + block, 1.0, 0.0).astype(BF)
        table = jnp.concatenate([ids[block].astype(F32).astype(BF), gates[block], fill], axis=0)
        meta += lax.dot_general(place, table, BY_COLUMN, preferred_element_type=F32)
    for distance, out in enumerate(outs):
        at = pl.ds(pl.multiple_of((idx[2] ^ distance) * width, LANES), width)
        for t in range(tokens):
            there = slice(t * blocks, (t + 1) * blocks)
            out[there, 0:width] = x[t, :, at]
            out[there, width : 2 * width] = dy[t, :, at]
        out[:, 2 * width :] = meta.astype(BF)


def pack(idx, x, dy, ids, gates, n_dp, width):
    shape = (x.shape[0] * x.shape[1], 2 * width + LANES)
    return pl.pallas_call(
        functools.partial(pack_kernel, width, ids.shape[1]),
        out_shape=(jax.ShapeDtypeStruct(shape, BF),) * n_dp,
        in_specs=[whole_smem()] + [whole_vmem()] * 4,
        out_specs=(whole_vmem(),) * n_dp,
        compiler_params=pltpu.CompilerParams(vmem_limit_bytes=24 * MIB),
        name="pack",
    )(idx, x, dy, ids, gates)


def shared_order(place, step, dp_at):
    owner = ((place.astype(F32) + 0.5) * (1.0 / step)).astype(jnp.int32)
    return place + ((owner ^ dp_at) - owner) * step


def route_kernel(n_local, n_expert, unit, top, width, step, kind, count, _, idx, *refs):
    parts, (pos, gate, offs, payload), rest = refs[:count], refs[count : count + 4], refs[count + 4 :]
    if kind == "own":
        for distance, part in enumerate(parts):
            payload[distance * step : (distance + 1) * step, :] = part[...]
        mixed, fits = rest
        mixed[:, 0:width] = jnp.where(
            idx[1] == 0, payload[:, 0:width], payload[:, width : 2 * width]
        )
        lane = lax.broadcasted_iota(jnp.int32, gate.shape, 1)
        names = payload[:, 2 * width :].astype(F32)
        first_name = (lane * n_local).astype(F32)
        named = jnp.zeros(gate.shape, F32)
        for k in range(top):
            name = names[:, k : k + 1]
            inside = jnp.logical_and(name >= first_name, name < first_name + n_local)
            named += jnp.where(jnp.logical_and(inside, lane < n_expert), 1.0, 0.0)
        most = jnp.max(jnp.sum(named, axis=0, keepdims=True), axis=1, keepdims=True)
        flag = jnp.where(most <= unit, 1.0, 0.0)
        fits[...] = jnp.broadcast_to(flag, fits.shape)
        mixed[:, width:] = jnp.where(lane == 2 * top, flag, names).astype(BF)
    else:
        first = 0
        for near, other in zip(parts[: count // 2], parts[count // 2 :]):
            rows = slice(first, first + near.shape[0])
            payload[rows, 0:width] = jnp.where(idx[1] == 0, near[:, 0:width], other[:, 0:width])
            payload[rows, width : 2 * width] = jnp.where(
                idx[1] == 0, other[:, 0:width], near[:, 0:width]
            )
            payload[rows, 2 * width :] = near[:, width:]
            first += near.shape[0]
    rows = payload.shape[0]
    meta = payload[:, 2 * width :].astype(F32)
    lane = lax.broadcasted_iota(jnp.int32, (rows, LANES), 1)
    here = (lane + idx[0] * n_local).astype(F32)
    chosen = jnp.zeros((rows, LANES), F32)
    gates = jnp.zeros((rows, LANES), F32)
    for k in range(top):
        hit = jnp.logical_and(meta[:, k : k + 1] == here, lane < n_local)
        chosen = jnp.where(hit, 1.0, chosen)
        gates = jnp.where(hit, meta[:, top + k : top + k + 1], gates)
    place_column = shared_order(lax.broadcasted_iota(jnp.int32, (rows, 1), 0), step, idx[2])
    place_row = shared_order(lax.broadcasted_iota(jnp.int32, (1, rows), 1), step, idx[2])
    earlier = jnp.where(place_row < place_column, 1.0, 0.0)
    rank = jnp.dot(earlier.astype(BF), chosen.astype(BF), preferred_element_type=F32)
    counts = jnp.broadcast_to(jnp.sum(chosen, axis=0, keepdims=True), (8, LANES))
    before = (
        lax.broadcasted_iota(jnp.int32, (LANES, LANES), 0)
        < lax.broadcasted_iota(jnp.int32, (LANES, LANES), 1)
    )
    starts = jnp.dot(
        counts, before.astype(F32), preferred_element_type=F32, precision=lax.Precision.HIGHEST
    )
    pos[...] = jnp.where(chosen > 0.0, rank + starts[0:1], -1.0).astype(jnp.int32)
    gate[...] = gates
    offs[...] = starts.astype(jnp.int32)


def route(earlier, idx, parts, kind, rows, n_local, n_expert, unit, top, width, step):
    out_shape = [
        jax.ShapeDtypeStruct((rows, LANES), jnp.int32),
        jax.ShapeDtypeStruct((rows, LANES), F32),
        jax.ShapeDtypeStruct((8, LANES), jnp.int32),
        jax.ShapeDtypeStruct((rows, 2 * width + LANES), BF),
    ]
    if kind == "own":
        out_shape.append(jax.ShapeDtypeStruct((rows, width + LANES), BF))
        out_shape.append(jax.ShapeDtypeStruct((8, LANES), F32))
    out = pl.pallas_call(
        functools.partial(
            route_kernel, n_local, n_expert, unit, top, width, step, kind, len(parts)
        ),
        out_shape=tuple(out_shape),
        in_specs=[pl.BlockSpec(memory_space=pl.ANY), whole_smem()] + [whole_vmem()] * len(parts),
        out_specs=(whole_vmem(),) * len(out_shape),
        compiler_params=pltpu.CompilerParams(vmem_limit_bytes=vmem_limit(rows)),
        name="route",
    )(earlier, idx, *parts)
    chunk = {"pos": out[0], "gate": out[1], "offs": out[2], "payload": out[3]}
    return (chunk, out[4], out[5]) if kind == "own" else chunk


def act_kernel(caps, window, idx, offs, x, dy, pos, gate, w_gate, w_up, w_down, *refs):
    outs, (acc, gate_acc) = refs[:-2], refs[-2:]
    expert = pl.program_id(0)
    hidden = w_gate.shape[2]
    cap = caps[0]

    @pl.when(expert == 0)
    def _():
        acc[...] = jnp.zeros_like(acc)
        gate_acc[...] = jnp.zeros_like(gate_acc)

    start = window_start(offs, expert, cap, window)
    column = expert_column(pos[...], expert)
    slot = lax.broadcasted_iota(jnp.int32, (x.shape[0], window), 1)
    pick = jnp.where(jnp.logical_and(column >= 0, column - start == slot), 1.0, 0.0).astype(BF)
    gate_col = jnp.broadcast_to(expert_column(gate[...], expert), gate.shape).astype(BF)
    slot_x = lax.dot_general(pick, x[...], BY_ROW, preferred_element_type=F32).astype(BF)
    slot_dy = lax.dot_general(pick, dy[...], BY_ROW, preferred_element_type=F32).astype(BF)
    slot_gate = lax.dot_general(pick, gate_col, BY_ROW, preferred_element_type=F32)
    row = start + lax.broadcasted_iota(jnp.int32, (window, 1), 0)
    mine = jnp.logical_and(row >= offs[0, expert], row < offs[0, expert + 1])
    rows = pl.ds(start, window)
    gate_acc[rows, :] = jnp.where(mine, slot_gate, gate_acc[rows, :])
    for part, (left, right) in enumerate(((slot_x, w_gate), (slot_x, w_up), (slot_dy, w_down))):
        columns = slice(part * hidden, (part + 1) * hidden)
        value = jnp.dot(left, right[0], preferred_element_type=F32)
        acc[rows, columns] = jnp.where(mine, value, acc[rows, columns])

    @pl.when(expert == pl.num_programs(0) - 1)
    def _():
        me = idx[2]

        def piece(quarter, other, first, count):
            at = pl.multiple_of((me ^ other) * quarter + first, ALIGN)
            return acc[pl.ds(at, count), :].astype(BF)

        for i, rows_of in enumerate(caps):
            quarter = rows_of // 4
            half = quarter // 2
            own, send_x, send_y, later_x, later_y, own_gate = outs[6 * i : 6 * i + 6]
            own[...] = piece(quarter, 0, 0, quarter)
            send_x[0:half, :] = piece(quarter, 3, 0, half)
            send_x[half:quarter, :] = piece(quarter, 1, 0, half)
            send_y[0:half, :] = piece(quarter, 3, half, half)
            send_y[half:quarter, :] = piece(quarter, 2, half, half)
            later_x[...] = piece(quarter, 1, half, half)
            later_y[...] = piece(quarter, 2, 0, half)
            own_gate[...] = gate_acc[pl.ds(pl.multiple_of(me * quarter, ALIGN), quarter), :]


def payload_specs(chunk, width):
    rows = chunk["payload"].shape[0]
    return [pl.BlockSpec((rows, width), lambda j, part=part: (0, part)) for part in range(2)]


def partial_acts(idx, chunk, weights, caps, window):
    n_local, width, hidden = weights[0].shape
    wide = 3 * hidden
    by_expert = pl.BlockSpec((1, width, hidden), lambda j: (j, 0, 0))
    out_shape = []
    for cap in caps:
        quarter = cap // 4
        for count in (quarter,) * 3 + (quarter // 2,) * 2:
            out_shape.append(jax.ShapeDtypeStruct((count, wide), BF))
        out_shape.append(jax.ShapeDtypeStruct((quarter, LANES), F32))
    out = pl.pallas_call(
        functools.partial(act_kernel, caps, window),
        grid=(n_local,),
        out_shape=tuple(out_shape),
        in_specs=[whole_smem(), whole_smem()]
        + payload_specs(chunk, width)
        + [whole_vmem()] * 2
        + [by_expert] * 3,
        out_specs=(whole_vmem(),) * len(out_shape),
        scratch_shapes=[pltpu.VMEM((caps[0], wide), F32), pltpu.VMEM((caps[0], LANES), F32)],
        compiler_params=pltpu.CompilerParams(
            vmem_limit_bytes=vmem_limit(chunk["payload"].shape[0])
        ),
        cost_estimate=cost(1e10),
        name="acts",
    )(
        idx, chunk["offs"], chunk["payload"], chunk["payload"], chunk["pos"], chunk["gate"],
        *weights,
    )
    return [out[6 * i : 6 * i + 6] for i in range(len(caps))]


def unit_kernel(_, *refs):
    parts, (gate, grads, route_part) = refs[:-3], refs[-3:]
    quarter, wide = grads.shape
    half = quarter // 2
    hidden = wide // 3
    for side in range(2):
        rows = slice(side * half, (side + 1) * half)
        own, from_x, from_y, late_x, late_y = parts
        near, late = ((from_x, late_y), (from_y, late_x))[side]
        sources = [(own, rows), (near, slice(half, quarter)), (late, slice(0, half))]

        def total(part):
            at = slice(part * hidden, (part + 1) * hidden)
            value = None
            for source, there in sources:
                term = source[there, at].astype(F32)
                value = term if value is None else value + term
            return value

        gate_act, up_act, back = total(0), total(1), total(2)
        sigma = 1.0 / (1.0 + jnp.exp(-gate_act))
        active = gate_act * sigma
        slope = sigma * (1.0 + gate_act * (1.0 - sigma))
        scaled = gate[rows, 0:1] * back
        unit = (active * up_act).astype(BF)
        grads[rows, 0:hidden] = (scaled * up_act * slope).astype(BF)
        grads[rows, hidden : 2 * hidden] = (scaled * active).astype(BF)
        grads[rows, 2 * hidden :] = unit
        sums = jnp.sum(back * unit.astype(F32), axis=1, keepdims=True)
        route_part[rows, :] = jnp.broadcast_to(sums, (half, LANES)).astype(BF)


def unit_grads(parts, earlier):
    quarter, wide = parts[0].shape
    return pl.pallas_call(
        unit_kernel,
        out_shape=(
            jax.ShapeDtypeStruct((quarter, wide), BF),
            jax.ShapeDtypeStruct((quarter, LANES), BF),
        ),
        in_specs=[pl.BlockSpec(memory_space=pl.ANY)] + [whole_vmem()] * len(parts),
        out_specs=(whole_vmem(),) * 2,
        compiler_params=pltpu.CompilerParams(vmem_limit_bytes=24 * MIB),
        name="units",
    )(earlier, *parts)


def place_quarters(me, pieces, target):
    own, from_x, from_y, first, second = pieces
    quarter = own.shape[0]
    half = quarter // 2

    def at(other, extra, count):
        return pl.ds(pl.multiple_of((me ^ other) * quarter + extra, ALIGN), count)

    target[at(0, 0, quarter), :] = own[...]
    target[at(1, 0, quarter), :] = from_x[...]
    target[at(2, 0, quarter), :] = from_y[...]
    target[at(3, 0, half), :] = first[...]
    target[at(3, half, half), :] = second[...]


def window_hits(members, caps, windows, total, offs, poss, expert):
    places, starts, lane_start = [], [], 0
    for c in members:
        start = window_start(offs[c], expert, caps[c], windows[c])
        column = expert_column(poss[c][...], expert)
        places.append(jnp.where(column >= 0, column - start + lane_start, -1))
        starts.append((c, start, lane_start))
        lane_start += windows[c]
    places = jnp.concatenate(places, axis=0)
    lanes = lax.broadcasted_iota(jnp.int32, (places.shape[0], total), 1)
    return places == lanes, starts


def token_kernel(caps, windows, groups, top, block, group, idx, *refs):
    count = len(caps)
    offs, refs = refs[:count], refs[count:]
    pieces, refs = refs[: 5 * count], refs[5 * count :]
    routes_own, poss, metas = (refs[i * count : (i + 1) * count] for i in range(3))
    refs = refs[3 * count :]
    w_gate, w_up, keep, send = refs[:4]
    grads, routes, refs = refs[4 : 4 + count], refs[4 + count : 4 + 2 * count], refs[4 + 2 * count :]
    acc, route_acc = refs[:2]
    stacks, route_stacks = refs[2 : 2 + len(groups)], refs[2 + len(groups) :]
    expert = pl.program_id(0)
    _, width, hidden = w_gate.shape
    n_local = pl.num_programs(0)

    @pl.when(expert == 0)
    def _():
        for c in range(count):
            place_quarters(idx[2], pieces[5 * c : 5 * c + 5], grads[c])
            routes[c][...] = jnp.zeros_like(routes[c])
            quarter = caps[c] // 4
            at = pl.ds(pl.multiple_of(idx[2] * quarter, ALIGN), quarter)
            routes[c][at, :] = routes_own[c][...]
        acc[...] = jnp.zeros_like(acc)
        route_acc[...] = jnp.zeros_like(route_acc)
        for stacked in stacks + route_stacks:
            stacked[...] = jnp.zeros_like(stacked)

    named = (expert + idx[0] * n_local).astype(F32)
    token_start = 0
    for members, stacked, route_stacked in zip(groups, stacks, route_stacks):
        hit, starts = window_hits(
            members, caps, windows, stacked.shape[0], offs, poss, expert
        )
        for c, start, lane_start in starts:
            there = slice(lane_start, lane_start + windows[c])
            stacked[there, :] = grads[c][pl.ds(start, windows[c]), :]
            route_stacked[there, :] = routes[c][pl.ds(start, windows[c]), :]
        pick = jnp.where(hit, 1.0, 0.0).astype(BF)
        row_grad = lax.dot_general(
            stacked[:, 0:hidden], w_gate[0], BY_COLUMN, preferred_element_type=F32
        ) + lax.dot_general(
            stacked[:, hidden : 2 * hidden],
            w_up[0],
            BY_COLUMN,
            preferred_element_type=F32,
        )
        rows = slice(token_start, token_start + hit.shape[0])
        acc[rows, :] += jnp.dot(pick, row_grad.astype(BF), preferred_element_type=F32)
        meta = jnp.concatenate([metas[c][...] for c in members], axis=0).astype(F32)
        lane = lax.broadcasted_iota(jnp.int32, meta.shape, 1)
        token_route = jnp.dot(pick, route_stacked[...], preferred_element_type=F32)
        route_acc[rows, :] = jnp.where(
            jnp.logical_and(lane < top, meta == named), token_route, route_acc[rows, :]
        )
        token_start += hit.shape[0]

    @pl.when(expert == n_local - 1)
    def _():
        blocks = group // block
        row = lax.broadcasted_iota(jnp.int32, (block, group), 0)
        column = lax.broadcasted_iota(jnp.int32, (block, group), 1)
        for target, which in ((keep, idx[1]), (send, 1 - idx[1])):
            chosen = jnp.where(column == row * blocks + which, 1.0, 0.0).astype(BF)
            for first in range(acc.shape[0] // group):
                rows = slice(first * group, (first + 1) * group)
                there = slice(first * block, (first + 1) * block)
                for lanes, values in ((slice(0, width), acc), (slice(width, None), route_acc)):
                    target[there, lanes] = jnp.dot(
                        chosen, values[rows, :].astype(BF), preferred_element_type=F32
                    ).astype(BF)


def chunk_groups(count, windows):
    groups = [tuple(range(min(count, 3)))] + [(c,) for c in range(3, count)]
    return groups, [round_up(sum(windows[c] for c in members), LANES) for members in groups]


def token_grads(idx, chunks, pieces, route_parts, weights, caps, windows, top, block, group):
    n_local, width, hidden = weights[0].shape
    by_expert = pl.BlockSpec((1, width, hidden), lambda j: (j, 0, 0))
    count = len(chunks)
    groups, totals = chunk_groups(count, windows)
    tokens = sum(chunk["payload"].shape[0] for chunk in chunks)
    result = jax.ShapeDtypeStruct((tokens // 2, width + LANES), BF)
    flat = [piece for group in pieces for piece in group]
    return pl.pallas_call(
        functools.partial(token_kernel, caps, windows, groups, top, block, group),
        grid=(n_local,),
        out_shape=(result, result),
        in_specs=[whole_smem()] * (1 + count)
        + [pl.BlockSpec((piece.shape[0], 2 * hidden), lambda j: (0, 0)) for piece in flat]
        + [whole_vmem()] * (2 * count)
        + [
            pl.BlockSpec((chunk["payload"].shape[0], LANES), lambda j: (0, 2 * width // LANES))
            for chunk in chunks
        ]
        + [by_expert] * 2,
        out_specs=(whole_vmem(),) * 2,
        scratch_shapes=[pltpu.VMEM((cap, 2 * hidden), BF) for cap in caps]
        + [pltpu.VMEM((cap, LANES), BF) for cap in caps]
        + [pltpu.VMEM((tokens, width), F32), pltpu.VMEM((tokens, LANES), F32)]
        + [pltpu.VMEM((total, 2 * hidden), BF) for total in totals]
        + [pltpu.VMEM((total, LANES), BF) for total in totals],
        compiler_params=pltpu.CompilerParams(vmem_limit_bytes=vmem_limit(tokens)),
        cost_estimate=cost(1e10),
        name="tokens",
    )(
        idx,
        *[chunk["offs"] for chunk in chunks],
        *flat,
        *route_parts,
        *[chunk["pos"] for chunk in chunks],
        *[chunk["payload"] for chunk in chunks],
        *weights[:2],
    )


def weight_kernel(caps, windows, groups, idx, *refs):
    count = len(caps)
    offs, refs = refs[:count], refs[count:]
    pieces, refs = refs[: 5 * count], refs[5 * count :]
    xs, dys, poss, gates = (refs[i * count : (i + 1) * count] for i in range(4))
    refs = refs[4 * count :]
    outs, done, grads, refs = refs[:3], refs[3], refs[4 : 4 + count], refs[4 + count :]
    x_turned, dy_turned, stacks = refs[0], refs[1], refs[2:]
    expert = pl.program_id(0)
    hidden = outs[0].shape[2]

    @pl.when(expert == 0)
    def _():
        for c in range(count):
            place_quarters(idx[2], pieces[5 * c : 5 * c + 5], grads[c])
        x_turned[...] = jnp.concatenate([ref[...] for ref in xs], axis=0).T
        dy_turned[...] = jnp.concatenate([ref[...] for ref in dys], axis=0).T
        for stacked in stacks:
            stacked[...] = jnp.zeros_like(stacked)
        done[...] = jnp.zeros_like(done)

    sums, token_start = [None] * 3, 0
    for members, stacked in zip(groups, stacks):
        hit, starts = window_hits(
            members, caps, windows, stacked.shape[0], offs, poss, expert
        )
        for c, start, lane_start in starts:
            there = slice(lane_start, lane_start + windows[c])
            stacked[there, :] = grads[c][pl.ds(start, windows[c]), :]
        scale = jnp.concatenate([expert_column(gates[c][...], expert) for c in members], axis=0)
        pick = jnp.where(hit, 1.0, 0.0).astype(BF)
        pick_scaled = jnp.where(hit, scale, 0.0).astype(BF)
        lanes = slice(token_start, token_start + hit.shape[0])
        slot_x = jnp.dot(x_turned[:, lanes], pick, preferred_element_type=F32).astype(BF)
        slot_dy = jnp.dot(dy_turned[:, lanes], pick_scaled, preferred_element_type=F32).astype(BF)
        for part, left in enumerate((slot_x, slot_x, slot_dy)):
            columns = slice(part * hidden, (part + 1) * hidden)
            value = jnp.dot(left, stacked[:, columns], preferred_element_type=F32)
            sums[part] = value if sums[part] is None else sums[part] + value
        token_start += hit.shape[0]
    for out, value in zip(outs, sums):
        out[0] = value.astype(BF)


def weight_grads(idx, chunks, pieces, caps, windows, n_local, width, hidden):
    count = len(chunks)
    wide = 3 * hidden
    groups, totals = chunk_groups(count, windows)
    tokens = sum(chunk["payload"].shape[0] for chunk in chunks)
    by_expert = pl.BlockSpec((1, width, hidden), lambda j: (j, 0, 0))
    return pl.pallas_call(
        functools.partial(weight_kernel, caps, windows, groups),
        grid=(n_local,),
        out_shape=(jax.ShapeDtypeStruct((n_local, width, hidden), BF),) * 3
        + (jax.ShapeDtypeStruct((8, LANES), F32),),
        in_specs=[whole_smem()] * (1 + count)
        + [whole_vmem()] * (5 * count)
        + [payload_specs(chunk, width)[side] for side in range(2) for chunk in chunks]
        + [whole_vmem()] * (2 * count),
        out_specs=(by_expert,) * 3 + (whole_vmem(),),
        scratch_shapes=[pltpu.VMEM((cap, wide), BF) for cap in caps]
        + [pltpu.VMEM((width, tokens), BF)] * 2
        + [pltpu.VMEM((total, wide), BF) for total in totals],
        compiler_params=pltpu.CompilerParams(
            vmem_limit_bytes=(32 if tokens <= 512 else 56) * MIB
        ),
        cost_estimate=cost(2e10),
        name="weights",
    )(
        idx,
        *[chunk["offs"] for chunk in chunks],
        *[piece for group in pieces for piece in group],
        *[chunk["payload"] for chunk in chunks],
        *[chunk["payload"] for chunk in chunks],
        *[chunk["pos"] for chunk in chunks],
        *[chunk["gate"] for chunk in chunks],
    )


def to_partner(value, axis, other):
    return lax.ppermute(value, axis, [(i, i ^ other) for i in range(lax.axis_size(axis))])


def sum_over_dp(parts, earlier):
    own, send_x, send_y, later_x, later_y, gate = parts
    from_x = to_partner(send_x, "dp", 1)
    from_y = to_partner(send_y, "dp", 2)
    send_x, send_y = pair_sums(earlier, later_x, from_y, later_y, from_x)
    late_x = to_partner(send_x, "dp", 1)
    late_y = to_partner(send_y, "dp", 2)
    return [own, from_x, from_y, late_x, late_y, gate, send_x]


def gather_over_dp(own):
    half = own.shape[0] // 2
    from_x = to_partner(own, "dp", 1)
    from_y = to_partner(own, "dp", 2)
    first = to_partner(from_x[:half], "dp", 2)
    second = to_partner(from_y[half:], "dp", 1)
    return own, from_x, from_y, first, second


def finish_kernel(width, top, idx, *refs):
    parts, (token_grad, route_grad) = refs[:-2], refs[-2:]
    routes = None
    for distance, part in enumerate(parts):
        at = pl.ds(pl.multiple_of((idx[2] ^ distance) * width, LANES), width)
        token_grad[:, at] = part[:, 0:width]
        value = part[:, width:].astype(F32)
        routes = value if routes is None else routes + value
    route_grad[...] = routes[:, 0:top].astype(BF)


def finish(idx, parts, width, top):
    rows = parts[0].shape[0]
    return pl.pallas_call(
        functools.partial(finish_kernel, width, top),
        out_shape=(
            jax.ShapeDtypeStruct((rows, width * len(parts)), BF),
            jax.ShapeDtypeStruct((rows, top), BF),
        ),
        in_specs=[whole_smem()] + [whole_vmem()] * len(parts),
        out_specs=(whole_vmem(),) * 2,
        compiler_params=pltpu.CompilerParams(vmem_limit_bytes=24 * MIB),
        name="finish",
    )(idx, *parts)


def in_hbm(value):
    return pltpu.with_memory_space_constraint(value, pltpu.HBM)


def touch_kernel(*refs):
    ready = refs[-1]
    ready[...] = jnp.zeros_like(ready)


def touch(weights, earlier):
    near = [pltpu.with_memory_space_constraint(weight, pltpu.VMEM) for weight in weights]
    return pl.pallas_call(
        touch_kernel,
        out_shape=jax.ShapeDtypeStruct((8, LANES), F32),
        in_specs=[pl.BlockSpec(memory_space=pl.ANY)] + [whole_vmem()] * len(weights),
        out_specs=whole_vmem(),
        compiler_params=pltpu.CompilerParams(vmem_limit_bytes=24 * MIB),
        name="touch",
    )(earlier, *near)


def fits_kernel(lane, _, *refs):
    flags, parts, out = refs[:2], refs[2:-1], refs[-1]
    value = flags[0][0:1, 0:1]
    for flag in flags[1:]:
        value = jnp.minimum(value, flag[0:1, 0:1])
    for part in parts:
        value = jnp.minimum(value, part[0:16, lane : lane + 1].astype(F32)[0:1, :])
    out[0] = (value[0, 0] > 0.5).astype(jnp.int32)


def all_fit(earlier, flags, parts, width, top):
    lane = width // LANES
    return pl.pallas_call(
        functools.partial(fits_kernel, 2 * top),
        grid=(1,),
        out_shape=jax.ShapeDtypeStruct((1,), jnp.int32),
        in_specs=[pl.BlockSpec(memory_space=pl.ANY)]
        + [pl.BlockSpec((8, LANES), lambda i: (0, 0))] * len(flags)
        + [pl.BlockSpec((part.shape[0], LANES), lambda i: (0, lane)) for part in parts],
        out_specs=whole_smem(),
        compiler_params=pltpu.CompilerParams(vmem_limit_bytes=24 * MIB),
        name="fits",
    )(earlier, *flags, *parts)[0]


def relay_kernel(_, *refs):
    parts, out = refs[:-1], refs[-1]
    first = 0
    for part in parts:
        out[first : first + part.shape[0], :] = part[...]
        first += part.shape[0]


def relay(parts, earlier):
    rows = sum(part.shape[0] for part in parts)
    return pl.pallas_call(
        relay_kernel,
        out_shape=jax.ShapeDtypeStruct((rows, parts[0].shape[1]), BF),
        in_specs=[pl.BlockSpec(memory_space=pl.ANY)] + [whole_vmem()] * len(parts),
        out_specs=whole_vmem(),
        compiler_params=pltpu.CompilerParams(vmem_limit_bytes=24 * MIB),
        name="relay",
    )(earlier, *parts)


def pair_kernel(_, later_x, from_y, later_y, from_x, out_x, out_y):
    out_x[...] = (later_x[...].astype(F32) + from_y[...].astype(F32)).astype(BF)
    out_y[...] = (later_y[...].astype(F32) + from_x[...].astype(F32)).astype(BF)


def pair_sums(earlier, later_x, from_y, later_y, from_x):
    spec = pl.BlockSpec(later_x.shape, lambda i: (0, 0))
    return pl.pallas_call(
        pair_kernel,
        grid=(1,),
        out_shape=(jax.ShapeDtypeStruct(later_x.shape, BF),) * 2,
        in_specs=[pl.BlockSpec(memory_space=pl.ANY)] + [spec] * 4,
        out_specs=(spec,) * 2,
        compiler_params=pltpu.CompilerParams(vmem_limit_bytes=24 * MIB),
        name="pair",
    )(earlier, later_x, from_y, later_y, from_x)


def add_kernel(count, _, *refs):
    parts, outs = refs[:count], refs[count:]
    total = parts[0][...].astype(F32)
    for part in parts[1:]:
        total = total + part[...].astype(F32)
    rows = outs[0].shape[0]
    for i, out in enumerate(outs):
        out[...] = total[i * rows : (i + 1) * rows, :].astype(BF)


def add_up(parts, earlier, pieces):
    rows, lanes = parts[0].shape
    return pl.pallas_call(
        functools.partial(add_kernel, len(parts)),
        out_shape=(jax.ShapeDtypeStruct((rows // pieces, lanes), BF),) * pieces,
        in_specs=[pl.BlockSpec(memory_space=pl.ANY)] + [whole_vmem()] * len(parts),
        out_specs=(whole_vmem(),) * pieces,
        compiler_params=pltpu.CompilerParams(vmem_limit_bytes=24 * MIB),
        name="add",
    )(earlier, *parts)


def on_device(tokens_in, cotangent, expert_ids, gate_probs, gate_weight, up_weight, down_weight):
    n_expert, n_dp = lax.axis_size("expert"), lax.axis_size("dp")
    expert_at, half_at, dp_at = (lax.axis_index(name) for name in ("expert", "half", "dp"))
    idx = jnp.stack([expert_at, half_at, dp_at]).astype(jnp.int32)
    n_local, width, hidden = gate_weight.shape
    weights = (gate_weight, up_weight, down_weight)
    _, blocks, block_tokens, _ = tokens_in.shape
    top = expert_ids.shape[3]
    block = n_dp * block_tokens
    owner_rows = blocks * block_tokens
    group = blocks * block

    parts = pack(
        idx,
        in_hbm(tokens_in[0].transpose(1, 0, 2)),
        in_hbm(cotangent[0].transpose(1, 0, 2)),
        in_hbm(expert_ids[0].transpose(0, 2, 1)),
        in_hbm(gate_probs[0].transpose(0, 2, 1)),
        n_dp,
        width,
    )
    parts = [parts[0]] + [to_partner(parts[k], "dp", k) for k in range(1, n_dp)]

    unit = round_up(n_local * group // 2, LANES)
    small = round_up(n_local * group // 3, LANES)
    choose = small < unit and n_expert <= 4

    def put_together(earlier, parts, kind, span):
        rows = span * group
        return route(
            earlier, idx, parts, kind, rows, n_local, n_expert, small, top, width, owner_rows
        )

    ready = touch(weights[:2], parts[0])
    own, mixed, fits = put_together(ready, parts, "own", 1)
    got = [to_partner(mixed, "expert", k) for k in (1, 2) if k < n_expert]
    window = round_up(group // 2 + ALIGN, LANES)
    units = (unit, small) if choose else (unit,)
    own_sums = partial_acts(idx, own, weights, units, window)
    operands = (own, own_sums, got, weights)
    rest = functools.partial(
        exchange_and_multiply, put_together, idx, half_at, n_expert, n_dp, top, block, group
    )
    if not choose:
        return rest(0, unit, operands)
    flags = [fits, to_partner(fits, "expert", n_expert - 1)]
    return lax.cond(
        all_fit(own_sums[0][-1], flags, got, width, top) == 1,
        functools.partial(rest, 1, small),
        functools.partial(rest, 0, unit),
        operands,
    )


def exchange_and_multiply(
    put_together, idx, half_at, n_expert, n_dp, top, block, group, choice, unit, operands
):
    own, own_sums, got, weights = operands
    own_sums = own_sums[choice]
    n_local, width, hidden = weights[0].shape

    chunks, sums, caps, windows, held = [], [], [], [], 0
    while held < n_expert:
        if held == 0:
            chunk, span, cap = own, 1, unit
        else:
            if held == 1:
                far = relay(got, own_sums[-1])
                ready = touch(weights, far)
            elif held == 3:
                far = to_partner(got[1], "expert", 1)
                own_total = sum_over_dp(own_sums, sums[1][-1])
                ready = own_total[-1]
            else:
                known = jnp.concatenate([chunk["payload"] for chunk in chunks], axis=0)
                side = jnp.where(half_at == 0, known[:, :width], known[:, width : 2 * width])
                far = jnp.concatenate([side, known[:, 2 * width :]], axis=1)
                far = to_partner(far, "expert", held)
            span = far.shape[0] // group
            chunk = put_together(ready, [far, to_partner(far, "half", 1)], "far", span)
            cap = round_up(span * unit, LANES)
        most = span * group // 2
        chunks.append(chunk)
        caps.append(cap)
        windows.append(round_up(most + ALIGN, ALIGN))
        if held == 0:
            sums.append(own_sums)
        else:
            wide_window = round_up(most + ALIGN, LANES)
            sums.append(partial_acts(idx, chunk, weights, (cap,), wide_window)[0])
        held += span

    pieces, route_parts = [], []
    for i, parts in enumerate(sums):
        following = route_parts[0] if i == 1 else sums[min(i + 1, len(sums) - 1)][-1]
        last = sums[min(2, len(sums) - 1)][-1] if i == 0 else parts[-1]
        total = own_total if i == 0 and len(sums) > 2 else sum_over_dp(parts, following)
        grads, route_part = unit_grads(total[:-1], last)
        pieces.append(gather_over_dp(grads))
        route_parts.append(route_part)

    keep, send = token_grads(
        idx, chunks, pieces, route_parts, weights, caps, windows, top, block, group
    )
    both = (keep.astype(F32) + to_partner(send, "half", 1).astype(F32)).astype(BF)
    *weight_out, written = weight_grads(
        idx, chunks, pieces, caps, windows, n_local, width, hidden
    )
    held = jnp.split(both, n_expert, axis=0)
    step = n_expert // 2
    while step > 2:
        got = to_partner(jnp.concatenate(held[step:], axis=0), "expert", step)
        held = [
            (mine.astype(F32) + other.astype(F32)).astype(BF)
            for mine, other in zip(held[:step], jnp.split(got, step, axis=0))
        ]
        step //= 2
    total = held[:1] + [to_partner(held[k], "expert", k) for k in range(1, len(held))]
    total = add_up(total, written, n_dp)
    total = [total[0]] + [to_partner(total[k], "dp", k) for k in range(1, n_dp)]
    token_grad, route_grad = finish(idx, total, width, top)
    return (token_grad[None, None], route_grad[None, None]) + tuple(weight_out)


def solution(mesh):
    return jax.shard_map(
        on_device,
        mesh=mesh,
        in_specs=(
            P(("expert", "dp"), None, None, None),
            P(("expert", "dp"), None, None, None),
            P(("expert", "dp"), None, None, None),
            P(("expert", "dp"), None, None, None),
            P("expert", "dp", "half"),
            P("expert", "dp", "half"),
            P("expert", "dp", "half"),
        ),
        out_specs=(
            P(("expert", "dp"), "half", None, None),
            P(("expert", "dp"), "half", None, None),
            P("expert", "dp", "half"),
            P("expert", "dp", "half"),
            P("expert", "dp", "half"),
        ),
        check_vma=False,
    )
```

```python
import functools

import jax
import jax.numpy as jnp
from jax import lax
from jax.experimental import pallas as pl
from jax.experimental.pallas import tpu as pltpu
from jax.sharding import PartitionSpec as P

LANES = 128
ALIGN = 16
BF = jnp.bfloat16
F32 = jnp.float32
BY_ROW = (((0,), (0,)), ((), ()))
BY_COLUMN = (((1,), (1,)), ((), ()))
MIB = 1 << 20


def round_up(value, step):
    return -(-value // step) * step


def cost(flops):
    return pl.CostEstimate(flops=int(flops), bytes_accessed=0, transcendentals=0)


def vmem_limit(rows):
    return (24 if rows <= 512 else 56) * MIB


def whole_vmem():
    return pl.BlockSpec(memory_space=pltpu.VMEM)


def whole_smem():
    return pl.BlockSpec(memory_space=pltpu.SMEM)


def expert_column(table, expert):
    lane = lax.broadcasted_iota(jnp.int32, table.shape, 1)
    return jnp.sum(jnp.where(lane == expert, table, 0), axis=1, keepdims=True)


def window_start(offs, expert, cap, window):
    start = jnp.minimum((offs[0, expert] // ALIGN) * ALIGN, cap - window)
    return pl.multiple_of(start, ALIGN)


def pack_kernel(width, top, idx, x, dy, ids, gates, *outs):
    tokens, blocks, _ = x.shape
    rows = tokens * blocks
    row = lax.broadcasted_iota(jnp.int32, (rows, tokens), 0)
    token = lax.broadcasted_iota(jnp.int32, (rows, tokens), 1)
    fill = jnp.full((LANES - 2 * top, tokens), -1.0, BF)
    meta = jnp.zeros((rows, LANES), F32)
    for block in range(blocks):
        place = jnp.where(row == token * blocks + block, 1.0, 0.0).astype(BF)
        table = jnp.concatenate([ids[block].astype(F32).astype(BF), gates[block], fill], axis=0)
        meta += lax.dot_general(place, table, BY_COLUMN, preferred_element_type=F32)
    for distance, out in enumerate(outs):
        at = pl.ds(pl.multiple_of((idx[2] ^ distance) * width, LANES), width)
        for t in range(tokens):
            there = slice(t * blocks, (t + 1) * blocks)
            out[there, 0:width] = x[t, :, at]
            out[there, width : 2 * width] = dy[t, :, at]
        out[:, 2 * width :] = meta.astype(BF)


def pack(idx, x, dy, ids, gates, n_dp, width):
    shape = (x.shape[0] * x.shape[1], 2 * width + LANES)
    return pl.pallas_call(
        functools.partial(pack_kernel, width, ids.shape[1]),
        out_shape=(jax.ShapeDtypeStruct(shape, BF),) * n_dp,
        in_specs=[whole_smem()] + [whole_vmem()] * 4,
        out_specs=(whole_vmem(),) * n_dp,
        compiler_params=pltpu.CompilerParams(vmem_limit_bytes=24 * MIB),
        name="pack",
    )(idx, x, dy, ids, gates)


def shared_order(place, step, dp_at):
    owner = ((place.astype(F32) + 0.5) * (1.0 / step)).astype(jnp.int32)
    return place + ((owner ^ dp_at) - owner) * step


def route_kernel(n_local, n_expert, unit, top, width, step, kind, count, _, idx, *refs):
    parts, (pos, gate, offs, payload), rest = refs[:count], refs[count : count + 4], refs[count + 4 :]
    if kind == "own":
        for distance, part in enumerate(parts):
            payload[distance * step : (distance + 1) * step, :] = part[...]
        mixed, fits = rest
        mixed[:, 0:width] = jnp.where(
            idx[1] == 0, payload[:, 0:width], payload[:, width : 2 * width]
        )
        lane = lax.broadcasted_iota(jnp.int32, gate.shape, 1)
        names = payload[:, 2 * width :].astype(F32)
        first_name = (lane * n_local).astype(F32)
        named = jnp.zeros(gate.shape, F32)
        for k in range(top):
            name = names[:, k : k + 1]
            inside = jnp.logical_and(name >= first_name, name < first_name + n_local)
            named += jnp.where(jnp.logical_and(inside, lane < n_expert), 1.0, 0.0)
        most = jnp.max(jnp.sum(named, axis=0, keepdims=True), axis=1, keepdims=True)
        flag = jnp.where(most <= unit, 1.0, 0.0)
        fits[...] = jnp.broadcast_to(flag, fits.shape)
        mixed[:, width:] = jnp.where(lane == 2 * top, flag, names).astype(BF)
    else:
        first = 0
        for near, other in zip(parts[: count // 2], parts[count // 2 :]):
            rows = slice(first, first + near.shape[0])
            payload[rows, 0:width] = jnp.where(idx[1] == 0, near[:, 0:width], other[:, 0:width])
            payload[rows, width : 2 * width] = jnp.where(
                idx[1] == 0, other[:, 0:width], near[:, 0:width]
            )
            payload[rows, 2 * width :] = near[:, width:]
            first += near.shape[0]
    rows = payload.shape[0]
    meta = payload[:, 2 * width :].astype(F32)
    lane = lax.broadcasted_iota(jnp.int32, (rows, LANES), 1)
    here = (lane + idx[0] * n_local).astype(F32)
    chosen = jnp.zeros((rows, LANES), F32)
    gates = jnp.zeros((rows, LANES), F32)
    for k in range(top):
        hit = jnp.logical_and(meta[:, k : k + 1] == here, lane < n_local)
        chosen = jnp.where(hit, 1.0, chosen)
        gates = jnp.where(hit, meta[:, top + k : top + k + 1], gates)
    place_column = shared_order(lax.broadcasted_iota(jnp.int32, (rows, 1), 0), step, idx[2])
    place_row = shared_order(lax.broadcasted_iota(jnp.int32, (1, rows), 1), step, idx[2])
    earlier = jnp.where(place_row < place_column, 1.0, 0.0)
    rank = jnp.dot(earlier.astype(BF), chosen.astype(BF), preferred_element_type=F32)
    counts = jnp.broadcast_to(jnp.sum(chosen, axis=0, keepdims=True), (8, LANES))
    before = (
        lax.broadcasted_iota(jnp.int32, (LANES, LANES), 0)
        < lax.broadcasted_iota(jnp.int32, (LANES, LANES), 1)
    )
    starts = jnp.dot(
        counts, before.astype(F32), preferred_element_type=F32, precision=lax.Precision.HIGHEST
    )
    pos[...] = jnp.where(chosen > 0.0, rank + starts[0:1], -1.0).astype(jnp.int32)
    gate[...] = gates
    offs[...] = starts.astype(jnp.int32)


def route(earlier, idx, parts, kind, rows, n_local, n_expert, unit, top, width, step):
    out_shape = [
        jax.ShapeDtypeStruct((rows, LANES), jnp.int32),
        jax.ShapeDtypeStruct((rows, LANES), F32),
        jax.ShapeDtypeStruct((8, LANES), jnp.int32),
        jax.ShapeDtypeStruct((rows, 2 * width + LANES), BF),
    ]
    if kind == "own":
        out_shape.append(jax.ShapeDtypeStruct((rows, width + LANES), BF))
        out_shape.append(jax.ShapeDtypeStruct((8, LANES), F32))
    out = pl.pallas_call(
        functools.partial(
            route_kernel, n_local, n_expert, unit, top, width, step, kind, len(parts)
        ),
        out_shape=tuple(out_shape),
        in_specs=[pl.BlockSpec(memory_space=pl.ANY), whole_smem()] + [whole_vmem()] * len(parts),
        out_specs=(whole_vmem(),) * len(out_shape),
        compiler_params=pltpu.CompilerParams(vmem_limit_bytes=vmem_limit(rows)),
        name="route",
    )(earlier, idx, *parts)
    chunk = {"pos": out[0], "gate": out[1], "offs": out[2], "payload": out[3]}
    return (chunk, out[4], out[5]) if kind == "own" else chunk


def act_kernel(caps, window, idx, offs, x, dy, pos, gate, w_gate, w_up, w_down, *refs):
    outs, (acc, gate_acc) = refs[:-2], refs[-2:]
    expert = pl.program_id(0)
    hidden = w_gate.shape[2]
    cap = caps[0]

    @pl.when(expert == 0)
    def _():
        acc[...] = jnp.zeros_like(acc)
        gate_acc[...] = jnp.zeros_like(gate_acc)

    start = window_start(offs, expert, cap, window)
    column = expert_column(pos[...], expert)
    slot = lax.broadcasted_iota(jnp.int32, (x.shape[0], window), 1)
    pick = jnp.where(jnp.logical_and(column >= 0, column - start == slot), 1.0, 0.0).astype(BF)
    gate_col = jnp.broadcast_to(expert_column(gate[...], expert), gate.shape).astype(BF)
    slot_x = lax.dot_general(pick, x[...], BY_ROW, preferred_element_type=F32).astype(BF)
    slot_dy = lax.dot_general(pick, dy[...], BY_ROW, preferred_element_type=F32).astype(BF)
    slot_gate = lax.dot_general(pick, gate_col, BY_ROW, preferred_element_type=F32)
    row = start + lax.broadcasted_iota(jnp.int32, (window, 1), 0)
    mine = jnp.logical_and(row >= offs[0, expert], row < offs[0, expert + 1])
    rows = pl.ds(start, window)
    gate_acc[rows, :] = jnp.where(mine, slot_gate, gate_acc[rows, :])
    for part, (left, right) in enumerate(((slot_x, w_gate), (slot_x, w_up), (slot_dy, w_down))):
        columns = slice(part * hidden, (part + 1) * hidden)
        value = jnp.dot(left, right[0], preferred_element_type=F32)
        acc[rows, columns] = jnp.where(mine, value, acc[rows, columns])

    @pl.when(expert == pl.num_programs(0) - 1)
    def _():
        me = idx[2]

        def piece(quarter, other, first, count):
            at = pl.multiple_of((me ^ other) * quarter + first, ALIGN)
            return acc[pl.ds(at, count), :].astype(BF)

        for i, rows_of in enumerate(caps):
            quarter = rows_of // 4
            half = quarter // 2
            own, send_x, send_y, later_x, later_y, own_gate = outs[6 * i : 6 * i + 6]
            own[...] = piece(quarter, 0, 0, quarter)
            send_x[0:half, :] = piece(quarter, 3, 0, half)
            send_x[half:quarter, :] = piece(quarter, 1, 0, half)
            send_y[0:half, :] = piece(quarter, 3, half, half)
            send_y[half:quarter, :] = piece(quarter, 2, half, half)
            later_x[...] = piece(quarter, 1, half, half)
            later_y[...] = piece(quarter, 2, 0, half)
            own_gate[...] = gate_acc[pl.ds(pl.multiple_of(me * quarter, ALIGN), quarter), :]


def payload_specs(chunk, width):
    rows = chunk["payload"].shape[0]
    return [pl.BlockSpec((rows, width), lambda j, part=part: (0, part)) for part in range(2)]


def partial_acts(idx, chunk, weights, caps, window):
    n_local, width, hidden = weights[0].shape
    wide = 3 * hidden
    by_expert = pl.BlockSpec((1, width, hidden), lambda j: (j, 0, 0))
    out_shape = []
    for cap in caps:
        quarter = cap // 4
        for count in (quarter,) * 3 + (quarter // 2,) * 2:
            out_shape.append(jax.ShapeDtypeStruct((count, wide), BF))
        out_shape.append(jax.ShapeDtypeStruct((quarter, LANES), F32))
    out = pl.pallas_call(
        functools.partial(act_kernel, caps, window),
        grid=(n_local,),
        out_shape=tuple(out_shape),
        in_specs=[whole_smem(), whole_smem()]
        + payload_specs(chunk, width)
        + [whole_vmem()] * 2
        + [by_expert] * 3,
        out_specs=(whole_vmem(),) * len(out_shape),
        scratch_shapes=[pltpu.VMEM((caps[0], wide), F32), pltpu.VMEM((caps[0], LANES), F32)],
        compiler_params=pltpu.CompilerParams(
            vmem_limit_bytes=vmem_limit(chunk["payload"].shape[0])
        ),
        cost_estimate=cost(1e10),
        name="acts",
    )(
        idx, chunk["offs"], chunk["payload"], chunk["payload"], chunk["pos"], chunk["gate"],
        *weights,
    )
    return [out[6 * i : 6 * i + 6] for i in range(len(caps))]


def unit_kernel(_, *refs):
    parts, (gate, grads, route_part) = refs[:-3], refs[-3:]
    quarter, wide = grads.shape
    half = quarter // 2
    hidden = wide // 3
    for side in range(2):
        rows = slice(side * half, (side + 1) * half)
        own, from_x, from_y, late_x, late_y = parts
        near, late = ((from_x, late_y), (from_y, late_x))[side]
        sources = [(own, rows), (near, slice(half, quarter)), (late, slice(0, half))]

        def total(part):
            at = slice(part * hidden, (part + 1) * hidden)
            value = None
            for source, there in sources:
                term = source[there, at].astype(F32)
                value = term if value is None else value + term
            return value

        gate_act, up_act, back = total(0), total(1), total(2)
        sigma = 1.0 / (1.0 + jnp.exp(-gate_act))
        active = gate_act * sigma
        slope = sigma * (1.0 + gate_act * (1.0 - sigma))
        scaled = gate[rows, 0:1] * back
        unit = (active * up_act).astype(BF)
        grads[rows, 0:hidden] = (scaled * up_act * slope).astype(BF)
        grads[rows, hidden : 2 * hidden] = (scaled * active).astype(BF)
        grads[rows, 2 * hidden :] = unit
        sums = jnp.sum(back * unit.astype(F32), axis=1, keepdims=True)
        route_part[rows, :] = jnp.broadcast_to(sums, (half, LANES)).astype(BF)


def unit_grads(parts, earlier):
    quarter, wide = parts[0].shape
    return pl.pallas_call(
        unit_kernel,
        out_shape=(
            jax.ShapeDtypeStruct((quarter, wide), BF),
            jax.ShapeDtypeStruct((quarter, LANES), BF),
        ),
        in_specs=[pl.BlockSpec(memory_space=pl.ANY)] + [whole_vmem()] * len(parts),
        out_specs=(whole_vmem(),) * 2,
        compiler_params=pltpu.CompilerParams(vmem_limit_bytes=24 * MIB),
        name="units",
    )(earlier, *parts)


def place_quarters(me, pieces, target):
    own, from_x, from_y, first, second = pieces
    quarter = own.shape[0]
    half = quarter // 2

    def at(other, extra, count):
        return pl.ds(pl.multiple_of((me ^ other) * quarter + extra, ALIGN), count)

    target[at(0, 0, quarter), :] = own[...]
    target[at(1, 0, quarter), :] = from_x[...]
    target[at(2, 0, quarter), :] = from_y[...]
    target[at(3, 0, half), :] = first[...]
    target[at(3, half, half), :] = second[...]


def window_hits(members, caps, windows, total, offs, poss, expert):
    places, starts, lane_start = [], [], 0
    for c in members:
        start = window_start(offs[c], expert, caps[c], windows[c])
        column = expert_column(poss[c][...], expert)
        places.append(jnp.where(column >= 0, column - start + lane_start, -1))
        starts.append((c, start, lane_start))
        lane_start += windows[c]
    places = jnp.concatenate(places, axis=0)
    lanes = lax.broadcasted_iota(jnp.int32, (places.shape[0], total), 1)
    return places == lanes, starts


def slot_kernel(caps, windows, groups, first, given, _, *refs):
    count, size = len(caps), len(groups)
    offs, refs = refs[:count], refs[count:]
    xs, dys, poss, gates = (refs[i * count : (i + 1) * count] for i in range(4))
    refs = refs[4 * count + given :]
    outs, done, (x_turned, dy_turned) = refs[: 3 * size], refs[3 * size], refs[3 * size + 1 :]
    expert = pl.program_id(0) + first

    @pl.when(expert == first)
    def _():
        x_turned[...] = jnp.concatenate([ref[...] for ref in xs], axis=0).T
        dy_turned[...] = jnp.concatenate([ref[...] for ref in dys], axis=0).T
        done[...] = jnp.zeros_like(done)

    token_start = 0
    for i, members in enumerate(groups):
        pick_out, x_out, dy_out = outs[3 * i : 3 * i + 3]
        hit, _ = window_hits(members, caps, windows, pick_out.shape[2], offs, poss, expert)
        scale = jnp.concatenate([expert_column(gates[c][...], expert) for c in members], axis=0)
        pick = jnp.where(hit, 1.0, 0.0).astype(BF)
        pick_scaled = jnp.where(hit, scale, 0.0).astype(BF)
        lanes = slice(token_start, token_start + hit.shape[0])
        pick_out[0] = pick
        x_out[0] = jnp.dot(x_turned[:, lanes], pick, preferred_element_type=F32).astype(BF)
        dy_out[0] = jnp.dot(
            dy_turned[:, lanes], pick_scaled, preferred_element_type=F32
        ).astype(BF)
        token_start += hit.shape[0]


def gather_slots(earlier, tables, first, last, chunks, caps, windows, n_local, width):
    count = len(chunks)
    groups, totals = chunk_groups(count, windows)
    tokens = sum(chunk["payload"].shape[0] for chunk in chunks)
    shapes = []
    for members, total in zip(groups, totals):
        rows = sum(chunks[c]["payload"].shape[0] for c in members)
        shapes += [(rows, total), (width, total), (width, total)]
    out = pl.pallas_call(
        functools.partial(slot_kernel, caps, windows, groups, first, len(tables)),
        grid=(last - first,),
        out_shape=tuple(jax.ShapeDtypeStruct((n_local,) + shape, BF) for shape in shapes)
        + (jax.ShapeDtypeStruct((8, LANES), F32),),
        in_specs=[pl.BlockSpec(memory_space=pl.ANY)]
        + [whole_smem()] * count
        + [payload_specs(chunk, width)[side] for side in range(2) for chunk in chunks]
        + [whole_vmem()] * (2 * count)
        + [pl.BlockSpec(memory_space=pl.ANY)] * len(tables),
        out_specs=tuple(
            pl.BlockSpec((1,) + shape, lambda j: (j + first, 0, 0)) for shape in shapes
        )
        + (whole_vmem(),),
        scratch_shapes=[pltpu.VMEM((width, tokens), BF)] * 2,
        input_output_aliases={1 + 5 * count + i: i for i in range(len(tables))},
        compiler_params=pltpu.CompilerParams(vmem_limit_bytes=vmem_limit(tokens)),
        cost_estimate=cost(1e9),
        name="slots",
    )(
        earlier,
        *[chunk["offs"] for chunk in chunks],
        *[chunk["payload"] for chunk in chunks],
        *[chunk["payload"] for chunk in chunks],
        *[chunk["pos"] for chunk in chunks],
        *[chunk["gate"] for chunk in chunks],
        *tables,
    )
    return out[:-1], out[-1]


def window_starts(members, caps, windows, offs, expert):
    starts, lane_start = [], 0
    for c in members:
        starts.append((c, window_start(offs[c], expert, caps[c], windows[c]), lane_start))
        lane_start += windows[c]
    return starts


def token_kernel(caps, windows, groups, top, block, group, idx, *refs):
    count = len(caps)
    offs, refs = refs[:count], refs[count:]
    pieces, refs = refs[: 5 * count], refs[5 * count :]
    routes_own, metas = refs[:count], refs[count : 2 * count]
    picks, refs = refs[2 * count : 2 * count + len(groups)], refs[2 * count + len(groups) :]
    w_gate, w_up, keep, send = refs[:4]
    grads, routes, refs = refs[4 : 4 + count], refs[4 + count : 4 + 2 * count], refs[4 + 2 * count :]
    acc, route_acc = refs[:2]
    stacks, route_stacks = refs[2 : 2 + len(groups)], refs[2 + len(groups) :]
    expert = pl.program_id(0)
    _, width, hidden = w_gate.shape
    n_local = pl.num_programs(0)

    @pl.when(expert == 0)
    def _():
        for c in range(count):
            place_quarters(idx[2], pieces[5 * c : 5 * c + 5], grads[c])
            routes[c][...] = jnp.zeros_like(routes[c])
            quarter = caps[c] // 4
            at = pl.ds(pl.multiple_of(idx[2] * quarter, ALIGN), quarter)
            routes[c][at, :] = routes_own[c][...]
        acc[...] = jnp.zeros_like(acc)
        route_acc[...] = jnp.zeros_like(route_acc)
        for stacked in stacks + route_stacks:
            stacked[...] = jnp.zeros_like(stacked)

    named = (expert + idx[0] * n_local).astype(F32)
    token_start = 0
    for members, pick_ref, stacked, route_stacked in zip(groups, picks, stacks, route_stacks):
        for c, start, lane_start in window_starts(members, caps, windows, offs, expert):
            there = slice(lane_start, lane_start + windows[c])
            stacked[there, :] = grads[c][pl.ds(start, windows[c]), :]
            route_stacked[there, :] = routes[c][pl.ds(start, windows[c]), :]
        pick = pick_ref[0]
        row_grad = lax.dot_general(
            stacked[:, 0:hidden], w_gate[0], BY_COLUMN, preferred_element_type=F32
        ) + lax.dot_general(
            stacked[:, hidden : 2 * hidden],
            w_up[0],
            BY_COLUMN,
            preferred_element_type=F32,
        )
        rows = slice(token_start, token_start + pick.shape[0])
        acc[rows, :] += jnp.dot(pick, row_grad.astype(BF), preferred_element_type=F32)
        meta = jnp.concatenate([metas[c][...] for c in members], axis=0).astype(F32)
        lane = lax.broadcasted_iota(jnp.int32, meta.shape, 1)
        token_route = jnp.dot(pick, route_stacked[...], preferred_element_type=F32)
        route_acc[rows, :] = jnp.where(
            jnp.logical_and(lane < top, meta == named), token_route, route_acc[rows, :]
        )
        token_start += pick.shape[0]

    @pl.when(expert == n_local - 1)
    def _():
        blocks = group // block
        row = lax.broadcasted_iota(jnp.int32, (block, group), 0)
        column = lax.broadcasted_iota(jnp.int32, (block, group), 1)
        for target, which in ((keep, idx[1]), (send, 1 - idx[1])):
            chosen = jnp.where(column == row * blocks + which, 1.0, 0.0).astype(BF)
            for first in range(acc.shape[0] // group):
                rows = slice(first * group, (first + 1) * group)
                there = slice(first * block, (first + 1) * block)
                for lanes, values in ((slice(0, width), acc), (slice(width, None), route_acc)):
                    target[there, lanes] = jnp.dot(
                        chosen, values[rows, :].astype(BF), preferred_element_type=F32
                    ).astype(BF)


def chunk_groups(count, windows):
    groups = [tuple(range(min(count, 3)))] + [(c,) for c in range(3, count)]
    return groups, [round_up(sum(windows[c] for c in members), LANES) for members in groups]


def token_grads(
    idx, chunks, pieces, route_parts, tables, weights, caps, windows, top, block, group
):
    n_local, width, hidden = weights[0].shape
    by_expert = pl.BlockSpec((1, width, hidden), lambda j: (j, 0, 0))
    count = len(chunks)
    groups, totals = chunk_groups(count, windows)
    tokens = sum(chunk["payload"].shape[0] for chunk in chunks)
    result = jax.ShapeDtypeStruct((tokens // 2, width + LANES), BF)
    flat = [piece for group in pieces for piece in group]
    return pl.pallas_call(
        functools.partial(token_kernel, caps, windows, groups, top, block, group),
        grid=(n_local,),
        out_shape=(result, result),
        in_specs=[whole_smem()] * (1 + count)
        + [pl.BlockSpec((piece.shape[0], 2 * hidden), lambda j: (0, 0)) for piece in flat]
        + [whole_vmem()] * count
        + [
            pl.BlockSpec((chunk["payload"].shape[0], LANES), lambda j: (0, 2 * width // LANES))
            for chunk in chunks
        ]
        + [pl.BlockSpec((1,) + table[0].shape[1:], lambda j: (j, 0, 0)) for table in tables]
        + [by_expert] * 2,
        out_specs=(whole_vmem(),) * 2,
        scratch_shapes=[pltpu.VMEM((cap, 2 * hidden), BF) for cap in caps]
        + [pltpu.VMEM((cap, LANES), BF) for cap in caps]
        + [pltpu.VMEM((tokens, width), F32), pltpu.VMEM((tokens, LANES), F32)]
        + [pltpu.VMEM((total, 2 * hidden), BF) for total in totals]
        + [pltpu.VMEM((total, LANES), BF) for total in totals],
        compiler_params=pltpu.CompilerParams(vmem_limit_bytes=vmem_limit(tokens)),
        cost_estimate=cost(1e10),
        name="tokens",
    )(
        idx,
        *[chunk["offs"] for chunk in chunks],
        *flat,
        *route_parts,
        *[chunk["payload"] for chunk in chunks],
        *[table[0] for table in tables],
        *weights[:2],
    )


def weight_kernel(caps, windows, groups, idx, *refs):
    count, size = len(caps), len(groups)
    offs, refs = refs[:count], refs[count:]
    pieces, refs = refs[: 5 * count], refs[5 * count :]
    xs, dys, refs = refs[:size], refs[size : 2 * size], refs[2 * size :]
    outs, done, grads, stacks = refs[:3], refs[3], refs[4 : 4 + count], refs[4 + count :]
    expert = pl.program_id(0)
    hidden = outs[0].shape[2]

    @pl.when(expert == 0)
    def _():
        for c in range(count):
            place_quarters(idx[2], pieces[5 * c : 5 * c + 5], grads[c])
        for stacked in stacks:
            stacked[...] = jnp.zeros_like(stacked)
        done[...] = jnp.zeros_like(done)

    sums = [None] * 3
    for members, slot_x, slot_dy, stacked in zip(groups, xs, dys, stacks):
        for c, start, lane_start in window_starts(members, caps, windows, offs, expert):
            there = slice(lane_start, lane_start + windows[c])
            stacked[there, :] = grads[c][pl.ds(start, windows[c]), :]
        for part, left in enumerate((slot_x, slot_x, slot_dy)):
            columns = slice(part * hidden, (part + 1) * hidden)
            value = jnp.dot(left[0], stacked[:, columns], preferred_element_type=F32)
            sums[part] = value if sums[part] is None else sums[part] + value
    for out, value in zip(outs, sums):
        out[0] = value.astype(BF)


def weight_grads(idx, chunks, pieces, tables, caps, windows, n_local, width, hidden):
    count = len(chunks)
    wide = 3 * hidden
    groups, totals = chunk_groups(count, windows)
    tokens = sum(chunk["payload"].shape[0] for chunk in chunks)
    by_expert = pl.BlockSpec((1, width, hidden), lambda j: (j, 0, 0))
    slots = [table[side] for side in (1, 2) for table in tables]
    return pl.pallas_call(
        functools.partial(weight_kernel, caps, windows, groups),
        grid=(n_local,),
        out_shape=(jax.ShapeDtypeStruct((n_local, width, hidden), BF),) * 3
        + (jax.ShapeDtypeStruct((8, LANES), F32),),
        in_specs=[whole_smem()] * (1 + count)
        + [whole_vmem()] * (5 * count)
        + [pl.BlockSpec((1,) + slot.shape[1:], lambda j: (j, 0, 0)) for slot in slots],
        out_specs=(by_expert,) * 3 + (whole_vmem(),),
        scratch_shapes=[pltpu.VMEM((cap, wide), BF) for cap in caps]
        + [pltpu.VMEM((total, wide), BF) for total in totals],
        compiler_params=pltpu.CompilerParams(
            vmem_limit_bytes=(32 if tokens <= 512 else 56) * MIB
        ),
        cost_estimate=cost(2e10),
        name="weights",
    )(
        idx,
        *[chunk["offs"] for chunk in chunks],
        *[piece for group in pieces for piece in group],
        *slots,
    )


def to_partner(value, axis, other):
    return lax.ppermute(value, axis, [(i, i ^ other) for i in range(lax.axis_size(axis))])


def sum_over_dp(parts, earlier):
    own, send_x, send_y, later_x, later_y, gate = parts
    from_x = to_partner(send_x, "dp", 1)
    from_y = to_partner(send_y, "dp", 2)
    send_x, send_y = pair_sums(earlier, later_x, from_y, later_y, from_x)
    late_x = to_partner(send_x, "dp", 1)
    late_y = to_partner(send_y, "dp", 2)
    return [own, from_x, from_y, late_x, late_y, gate, send_x]


def gather_over_dp(own):
    half = own.shape[0] // 2
    from_x = to_partner(own, "dp", 1)
    from_y = to_partner(own, "dp", 2)
    first = to_partner(from_x[:half], "dp", 2)
    second = to_partner(from_y[half:], "dp", 1)
    return own, from_x, from_y, first, second


def finish_kernel(width, top, idx, *refs):
    parts, (token_grad, route_grad) = refs[:-2], refs[-2:]
    routes = None
    for distance, part in enumerate(parts):
        at = pl.ds(pl.multiple_of((idx[2] ^ distance) * width, LANES), width)
        token_grad[:, at] = part[:, 0:width]
        value = part[:, width:].astype(F32)
        routes = value if routes is None else routes + value
    route_grad[...] = routes[:, 0:top].astype(BF)


def finish(idx, parts, width, top):
    rows = parts[0].shape[0]
    return pl.pallas_call(
        functools.partial(finish_kernel, width, top),
        out_shape=(
            jax.ShapeDtypeStruct((rows, width * len(parts)), BF),
            jax.ShapeDtypeStruct((rows, top), BF),
        ),
        in_specs=[whole_smem()] + [whole_vmem()] * len(parts),
        out_specs=(whole_vmem(),) * 2,
        compiler_params=pltpu.CompilerParams(vmem_limit_bytes=24 * MIB),
        name="finish",
    )(idx, *parts)


def in_hbm(value):
    return pltpu.with_memory_space_constraint(value, pltpu.HBM)


def touch_kernel(*refs):
    ready = refs[-1]
    ready[...] = jnp.zeros_like(ready)


def touch(weights, earlier):
    near = [pltpu.with_memory_space_constraint(weight, pltpu.VMEM) for weight in weights]
    return pl.pallas_call(
        touch_kernel,
        out_shape=jax.ShapeDtypeStruct((8, LANES), F32),
        in_specs=[pl.BlockSpec(memory_space=pl.ANY)] + [whole_vmem()] * len(weights),
        out_specs=whole_vmem(),
        compiler_params=pltpu.CompilerParams(vmem_limit_bytes=24 * MIB),
        name="touch",
    )(earlier, *near)


def fits_kernel(lane, _, *refs):
    flags, parts, out = refs[:2], refs[2:-1], refs[-1]
    value = flags[0][0:1, 0:1]
    for flag in flags[1:]:
        value = jnp.minimum(value, flag[0:1, 0:1])
    for part in parts:
        value = jnp.minimum(value, part[0:16, lane : lane + 1].astype(F32)[0:1, :])
    out[0] = (value[0, 0] > 0.5).astype(jnp.int32)


def all_fit(earlier, flags, parts, width, top):
    lane = width // LANES
    return pl.pallas_call(
        functools.partial(fits_kernel, 2 * top),
        grid=(1,),
        out_shape=jax.ShapeDtypeStruct((1,), jnp.int32),
        in_specs=[pl.BlockSpec(memory_space=pl.ANY)]
        + [pl.BlockSpec((8, LANES), lambda i: (0, 0))] * len(flags)
        + [pl.BlockSpec((part.shape[0], LANES), lambda i: (0, lane)) for part in parts],
        out_specs=whole_smem(),
        compiler_params=pltpu.CompilerParams(vmem_limit_bytes=24 * MIB),
        name="fits",
    )(earlier, *flags, *parts)[0]


def relay_kernel(_, *refs):
    parts, out = refs[:-1], refs[-1]
    first = 0
    for part in parts:
        out[first : first + part.shape[0], :] = part[...]
        first += part.shape[0]


def relay(parts, earlier):
    rows = sum(part.shape[0] for part in parts)
    return pl.pallas_call(
        relay_kernel,
        out_shape=jax.ShapeDtypeStruct((rows, parts[0].shape[1]), BF),
        in_specs=[pl.BlockSpec(memory_space=pl.ANY)] + [whole_vmem()] * len(parts),
        out_specs=whole_vmem(),
        compiler_params=pltpu.CompilerParams(vmem_limit_bytes=24 * MIB),
        name="relay",
    )(earlier, *parts)


def pair_kernel(_, later_x, from_y, later_y, from_x, out_x, out_y):
    out_x[...] = (later_x[...].astype(F32) + from_y[...].astype(F32)).astype(BF)
    out_y[...] = (later_y[...].astype(F32) + from_x[...].astype(F32)).astype(BF)


def pair_sums(earlier, later_x, from_y, later_y, from_x):
    spec = pl.BlockSpec(later_x.shape, lambda i: (0, 0))
    return pl.pallas_call(
        pair_kernel,
        grid=(1,),
        out_shape=(jax.ShapeDtypeStruct(later_x.shape, BF),) * 2,
        in_specs=[pl.BlockSpec(memory_space=pl.ANY)] + [spec] * 4,
        out_specs=(spec,) * 2,
        compiler_params=pltpu.CompilerParams(vmem_limit_bytes=24 * MIB),
        name="pair",
    )(earlier, later_x, from_y, later_y, from_x)


def add_kernel(count, _, *refs):
    parts, outs = refs[:count], refs[count:]
    total = parts[0][...].astype(F32)
    for part in parts[1:]:
        total = total + part[...].astype(F32)
    rows = outs[0].shape[0]
    for i, out in enumerate(outs):
        out[...] = total[i * rows : (i + 1) * rows, :].astype(BF)


def add_up(parts, earlier, pieces):
    rows, lanes = parts[0].shape
    return pl.pallas_call(
        functools.partial(add_kernel, len(parts)),
        out_shape=(jax.ShapeDtypeStruct((rows // pieces, lanes), BF),) * pieces,
        in_specs=[pl.BlockSpec(memory_space=pl.ANY)] + [whole_vmem()] * len(parts),
        out_specs=(whole_vmem(),) * pieces,
        compiler_params=pltpu.CompilerParams(vmem_limit_bytes=24 * MIB),
        name="add",
    )(earlier, *parts)


def on_device(tokens_in, cotangent, expert_ids, gate_probs, gate_weight, up_weight, down_weight):
    n_expert, n_dp = lax.axis_size("expert"), lax.axis_size("dp")
    expert_at, half_at, dp_at = (lax.axis_index(name) for name in ("expert", "half", "dp"))
    idx = jnp.stack([expert_at, half_at, dp_at]).astype(jnp.int32)
    n_local, width, hidden = gate_weight.shape
    weights = (gate_weight, up_weight, down_weight)
    _, blocks, block_tokens, _ = tokens_in.shape
    top = expert_ids.shape[3]
    block = n_dp * block_tokens
    owner_rows = blocks * block_tokens
    group = blocks * block

    parts = pack(
        idx,
        in_hbm(tokens_in[0].transpose(1, 0, 2)),
        in_hbm(cotangent[0].transpose(1, 0, 2)),
        in_hbm(expert_ids[0].transpose(0, 2, 1)),
        in_hbm(gate_probs[0].transpose(0, 2, 1)),
        n_dp,
        width,
    )
    parts = [parts[0]] + [to_partner(parts[k], "dp", k) for k in range(1, n_dp)]

    unit = round_up(n_local * group // 2, LANES)
    small = round_up(n_local * group // 3, LANES)
    choose = small < unit and n_expert <= 4

    def put_together(earlier, parts, kind, span):
        rows = span * group
        return route(
            earlier, idx, parts, kind, rows, n_local, n_expert, small, top, width, owner_rows
        )

    ready = touch(weights[:2], parts[0])
    own, mixed, fits = put_together(ready, parts, "own", 1)
    got = [to_partner(mixed, "expert", k) for k in (1, 2) if k < n_expert]
    window = round_up(group // 2 + ALIGN, LANES)
    units = (unit, small) if choose else (unit,)
    own_sums = partial_acts(idx, own, weights, units, window)
    operands = (own, own_sums, got, weights)
    rest = functools.partial(
        exchange_and_multiply, put_together, idx, half_at, n_expert, n_dp, top, block, group
    )
    if not choose:
        return rest(0, unit, operands)
    flags = [fits, to_partner(fits, "expert", n_expert - 1)]
    return lax.cond(
        all_fit(own_sums[0][-1], flags, got, width, top) == 1,
        functools.partial(rest, 1, small),
        functools.partial(rest, 0, unit),
        operands,
    )


def exchange_and_multiply(
    put_together, idx, half_at, n_expert, n_dp, top, block, group, choice, unit, operands
):
    own, own_sums, got, weights = operands
    own_sums = own_sums[choice]
    n_local, width, hidden = weights[0].shape

    chunks, sums, caps, windows, held = [], [], [], [], 0
    while held < n_expert:
        if held == 0:
            chunk, span, cap = own, 1, unit
        else:
            if held == 1:
                far = relay(got, own_sums[-1])
                ready = touch(weights, far)
            elif held == 3:
                far = to_partner(got[1], "expert", 1)
                own_total = sum_over_dp(own_sums, sums[1][-1])
                ready = own_total[-1]
            else:
                known = jnp.concatenate([chunk["payload"] for chunk in chunks], axis=0)
                side = jnp.where(half_at == 0, known[:, :width], known[:, width : 2 * width])
                far = jnp.concatenate([side, known[:, 2 * width :]], axis=1)
                far = to_partner(far, "expert", held)
            span = far.shape[0] // group
            chunk = put_together(ready, [far, to_partner(far, "half", 1)], "far", span)
            cap = round_up(span * unit, LANES)
        most = span * group // 2
        chunks.append(chunk)
        caps.append(cap)
        windows.append(round_up(most + ALIGN, ALIGN))
        if held == 0:
            sums.append(own_sums)
        else:
            wide_window = round_up(most + ALIGN, LANES)
            sums.append(partial_acts(idx, chunk, weights, (cap,), wide_window)[0])
        held += span

    pieces, route_parts = [], []

    def finish_units(total, earlier):
        grads, route_part = unit_grads(total[:-1], earlier)
        pieces.append(gather_over_dp(grads))
        route_parts.append(route_part)

    if len(sums) <= 2:
        own_total = sum_over_dp(own_sums, sums[-1][-1])
    finish_units(own_total, sums[min(2, len(sums) - 1)][-1])
    tables, ready = [], n_local // 2

    def slots(earlier, tables, first, last):
        return gather_slots(
            earlier, tables, first, last, chunks, caps, windows, n_local, width
        )

    totals = [
        sum_over_dp(parts, route_parts[0] if i == 0 else parts[-1])
        for i, parts in enumerate(sums[1:])
    ]
    for i, total in enumerate(totals):
        earlier = pieces[0][2] if i == 0 else total[-2]
        if ready and i == len(totals) - 1:
            tables, earlier = slots(route_parts[-1], tables, 0, ready)
        finish_units(total, earlier)
    tables, _ = slots(route_parts[-1], tables, ready if tables else 0, n_local)
    tables = [tables[i : i + 3] for i in range(0, len(tables), 3)]

    keep, send = token_grads(
        idx, chunks, pieces, route_parts, tables, weights, caps, windows, top, block, group
    )
    both = (keep.astype(F32) + to_partner(send, "half", 1).astype(F32)).astype(BF)
    *weight_out, written = weight_grads(
        idx, chunks, pieces, tables, caps, windows, n_local, width, hidden
    )
    held = jnp.split(both, n_expert, axis=0)
    step = n_expert // 2
    while step > 2:
        got = to_partner(jnp.concatenate(held[step:], axis=0), "expert", step)
        held = [
            (mine.astype(F32) + other.astype(F32)).astype(BF)
            for mine, other in zip(held[:step], jnp.split(got, step, axis=0))
        ]
        step //= 2
    total = held[:1] + [to_partner(held[k], "expert", k) for k in range(1, len(held))]
    total = add_up(total, written, n_dp)
    total = [total[0]] + [to_partner(total[k], "dp", k) for k in range(1, n_dp)]
    token_grad, route_grad = finish(idx, total, width, top)
    return (token_grad[None, None], route_grad[None, None]) + tuple(weight_out)


def solution(mesh):
    return jax.shard_map(
        on_device,
        mesh=mesh,
        in_specs=(
            P(("expert", "dp"), None, None, None),
            P(("expert", "dp"), None, None, None),
            P(("expert", "dp"), None, None, None),
            P(("expert", "dp"), None, None, None),
            P("expert", "dp", "half"),
            P("expert", "dp", "half"),
            P("expert", "dp", "half"),
        ),
        out_specs=(
            P(("expert", "dp"), "half", None, None),
            P(("expert", "dp"), "half", None, None),
            P("expert", "dp", "half"),
            P("expert", "dp", "half"),
            P("expert", "dp", "half"),
        ),
        check_vma=False,
    )
```

```python
import functools

import jax
import jax.numpy as jnp
from jax import lax
from jax.experimental import pallas as pl
from jax.experimental.pallas import tpu as pltpu
from jax.sharding import PartitionSpec as P

LANES = 128
ALIGN = 16
BF = jnp.bfloat16
F32 = jnp.float32
BY_ROW = (((0,), (0,)), ((), ()))
BY_COLUMN = (((1,), (1,)), ((), ()))
MIB = 1 << 20


def round_up(value, step):
    return -(-value // step) * step


def cost(flops):
    return pl.CostEstimate(flops=int(flops), bytes_accessed=0, transcendentals=0)


def vmem_limit(rows):
    return (24 if rows <= 512 else 56) * MIB


def whole_vmem():
    return pl.BlockSpec(memory_space=pltpu.VMEM)


def whole_smem():
    return pl.BlockSpec(memory_space=pltpu.SMEM)


def expert_column(table, expert):
    lane = lax.broadcasted_iota(jnp.int32, table.shape, 1)
    return jnp.sum(jnp.where(lane == expert, table, 0), axis=1, keepdims=True)


def window_start(offs, expert, cap, window):
    start = jnp.minimum((offs[0, expert] // ALIGN) * ALIGN, cap - window)
    return pl.multiple_of(start, ALIGN)


def pack_kernel(width, top, idx, x, dy, ids, gates, *outs):
    tokens, blocks, _ = x.shape
    rows = tokens * blocks
    row = lax.broadcasted_iota(jnp.int32, (rows, tokens), 0)
    token = lax.broadcasted_iota(jnp.int32, (rows, tokens), 1)
    fill = jnp.full((LANES - 2 * top, tokens), -1.0, BF)
    meta = jnp.zeros((rows, LANES), F32)
    for block in range(blocks):
        place = jnp.where(row == token * blocks + block, 1.0, 0.0).astype(BF)
        table = jnp.concatenate([ids[block].astype(F32).astype(BF), gates[block], fill], axis=0)
        meta += lax.dot_general(place, table, BY_COLUMN, preferred_element_type=F32)
    for distance, out in enumerate(outs):
        at = pl.ds(pl.multiple_of((idx[2] ^ distance) * width, LANES), width)
        for t in range(tokens):
            there = slice(t * blocks, (t + 1) * blocks)
            out[there, 0:width] = x[t, :, at]
            out[there, width : 2 * width] = dy[t, :, at]
        out[:, 2 * width :] = meta.astype(BF)


def pack(idx, x, dy, ids, gates, n_dp, width):
    shape = (x.shape[0] * x.shape[1], 2 * width + LANES)
    return pl.pallas_call(
        functools.partial(pack_kernel, width, ids.shape[1]),
        out_shape=(jax.ShapeDtypeStruct(shape, BF),) * n_dp,
        in_specs=[whole_smem()] + [whole_vmem()] * 4,
        out_specs=(whole_vmem(),) * n_dp,
        compiler_params=pltpu.CompilerParams(vmem_limit_bytes=24 * MIB),
        name="pack",
    )(idx, x, dy, ids, gates)


def shared_order(place, step, dp_at):
    owner = ((place.astype(F32) + 0.5) * (1.0 / step)).astype(jnp.int32)
    return place + ((owner ^ dp_at) - owner) * step


def route_kernel(n_local, n_expert, unit, top, width, step, kind, count, _, idx, *refs):
    parts, (pos, gate, offs, payload), rest = refs[:count], refs[count : count + 4], refs[count + 4 :]
    if kind == "own":
        for distance, part in enumerate(parts):
            payload[distance * step : (distance + 1) * step, :] = part[...]
        mixed, fits = rest
        mixed[:, 0:width] = jnp.where(
            idx[1] == 0, payload[:, 0:width], payload[:, width : 2 * width]
        )
        lane = lax.broadcasted_iota(jnp.int32, gate.shape, 1)
        names = payload[:, 2 * width :].astype(F32)
        first_name = (lane * n_local).astype(F32)
        named = jnp.zeros(gate.shape, F32)
        for k in range(top):
            name = names[:, k : k + 1]
            inside = jnp.logical_and(name >= first_name, name < first_name + n_local)
            named += jnp.where(jnp.logical_and(inside, lane < n_expert), 1.0, 0.0)
        most = jnp.max(jnp.sum(named, axis=0, keepdims=True), axis=1, keepdims=True)
        flag = jnp.where(most <= unit, 1.0, 0.0)
        fits[...] = jnp.broadcast_to(flag, fits.shape)
        mixed[:, width:] = jnp.where(lane == 2 * top, flag, names).astype(BF)
    else:
        first = 0
        for near, other in zip(parts[: count // 2], parts[count // 2 :]):
            rows = slice(first, first + near.shape[0])
            payload[rows, 0:width] = jnp.where(idx[1] == 0, near[:, 0:width], other[:, 0:width])
            payload[rows, width : 2 * width] = jnp.where(
                idx[1] == 0, other[:, 0:width], near[:, 0:width]
            )
            payload[rows, 2 * width :] = near[:, width:]
            first += near.shape[0]
    rows = payload.shape[0]
    meta = payload[:, 2 * width :].astype(F32)
    lane = lax.broadcasted_iota(jnp.int32, (rows, LANES), 1)
    here = (lane + idx[0] * n_local).astype(F32)
    chosen = jnp.zeros((rows, LANES), F32)
    gates = jnp.zeros((rows, LANES), F32)
    for k in range(top):
        hit = jnp.logical_and(meta[:, k : k + 1] == here, lane < n_local)
        chosen = jnp.where(hit, 1.0, chosen)
        gates = jnp.where(hit, meta[:, top + k : top + k + 1], gates)
    place_column = shared_order(lax.broadcasted_iota(jnp.int32, (rows, 1), 0), step, idx[2])
    place_row = shared_order(lax.broadcasted_iota(jnp.int32, (1, rows), 1), step, idx[2])
    earlier = jnp.where(place_row < place_column, 1.0, 0.0)
    rank = jnp.dot(earlier.astype(BF), chosen.astype(BF), preferred_element_type=F32)
    counts = jnp.broadcast_to(jnp.sum(chosen, axis=0, keepdims=True), (8, LANES))
    before = (
        lax.broadcasted_iota(jnp.int32, (LANES, LANES), 0)
        < lax.broadcasted_iota(jnp.int32, (LANES, LANES), 1)
    )
    starts = jnp.dot(
        counts, before.astype(F32), preferred_element_type=F32, precision=lax.Precision.HIGHEST
    )
    pos[...] = jnp.where(chosen > 0.0, rank + starts[0:1], -1.0).astype(jnp.int32)
    gate[...] = gates
    offs[...] = starts.astype(jnp.int32)


def route(earlier, idx, parts, kind, rows, n_local, n_expert, unit, top, width, step):
    out_shape = [
        jax.ShapeDtypeStruct((rows, LANES), jnp.int32),
        jax.ShapeDtypeStruct((rows, LANES), F32),
        jax.ShapeDtypeStruct((8, LANES), jnp.int32),
        jax.ShapeDtypeStruct((rows, 2 * width + LANES), BF),
    ]
    if kind == "own":
        out_shape.append(jax.ShapeDtypeStruct((rows, width + LANES), BF))
        out_shape.append(jax.ShapeDtypeStruct((8, LANES), F32))
    out = pl.pallas_call(
        functools.partial(
            route_kernel, n_local, n_expert, unit, top, width, step, kind, len(parts)
        ),
        out_shape=tuple(out_shape),
        in_specs=[pl.BlockSpec(memory_space=pl.ANY), whole_smem()] + [whole_vmem()] * len(parts),
        out_specs=(whole_vmem(),) * len(out_shape),
        compiler_params=pltpu.CompilerParams(vmem_limit_bytes=vmem_limit(rows)),
        name="route",
    )(earlier, idx, *parts)
    chunk = {"pos": out[0], "gate": out[1], "offs": out[2], "payload": out[3]}
    return (chunk, out[4], out[5]) if kind == "own" else chunk


def act_kernel(caps, window, idx, offs, x, dy, pos, gate, w_gate, w_up, w_down, *refs):
    outs, (acc, gate_acc) = refs[:-2], refs[-2:]
    expert = pl.program_id(0)
    hidden = w_gate.shape[2]

    @pl.when(expert == 0)
    def _():
        acc[...] = jnp.zeros_like(acc)
        gate_acc[...] = jnp.zeros_like(gate_acc)

    start = pl.multiple_of((offs[0, expert] // ALIGN) * ALIGN, ALIGN)
    column = expert_column(pos[...], expert)
    slot = lax.broadcasted_iota(jnp.int32, (x.shape[0], window), 1)
    pick = jnp.where(jnp.logical_and(column >= 0, column - start == slot), 1.0, 0.0).astype(BF)
    gate_col = jnp.broadcast_to(expert_column(gate[...], expert), gate.shape).astype(BF)
    slot_x = lax.dot_general(pick, x[...], BY_ROW, preferred_element_type=F32).astype(BF)
    slot_dy = lax.dot_general(pick, dy[...], BY_ROW, preferred_element_type=F32).astype(BF)
    slot_gate = lax.dot_general(pick, gate_col, BY_ROW, preferred_element_type=F32)
    row = start + lax.broadcasted_iota(jnp.int32, (ALIGN, 1), 0)
    mine = row >= offs[0, expert]
    edge, rest = pl.ds(start, ALIGN), pl.ds(start + ALIGN, window - ALIGN)

    def store(target, columns, value):
        target[edge, columns] = jnp.where(mine, value[:ALIGN], target[edge, columns])
        target[rest, columns] = value[ALIGN:]

    store(gate_acc, slice(None), slot_gate)
    for part, (left, right) in enumerate(((slot_x, w_gate), (slot_x, w_up), (slot_dy, w_down))):
        columns = slice(part * hidden, (part + 1) * hidden)
        store(acc, columns, jnp.dot(left, right[0], preferred_element_type=F32))

    @pl.when(expert == pl.num_programs(0) - 1)
    def _():
        me = idx[2]

        def piece(quarter, other, first, count):
            at = pl.multiple_of((me ^ other) * quarter + first, ALIGN)
            return acc[pl.ds(at, count), :].astype(BF)

        for i, rows_of in enumerate(caps):
            quarter = rows_of // 4
            half = quarter // 2
            own, send_x, send_y, later_x, later_y, own_gate = outs[6 * i : 6 * i + 6]
            own[...] = piece(quarter, 0, 0, quarter)
            send_x[0:half, :] = piece(quarter, 3, 0, half)
            send_x[half:quarter, :] = piece(quarter, 1, 0, half)
            send_y[0:half, :] = piece(quarter, 3, half, half)
            send_y[half:quarter, :] = piece(quarter, 2, half, half)
            later_x[...] = piece(quarter, 1, half, half)
            later_y[...] = piece(quarter, 2, 0, half)
            own_gate[...] = gate_acc[pl.ds(pl.multiple_of(me * quarter, ALIGN), quarter), :]


def payload_specs(chunk, width):
    rows = chunk["payload"].shape[0]
    return [pl.BlockSpec((rows, width), lambda j, part=part: (0, part)) for part in range(2)]


def partial_acts(idx, chunk, weights, caps, window):
    n_local, width, hidden = weights[0].shape
    wide = 3 * hidden
    by_expert = pl.BlockSpec((1, width, hidden), lambda j: (j, 0, 0))
    out_shape = []
    for cap in caps:
        quarter = cap // 4
        for count in (quarter,) * 3 + (quarter // 2,) * 2:
            out_shape.append(jax.ShapeDtypeStruct((count, wide), BF))
        out_shape.append(jax.ShapeDtypeStruct((quarter, LANES), F32))
    out = pl.pallas_call(
        functools.partial(act_kernel, caps, window),
        grid=(n_local,),
        out_shape=tuple(out_shape),
        in_specs=[whole_smem(), whole_smem()]
        + payload_specs(chunk, width)
        + [whole_vmem()] * 2
        + [by_expert] * 3,
        out_specs=(whole_vmem(),) * len(out_shape),
        scratch_shapes=[
            pltpu.VMEM((caps[0] + window, wide), F32),
            pltpu.VMEM((caps[0] + window, LANES), F32),
        ],
        compiler_params=pltpu.CompilerParams(
            vmem_limit_bytes=vmem_limit(chunk["payload"].shape[0])
        ),
        cost_estimate=cost(1e10),
        name="acts",
    )(
        idx, chunk["offs"], chunk["payload"], chunk["payload"], chunk["pos"], chunk["gate"],
        *weights,
    )
    return [out[6 * i : 6 * i + 6] for i in range(len(caps))]


def unit_kernel(_, *refs):
    parts, (gate, grads, route_part) = refs[:-3], refs[-3:]
    quarter, wide = grads.shape
    half = quarter // 2
    hidden = wide // 3
    for side in range(2):
        rows = slice(side * half, (side + 1) * half)
        own, from_x, from_y, late_x, late_y = parts
        near, late = ((from_x, late_y), (from_y, late_x))[side]
        sources = [(own, rows), (near, slice(half, quarter)), (late, slice(0, half))]

        def total(part):
            at = slice(part * hidden, (part + 1) * hidden)
            value = None
            for source, there in sources:
                term = source[there, at].astype(F32)
                value = term if value is None else value + term
            return value

        gate_act, up_act, back = total(0), total(1), total(2)
        sigma = 1.0 / (1.0 + jnp.exp(-gate_act))
        active = gate_act * sigma
        slope = sigma * (1.0 + gate_act * (1.0 - sigma))
        scaled = gate[rows, 0:1] * back
        unit = (active * up_act).astype(BF)
        grads[rows, 0:hidden] = (scaled * up_act * slope).astype(BF)
        grads[rows, hidden : 2 * hidden] = (scaled * active).astype(BF)
        grads[rows, 2 * hidden :] = unit
        sums = jnp.sum(back * unit.astype(F32), axis=1, keepdims=True)
        route_part[rows, :] = jnp.broadcast_to(sums, (half, LANES)).astype(BF)


def unit_grads(parts, earlier):
    quarter, wide = parts[0].shape
    return pl.pallas_call(
        unit_kernel,
        out_shape=(
            jax.ShapeDtypeStruct((quarter, wide), BF),
            jax.ShapeDtypeStruct((quarter, LANES), BF),
        ),
        in_specs=[pl.BlockSpec(memory_space=pl.ANY)] + [whole_vmem()] * len(parts),
        out_specs=(whole_vmem(),) * 2,
        compiler_params=pltpu.CompilerParams(vmem_limit_bytes=24 * MIB),
        name="units",
    )(earlier, *parts)


def place_quarters(me, pieces, target):
    own, from_x, from_y, first, second = pieces
    quarter = own.shape[0]
    half = quarter // 2

    def at(other, extra, count):
        return pl.ds(pl.multiple_of((me ^ other) * quarter + extra, ALIGN), count)

    target[at(0, 0, quarter), :] = own[...]
    target[at(1, 0, quarter), :] = from_x[...]
    target[at(2, 0, quarter), :] = from_y[...]
    target[at(3, 0, half), :] = first[...]
    target[at(3, half, half), :] = second[...]


def window_hits(members, caps, windows, total, offs, poss, expert):
    places, starts, lane_start = [], [], 0
    for c in members:
        start = window_start(offs[c], expert, caps[c], windows[c])
        column = expert_column(poss[c][...], expert)
        places.append(jnp.where(column >= 0, column - start + lane_start, -1))
        starts.append((c, start, lane_start))
        lane_start += windows[c]
    places = jnp.concatenate(places, axis=0)
    lanes = lax.broadcasted_iota(jnp.int32, (places.shape[0], total), 1)
    return places == lanes, starts


def slot_kernel(caps, windows, groups, first, given, _, *refs):
    count, size = len(caps), len(groups)
    offs, refs = refs[:count], refs[count:]
    xs, dys, poss, gates = (refs[i * count : (i + 1) * count] for i in range(4))
    refs = refs[4 * count + given :]
    outs, done, (x_turned, dy_turned) = refs[: 3 * size], refs[3 * size], refs[3 * size + 1 :]
    expert = pl.program_id(0) + first

    @pl.when(expert == first)
    def _():
        x_turned[...] = jnp.concatenate([ref[...] for ref in xs], axis=0).T
        dy_turned[...] = jnp.concatenate([ref[...] for ref in dys], axis=0).T
        done[...] = jnp.zeros_like(done)

    token_start = 0
    for i, members in enumerate(groups):
        pick_out, x_out, dy_out = outs[3 * i : 3 * i + 3]
        hit, _ = window_hits(members, caps, windows, pick_out.shape[2], offs, poss, expert)
        scale = jnp.concatenate([expert_column(gates[c][...], expert) for c in members], axis=0)
        pick = jnp.where(hit, 1.0, 0.0).astype(BF)
        pick_scaled = jnp.where(hit, scale, 0.0).astype(BF)
        lanes = slice(token_start, token_start + hit.shape[0])
        pick_out[0] = pick
        x_out[0] = jnp.dot(x_turned[:, lanes], pick, preferred_element_type=F32).astype(BF)
        dy_out[0] = jnp.dot(
            dy_turned[:, lanes], pick_scaled, preferred_element_type=F32
        ).astype(BF)
        token_start += hit.shape[0]


def gather_slots(earlier, tables, first, last, chunks, caps, windows, n_local, width):
    count = len(chunks)
    groups, totals = chunk_groups(count, windows)
    tokens = sum(chunk["payload"].shape[0] for chunk in chunks)
    shapes = []
    for members, total in zip(groups, totals):
        rows = sum(chunks[c]["payload"].shape[0] for c in members)
        shapes += [(rows, total), (width, total), (width, total)]
    out = pl.pallas_call(
        functools.partial(slot_kernel, caps, windows, groups, first, len(tables)),
        grid=(last - first,),
        out_shape=tuple(jax.ShapeDtypeStruct((n_local,) + shape, BF) for shape in shapes)
        + (jax.ShapeDtypeStruct((8, LANES), F32),),
        in_specs=[pl.BlockSpec(memory_space=pl.ANY)]
        + [whole_smem()] * count
        + [payload_specs(chunk, width)[side] for side in range(2) for chunk in chunks]
        + [whole_vmem()] * (2 * count)
        + [pl.BlockSpec(memory_space=pl.ANY)] * len(tables),
        out_specs=tuple(
            pl.BlockSpec((1,) + shape, lambda j: (j + first, 0, 0)) for shape in shapes
        )
        + (whole_vmem(),),
        scratch_shapes=[pltpu.VMEM((width, tokens), BF)] * 2,
        input_output_aliases={1 + 5 * count + i: i for i in range(len(tables))},
        compiler_params=pltpu.CompilerParams(vmem_limit_bytes=vmem_limit(tokens)),
        cost_estimate=cost(1e9),
        name="slots",
    )(
        earlier,
        *[chunk["offs"] for chunk in chunks],
        *[chunk["payload"] for chunk in chunks],
        *[chunk["payload"] for chunk in chunks],
        *[chunk["pos"] for chunk in chunks],
        *[chunk["gate"] for chunk in chunks],
        *tables,
    )
    return out[:-1], out[-1]


def window_starts(members, caps, windows, offs, expert):
    starts, lane_start = [], 0
    for c in members:
        starts.append((c, window_start(offs[c], expert, caps[c], windows[c]), lane_start))
        lane_start += windows[c]
    return starts


def token_kernel(caps, windows, groups, top, block, group, idx, *refs):
    count = len(caps)
    offs, refs = refs[:count], refs[count:]
    pieces, refs = refs[: 5 * count], refs[5 * count :]
    routes_own, metas = refs[:count], refs[count : 2 * count]
    picks, refs = refs[2 * count : 2 * count + len(groups)], refs[2 * count + len(groups) :]
    w_gate, w_up, keep, send = refs[:4]
    grads, routes, refs = refs[4 : 4 + count], refs[4 + count : 4 + 2 * count], refs[4 + 2 * count :]
    acc, route_acc = refs[:2]
    stacks, route_stacks = refs[2 : 2 + len(groups)], refs[2 + len(groups) :]
    expert = pl.program_id(0)
    _, width, hidden = w_gate.shape
    n_local = pl.num_programs(0)

    @pl.when(expert == 0)
    def _():
        for c in range(count):
            place_quarters(idx[2], pieces[5 * c : 5 * c + 5], grads[c])
            routes[c][...] = jnp.zeros_like(routes[c])
            quarter = caps[c] // 4
            at = pl.ds(pl.multiple_of(idx[2] * quarter, ALIGN), quarter)
            routes[c][at, :] = routes_own[c][...]
        acc[...] = jnp.zeros_like(acc)
        route_acc[...] = jnp.zeros_like(route_acc)
        for stacked in stacks + route_stacks:
            stacked[...] = jnp.zeros_like(stacked)

    named = (expert + idx[0] * n_local).astype(F32)
    token_start = 0
    for members, pick_ref, stacked, route_stacked in zip(groups, picks, stacks, route_stacks):
        for c, start, lane_start in window_starts(members, caps, windows, offs, expert):
            there = slice(lane_start, lane_start + windows[c])
            stacked[there, :] = grads[c][pl.ds(start, windows[c]), :]
            route_stacked[there, :] = routes[c][pl.ds(start, windows[c]), :]
        pick = pick_ref[0]
        row_grad = lax.dot_general(
            stacked[:, 0:hidden], w_gate[0], BY_COLUMN, preferred_element_type=F32
        ) + lax.dot_general(
            stacked[:, hidden : 2 * hidden],
            w_up[0],
            BY_COLUMN,
            preferred_element_type=F32,
        )
        rows = slice(token_start, token_start + pick.shape[0])
        acc[rows, :] += jnp.dot(pick, row_grad.astype(BF), preferred_element_type=F32)
        meta = jnp.concatenate([metas[c][...] for c in members], axis=0).astype(F32)
        lane = lax.broadcasted_iota(jnp.int32, meta.shape, 1)
        token_route = jnp.dot(pick, route_stacked[...], preferred_element_type=F32)
        route_acc[rows, :] = jnp.where(
            jnp.logical_and(lane < top, meta == named), token_route, route_acc[rows, :]
        )
        token_start += pick.shape[0]

    @pl.when(expert == n_local - 1)
    def _():
        blocks = group // block
        row = lax.broadcasted_iota(jnp.int32, (block, group), 0)
        column = lax.broadcasted_iota(jnp.int32, (block, group), 1)
        for target, which in ((keep, idx[1]), (send, 1 - idx[1])):
            chosen = jnp.where(column == row * blocks + which, 1.0, 0.0).astype(BF)
            for first in range(acc.shape[0] // group):
                rows = slice(first * group, (first + 1) * group)
                there = slice(first * block, (first + 1) * block)
                for lanes, values in ((slice(0, width), acc), (slice(width, None), route_acc)):
                    target[there, lanes] = jnp.dot(
                        chosen, values[rows, :].astype(BF), preferred_element_type=F32
                    ).astype(BF)


def chunk_groups(count, windows):
    groups = [tuple(range(min(count, 3)))] + [(c,) for c in range(3, count)]
    return groups, [round_up(sum(windows[c] for c in members), LANES) for members in groups]


def token_grads(
    idx, chunks, pieces, route_parts, tables, weights, caps, windows, top, block, group
):
    n_local, width, hidden = weights[0].shape
    by_expert = pl.BlockSpec((1, width, hidden), lambda j: (j, 0, 0))
    count = len(chunks)
    groups, totals = chunk_groups(count, windows)
    tokens = sum(chunk["payload"].shape[0] for chunk in chunks)
    result = jax.ShapeDtypeStruct((tokens // 2, width + LANES), BF)
    flat = [piece for group in pieces for piece in group]
    return pl.pallas_call(
        functools.partial(token_kernel, caps, windows, groups, top, block, group),
        grid=(n_local,),
        out_shape=(result, result),
        in_specs=[whole_smem()] * (1 + count)
        + [pl.BlockSpec((piece.shape[0], 2 * hidden), lambda j: (0, 0)) for piece in flat]
        + [whole_vmem()] * count
        + [
            pl.BlockSpec((chunk["payload"].shape[0], LANES), lambda j: (0, 2 * width // LANES))
            for chunk in chunks
        ]
        + [pl.BlockSpec((1,) + table[0].shape[1:], lambda j: (j, 0, 0)) for table in tables]
        + [by_expert] * 2,
        out_specs=(whole_vmem(),) * 2,
        scratch_shapes=[pltpu.VMEM((cap, 2 * hidden), BF) for cap in caps]
        + [pltpu.VMEM((cap, LANES), BF) for cap in caps]
        + [pltpu.VMEM((tokens, width), F32), pltpu.VMEM((tokens, LANES), F32)]
        + [pltpu.VMEM((total, 2 * hidden), BF) for total in totals]
        + [pltpu.VMEM((total, LANES), BF) for total in totals],
        compiler_params=pltpu.CompilerParams(vmem_limit_bytes=vmem_limit(tokens)),
        cost_estimate=cost(1e10),
        name="tokens",
    )(
        idx,
        *[chunk["offs"] for chunk in chunks],
        *flat,
        *route_parts,
        *[chunk["payload"] for chunk in chunks],
        *[table[0] for table in tables],
        *weights[:2],
    )


def weight_kernel(caps, windows, groups, idx, *refs):
    count, size = len(caps), len(groups)
    offs, refs = refs[:count], refs[count:]
    pieces, refs = refs[: 5 * count], refs[5 * count :]
    xs, dys, refs = refs[:size], refs[size : 2 * size], refs[2 * size :]
    outs, done, grads, stacks = refs[:3], refs[3], refs[4 : 4 + count], refs[4 + count :]
    expert = pl.program_id(0)
    hidden = outs[0].shape[2]

    @pl.when(expert == 0)
    def _():
        for c in range(count):
            place_quarters(idx[2], pieces[5 * c : 5 * c + 5], grads[c])
        for stacked in stacks:
            stacked[...] = jnp.zeros_like(stacked)
        done[...] = jnp.zeros_like(done)

    sums = [None] * 3
    for members, slot_x, slot_dy, stacked in zip(groups, xs, dys, stacks):
        for c, start, lane_start in window_starts(members, caps, windows, offs, expert):
            there = slice(lane_start, lane_start + windows[c])
            stacked[there, :] = grads[c][pl.ds(start, windows[c]), :]
        for part, left in enumerate((slot_x, slot_x, slot_dy)):
            columns = slice(part * hidden, (part + 1) * hidden)
            value = jnp.dot(left[0], stacked[:, columns], preferred_element_type=F32)
            sums[part] = value if sums[part] is None else sums[part] + value
    for out, value in zip(outs, sums):
        out[0] = value.astype(BF)


def weight_grads(idx, chunks, pieces, tables, caps, windows, n_local, width, hidden):
    count = len(chunks)
    wide = 3 * hidden
    groups, totals = chunk_groups(count, windows)
    tokens = sum(chunk["payload"].shape[0] for chunk in chunks)
    by_expert = pl.BlockSpec((1, width, hidden), lambda j: (j, 0, 0))
    slots = [table[side] for side in (1, 2) for table in tables]
    return pl.pallas_call(
        functools.partial(weight_kernel, caps, windows, groups),
        grid=(n_local,),
        out_shape=(jax.ShapeDtypeStruct((n_local, width, hidden), BF),) * 3
        + (jax.ShapeDtypeStruct((8, LANES), F32),),
        in_specs=[whole_smem()] * (1 + count)
        + [whole_vmem()] * (5 * count)
        + [pl.BlockSpec((1,) + slot.shape[1:], lambda j: (j, 0, 0)) for slot in slots],
        out_specs=(by_expert,) * 3 + (whole_vmem(),),
        scratch_shapes=[pltpu.VMEM((cap, wide), BF) for cap in caps]
        + [pltpu.VMEM((total, wide), BF) for total in totals],
        compiler_params=pltpu.CompilerParams(
            vmem_limit_bytes=(32 if tokens <= 512 else 56) * MIB
        ),
        cost_estimate=cost(2e10),
        name="weights",
    )(
        idx,
        *[chunk["offs"] for chunk in chunks],
        *[piece for group in pieces for piece in group],
        *slots,
    )


def to_partner(value, axis, other):
    return lax.ppermute(value, axis, [(i, i ^ other) for i in range(lax.axis_size(axis))])


def sum_over_dp(parts, earlier):
    own, send_x, send_y, later_x, later_y, gate = parts
    from_x = to_partner(send_x, "dp", 1)
    from_y = to_partner(send_y, "dp", 2)
    send_x, send_y = pair_sums(earlier, later_x, from_y, later_y, from_x)
    late_x = to_partner(send_x, "dp", 1)
    late_y = to_partner(send_y, "dp", 2)
    return [own, from_x, from_y, late_x, late_y, gate, send_x]


def gather_over_dp(own):
    half = own.shape[0] // 2
    from_x = to_partner(own, "dp", 1)
    from_y = to_partner(own, "dp", 2)
    first = to_partner(from_x[:half], "dp", 2)
    second = to_partner(from_y[half:], "dp", 1)
    return own, from_x, from_y, first, second


def finish_kernel(width, top, idx, *refs):
    parts, (token_grad, route_grad) = refs[:-2], refs[-2:]
    routes = None
    for distance, part in enumerate(parts):
        at = pl.ds(pl.multiple_of((idx[2] ^ distance) * width, LANES), width)
        token_grad[:, at] = part[:, 0:width]
        value = part[:, width:].astype(F32)
        routes = value if routes is None else routes + value
    route_grad[...] = routes[:, 0:top].astype(BF)


def finish(idx, parts, width, top):
    rows = parts[0].shape[0]
    return pl.pallas_call(
        functools.partial(finish_kernel, width, top),
        out_shape=(
            jax.ShapeDtypeStruct((rows, width * len(parts)), BF),
            jax.ShapeDtypeStruct((rows, top), BF),
        ),
        in_specs=[whole_smem()] + [whole_vmem()] * len(parts),
        out_specs=(whole_vmem(),) * 2,
        compiler_params=pltpu.CompilerParams(vmem_limit_bytes=24 * MIB),
        name="finish",
    )(idx, *parts)


def in_hbm(value):
    return pltpu.with_memory_space_constraint(value, pltpu.HBM)


def touch_kernel(*refs):
    ready = refs[-1]
    ready[...] = jnp.zeros_like(ready)


def touch(weights, earlier):
    near = [pltpu.with_memory_space_constraint(weight, pltpu.VMEM) for weight in weights]
    return pl.pallas_call(
        touch_kernel,
        out_shape=jax.ShapeDtypeStruct((8, LANES), F32),
        in_specs=[pl.BlockSpec(memory_space=pl.ANY)] + [whole_vmem()] * len(weights),
        out_specs=whole_vmem(),
        compiler_params=pltpu.CompilerParams(vmem_limit_bytes=24 * MIB),
        name="touch",
    )(earlier, *near)


def fits_kernel(lane, _, *refs):
    flags, parts, out = refs[:2], refs[2:-1], refs[-1]
    value = flags[0][0:1, 0:1]
    for flag in flags[1:]:
        value = jnp.minimum(value, flag[0:1, 0:1])
    for part in parts:
        value = jnp.minimum(value, part[0:16, lane : lane + 1].astype(F32)[0:1, :])
    out[0] = (value[0, 0] > 0.5).astype(jnp.int32)


def all_fit(earlier, flags, parts, width, top):
    lane = width // LANES
    return pl.pallas_call(
        functools.partial(fits_kernel, 2 * top),
        grid=(1,),
        out_shape=jax.ShapeDtypeStruct((1,), jnp.int32),
        in_specs=[pl.BlockSpec(memory_space=pl.ANY)]
        + [pl.BlockSpec((8, LANES), lambda i: (0, 0))] * len(flags)
        + [pl.BlockSpec((part.shape[0], LANES), lambda i: (0, lane)) for part in parts],
        out_specs=whole_smem(),
        compiler_params=pltpu.CompilerParams(vmem_limit_bytes=24 * MIB),
        name="fits",
    )(earlier, *flags, *parts)[0]


def relay_kernel(_, *refs):
    parts, out = refs[:-1], refs[-1]
    first = 0
    for part in parts:
        out[first : first + part.shape[0], :] = part[...]
        first += part.shape[0]


def relay(parts, earlier):
    rows = sum(part.shape[0] for part in parts)
    return pl.pallas_call(
        relay_kernel,
        out_shape=jax.ShapeDtypeStruct((rows, parts[0].shape[1]), BF),
        in_specs=[pl.BlockSpec(memory_space=pl.ANY)] + [whole_vmem()] * len(parts),
        out_specs=whole_vmem(),
        compiler_params=pltpu.CompilerParams(vmem_limit_bytes=24 * MIB),
        name="relay",
    )(earlier, *parts)


def pair_kernel(_, later_x, from_y, later_y, from_x, out_x, out_y):
    out_x[...] = (later_x[...].astype(F32) + from_y[...].astype(F32)).astype(BF)
    out_y[...] = (later_y[...].astype(F32) + from_x[...].astype(F32)).astype(BF)


def pair_sums(earlier, later_x, from_y, later_y, from_x):
    spec = pl.BlockSpec(later_x.shape, lambda i: (0, 0))
    return pl.pallas_call(
        pair_kernel,
        grid=(1,),
        out_shape=(jax.ShapeDtypeStruct(later_x.shape, BF),) * 2,
        in_specs=[pl.BlockSpec(memory_space=pl.ANY)] + [spec] * 4,
        out_specs=(spec,) * 2,
        compiler_params=pltpu.CompilerParams(vmem_limit_bytes=24 * MIB),
        name="pair",
    )(earlier, later_x, from_y, later_y, from_x)


def add_kernel(count, _, *refs):
    parts, outs = refs[:count], refs[count:]
    total = parts[0][...].astype(F32)
    for part in parts[1:]:
        total = total + part[...].astype(F32)
    rows = outs[0].shape[0]
    for i, out in enumerate(outs):
        out[...] = total[i * rows : (i + 1) * rows, :].astype(BF)


def add_up(parts, earlier, pieces):
    rows, lanes = parts[0].shape
    return pl.pallas_call(
        functools.partial(add_kernel, len(parts)),
        out_shape=(jax.ShapeDtypeStruct((rows // pieces, lanes), BF),) * pieces,
        in_specs=[pl.BlockSpec(memory_space=pl.ANY)] + [whole_vmem()] * len(parts),
        out_specs=(whole_vmem(),) * pieces,
        compiler_params=pltpu.CompilerParams(vmem_limit_bytes=24 * MIB),
        name="add",
    )(earlier, *parts)


def on_device(tokens_in, cotangent, expert_ids, gate_probs, gate_weight, up_weight, down_weight):
    n_expert, n_dp = lax.axis_size("expert"), lax.axis_size("dp")
    expert_at, half_at, dp_at = (lax.axis_index(name) for name in ("expert", "half", "dp"))
    idx = jnp.stack([expert_at, half_at, dp_at]).astype(jnp.int32)
    n_local, width, hidden = gate_weight.shape
    weights = (gate_weight, up_weight, down_weight)
    _, blocks, block_tokens, _ = tokens_in.shape
    top = expert_ids.shape[3]
    block = n_dp * block_tokens
    owner_rows = blocks * block_tokens
    group = blocks * block

    parts = pack(
        idx,
        in_hbm(tokens_in[0].transpose(1, 0, 2)),
        in_hbm(cotangent[0].transpose(1, 0, 2)),
        in_hbm(expert_ids[0].transpose(0, 2, 1)),
        in_hbm(gate_probs[0].transpose(0, 2, 1)),
        n_dp,
        width,
    )
    parts = [parts[0]] + [to_partner(parts[k], "dp", k) for k in range(1, n_dp)]

    unit = round_up(n_local * group // 2, LANES)
    small = round_up(n_local * group // 3, LANES)
    choose = small < unit and n_expert <= 4

    def put_together(earlier, parts, kind, span):
        rows = span * group
        return route(
            earlier, idx, parts, kind, rows, n_local, n_expert, small, top, width, owner_rows
        )

    ready = touch(weights[:2], parts[0])
    own, mixed, fits = put_together(ready, parts, "own", 1)
    got = [to_partner(mixed, "expert", k) for k in (1, 2) if k < n_expert]
    window = round_up(group // 2 + ALIGN, LANES)
    units = (unit, small) if choose else (unit,)
    own_sums = partial_acts(idx, own, weights, units, window)
    operands = (own, own_sums, got, weights)
    rest = functools.partial(
        exchange_and_multiply, put_together, idx, half_at, n_expert, n_dp, top, block, group
    )
    if not choose:
        return rest(0, unit, operands)
    flags = [fits, to_partner(fits, "expert", n_expert - 1)]
    return lax.cond(
        all_fit(own_sums[0][-1], flags, got, width, top) == 1,
        functools.partial(rest, 1, small),
        functools.partial(rest, 0, unit),
        operands,
    )


def exchange_and_multiply(
    put_together, idx, half_at, n_expert, n_dp, top, block, group, choice, unit, operands
):
    own, own_sums, got, weights = operands
    own_sums = own_sums[choice]
    n_local, width, hidden = weights[0].shape

    chunks, sums, caps, windows, held = [], [], [], [], 0
    while held < n_expert:
        if held == 0:
            chunk, span, cap = own, 1, unit
        else:
            if held == 1:
                far = relay(got, own_sums[-1])
                ready = touch(weights, far)
            elif held == 3:
                far = to_partner(got[1], "expert", 1)
                own_total = sum_over_dp(own_sums, sums[1][-1])
                ready = own_total[-1]
            else:
                known = jnp.concatenate([chunk["payload"] for chunk in chunks], axis=0)
                side = jnp.where(half_at == 0, known[:, :width], known[:, width : 2 * width])
                far = jnp.concatenate([side, known[:, 2 * width :]], axis=1)
                far = to_partner(far, "expert", held)
            span = far.shape[0] // group
            chunk = put_together(ready, [far, to_partner(far, "half", 1)], "far", span)
            cap = round_up(span * unit, LANES)
        most = span * group // 2
        chunks.append(chunk)
        caps.append(cap)
        windows.append(round_up(most + ALIGN, ALIGN))
        if held == 0:
            sums.append(own_sums)
        else:
            wide_window = round_up(most + ALIGN, LANES)
            sums.append(partial_acts(idx, chunk, weights, (cap,), wide_window)[0])
        held += span

    pieces, route_parts = [], []

    def finish_units(total, earlier):
        grads, route_part = unit_grads(total[:-1], earlier)
        pieces.append(gather_over_dp(grads))
        route_parts.append(route_part)

    if len(sums) <= 2:
        own_total = sum_over_dp(own_sums, sums[-1][-1])
    finish_units(own_total, sums[min(2, len(sums) - 1)][-1])
    tables, ready = [], n_local * 5 // 8

    def slots(earlier, tables, first, last):
        return gather_slots(
            earlier, tables, first, last, chunks, caps, windows, n_local, width
        )

    totals = [
        sum_over_dp(parts, route_parts[0] if i == 0 else parts[-1])
        for i, parts in enumerate(sums[1:])
    ]
    for i, total in enumerate(totals):
        earlier = pieces[0][2] if i == 0 else total[-2]
        if ready and i == len(totals) - 1:
            tables, earlier = slots(route_parts[-1], tables, 0, ready)
        finish_units(total, earlier)
    tables, _ = slots(route_parts[-1], tables, ready if tables else 0, n_local)
    tables = [tables[i : i + 3] for i in range(0, len(tables), 3)]

    keep, send = token_grads(
        idx, chunks, pieces, route_parts, tables, weights, caps, windows, top, block, group
    )
    both = (keep.astype(F32) + to_partner(send, "half", 1).astype(F32)).astype(BF)
    *weight_out, written = weight_grads(
        idx, chunks, pieces, tables, caps, windows, n_local, width, hidden
    )
    held = jnp.split(both, n_expert, axis=0)
    step = n_expert // 2
    while step > 2:
        got = to_partner(jnp.concatenate(held[step:], axis=0), "expert", step)
        held = [
            (mine.astype(F32) + other.astype(F32)).astype(BF)
            for mine, other in zip(held[:step], jnp.split(got, step, axis=0))
        ]
        step //= 2
    total = held[:1] + [to_partner(held[k], "expert", k) for k in range(1, len(held))]
    total = add_up(total, written, n_dp)
    total = [total[0]] + [to_partner(total[k], "dp", k) for k in range(1, n_dp)]
    token_grad, route_grad = finish(idx, total, width, top)
    return (token_grad[None, None], route_grad[None, None]) + tuple(weight_out)


def solution(mesh):
    return jax.shard_map(
        on_device,
        mesh=mesh,
        in_specs=(
            P(("expert", "dp"), None, None, None),
            P(("expert", "dp"), None, None, None),
            P(("expert", "dp"), None, None, None),
            P(("expert", "dp"), None, None, None),
            P("expert", "dp", "half"),
            P("expert", "dp", "half"),
            P("expert", "dp", "half"),
        ),
        out_specs=(
            P(("expert", "dp"), "half", None, None),
            P(("expert", "dp"), "half", None, None),
            P("expert", "dp", "half"),
            P("expert", "dp", "half"),
            P("expert", "dp", "half"),
        ),
        check_vma=False,
    )
```
